32 devices in a mesh: pipe: 2 (over x), dp: 4 (over y, core), tensor: 4 (over z).
Axes of the slice: x: 2, y: 2, z: 4, core: 2. Of those that a mesh axis runs over, the one named last changes fastest.
Arguments:
- inputs: bfloat16 [2, 4, 1024, 768], P('pipe', 'dp', 'tensor'), may hold values from -6 to 6
- cotangent: bfloat16 [2, 4, 1024, 768], P('pipe', 'dp', 'tensor'), may hold values from -6 to 6
- gain_one: float32 [2, 768], P('pipe'), may hold values from 0.5 to 1.5
- shift_one: float32 [2, 768], P('pipe'), may hold values from -1.5 to 1.5
- attend_in: bfloat16 [2, 768, 3, 768], P('pipe', None, None, 'tensor'), may hold values from -0.21875 to 0.21875
- attend_bias: float32 [2, 2, 768], P('pipe', None, 'tensor'), may hold values from -2.5 to 2.5
- attend_out: bfloat16 [2, 768, 768], P('pipe', 'tensor'), may hold values from -3.5 to 3.5
- out_bias: float32 [2, 768], P('pipe'), may hold values from -2.5 to 2.5
- gain_two: float32 [2, 768], P('pipe'), may hold values from 0.5 to 1.5
- shift_two: float32 [2, 768], P('pipe'), may hold values from -1.5 to 1.5
- expand_in: bfloat16 [2, 768, 3072], P('pipe', None, 'tensor'), may hold values from -0.21875 to 0.21875
- expand_bias: float32 [2, 3072], P('pipe', 'tensor'), may hold values from -2.5 to 2.5
- reduce_out: bfloat16 [2, 3072, 768], P('pipe', 'tensor'), may hold values from -0.4375 to 0.4375
- reduce_bias: float32 [2, 768], P('pipe'), may hold values from -2.5 to 2.5
Outputs:
- outputs: bfloat16 [2, 4, 1024, 768], P('pipe', 'dp', 'tensor')
- input_grad: bfloat16 [2, 4, 1024, 768], P('pipe', 'dp', 'tensor')
- grad_gain_one: float32 [2, 768], P('pipe')
- grad_shift_one: float32 [2, 768], P('pipe')
- grad_attend_in: float32 [2, 768, 3, 768], P('pipe', None, None, 'tensor')
- grad_attend_bias: float32 [2, 2, 768], P('pipe', None, 'tensor')
- grad_attend_out: float32 [2, 768, 768], P('pipe', 'tensor')
- grad_out_bias: float32 [2, 768], P('pipe')
- grad_gain_two: float32 [2, 768], P('pipe')
- grad_shift_two: float32 [2, 768], P('pipe')
- grad_expand_in: float32 [2, 768, 3072], P('pipe', None, 'tensor')
- grad_expand_bias: float32 [2, 3072], P('pipe', 'tensor')
- grad_reduce_out: float32 [2, 3072, 768], P('pipe', 'tensor')
- grad_reduce_bias: float32 [2, 768], P('pipe')
The draws below stay inside these ranges and needn't reach their ends.
All inputs are finite; a program needn't handle non-finite values.
Results may differ from the reference program's by a relative error of at most 0.022.
Values may be sent and summed in bfloat16 or wider, within the bound.
No kernel may reach another device: no remote copies, remote signals or barrier semaphores. Data moves between devices by JAX's collectives and lax.ppermute only.
A program may use at most 192 MiB of HBM per device.

```python
import jax
import jax.numpy as jnp
from jax import lax

D = 768
HEADS = 12
HEAD = 64
FF = 3072
SEQ = 1024
MICRO = 2
DEPTH = 12
SEQS = 4
LAYERS = 2


def block_scale(stream_key, dims, cuts, least, high):
    gain = 1.0
    for dim, shards_of in cuts:
        steps = jax.random.uniform(jax.random.fold_in(jax.random.fold_in(stream_key, 6), dim), (shards_of,), jnp.float32, least / len(cuts), high / len(cuts))
        gain = gain * jnp.repeat(jnp.exp(steps), dims[dim] // shards_of).reshape((-1,) + (1,) * (len(dims) - 1 - dim))
    return gain


def normal_values(rng, extent, scale, reach, pieces=(), dtype=jnp.bfloat16):
    level = block_scale(rng, extent, pieces, -0.22, 0.18) if pieces else 1.0
    entries = jax.random.normal(rng, extent, jnp.float32) * scale * level
    return jnp.minimum(jnp.maximum(entries, -reach), reach).astype(dtype)


def setup_inputs(seed: int = 0) -> dict:
    key_of = jax.random.split(jax.random.key(seed), 15)
    return {
        "inputs": normal_values(key_of[0], (MICRO, SEQS, SEQ, D), 1.0, 6.0, ((0, 2), (1, 4), (2, 4))),
        "cotangent": normal_values(key_of[1], (MICRO, SEQS, SEQ, D), 1.0, 6.0, ((0, 2), (1, 4), (2, 4))),
        "gain_one": jnp.clip(0.5 + 1.0 * jax.random.uniform(key_of[2], (LAYERS, D), jnp.float32) ** block_scale(key_of[2], (LAYERS, D), ((0, 2),), -0.2, 0.2), 0.5, 1.5),
        "shift_one": normal_values(key_of[3], (LAYERS, D), 0.3, 1.5, ((0, 2),), jnp.float32),
        "attend_in": normal_values(key_of[4], (LAYERS, D, 3, D), D ** -0.5, 0.21875, ((0, 2), (3, 4))),
        "attend_bias": normal_values(key_of[5], (LAYERS, 2, D), 0.5, 2.5, ((0, 2), (2, 4)), jnp.float32),
        "attend_out": normal_values(key_of[6], (LAYERS, D, D), (max(D // 256, 1)) ** -0.5, 3.5, ((0, 2), (1, 4))),
        "out_bias": normal_values(key_of[7], (LAYERS, D), 0.5, 2.5, ((0, 2),), jnp.float32),
        "gain_two": jnp.clip(0.5 + 1.0 * jax.random.uniform(key_of[8], (LAYERS, D), jnp.float32) ** block_scale(key_of[8], (LAYERS, D), ((0, 2),), -0.2, 0.2), 0.5, 1.5),
        "shift_two": normal_values(key_of[9], (LAYERS, D), 0.3, 1.5, ((0, 2),), jnp.float32),
        "expand_in": normal_values(key_of[10], (LAYERS, D, FF), D ** -0.5, 0.21875, ((0, 2), (2, 4))),
        "expand_bias": normal_values(key_of[11], (LAYERS, FF), 0.5, 2.5, ((0, 2), (1, 4)), jnp.float32),
        "reduce_out": normal_values(key_of[12], (LAYERS, FF, D), (max(FF // 16, 1)) ** -0.5, 0.4375, ((0, 2), (1, 4))),
        "reduce_bias": normal_values(key_of[13], (LAYERS, D), 0.5, 2.5, ((0, 2),), jnp.float32),
    }


@jax.custom_vjp
def low(v):
    return lax.optimization_barrier(v.astype(jnp.bfloat16)).astype(jnp.float32)

@jax.custom_vjp
def low_back(v):
    return v

def low_keep(v):
    return (low(v), None)

def low_pass(kept, grad):
    return (grad,)

def back_keep(v):
    return (v, None)

def back_low(kept, grad):
    return (low(grad),)
low.defvjp(low_keep, low_pass)
low_back.defvjp(back_keep, back_low)
EPSILON = 1e-05
NEGATIVE = -1e+30

def matmul(left, right):
    return jnp.dot(left, right, precision=lax.Precision.HIGHEST)

def normalize(tok_rows, gain_vec, shift_vec):
    centred = tok_rows - lax.optimization_barrier(jnp.mean(tok_rows, axis=-1, keepdims=True))
    scaled = centred * lax.rsqrt(lax.optimization_barrier(jnp.mean(centred * centred, axis=-1, keepdims=True)) + EPSILON)
    return scaled * gain_vec + shift_vec

def one_layer(tok_rows, params):
    gain_a, shift_a, proj_in, proj_bias, proj_out, bias_out, gain_b, shift_b, expand_w, expand_b, reduce_w, reduce_b = params
    branch = DEPTH ** (-0.5)
    normed = low(normalize(tok_rows, gain_a, shift_a))
    queries = low(low_back(matmul(normed, proj_in[:, 0])) + proj_bias[0])
    key_rows = low(low_back(matmul(normed, proj_in[:, 1])))
    values = low(low_back(matmul(normed, proj_in[:, 2])) + proj_bias[1])
    queries = queries.reshape(SEQ, HEADS, HEAD)
    key_rows = key_rows.reshape(SEQ, HEADS, HEAD)
    values = values.reshape(SEQ, HEADS, HEAD)
    scores = jnp.einsum('qhe,khe->hqk', queries, key_rows, precision=lax.Precision.HIGHEST)
    scores = low_back(scores * HEAD ** (-0.5))
    places = jnp.arange(SEQ)
    allowed = places[:, None] >= places[None, :]
    scores = jnp.where(allowed[None], scores, NEGATIVE)
    peak_score = lax.optimization_barrier(jnp.max(scores, axis=-1, keepdims=True))
    weights = jnp.exp(scores - peak_score)
    weights = low(weights / lax.optimization_barrier(jnp.sum(weights, axis=-1, keepdims=True)))
    mixed_heads = jnp.einsum('hqk,khe->qhe', weights, values, precision=lax.Precision.HIGHEST).reshape(SEQ, D)
    mixed_heads = low(low_back(mixed_heads))
    attended = low_back(matmul(mixed_heads, proj_out)) + bias_out
    middle = tok_rows + branch * attended
    normed_two = low(normalize(middle, gain_b, shift_b))
    hidden_pre = low_back(matmul(normed_two, expand_w)) + expand_b
    hidden = low(jax.nn.gelu(hidden_pre, approximate=True))
    outcome = low_back(matmul(hidden, reduce_w)) + reduce_b
    return middle + branch * outcome

def two_layers(sequence, stacked):
    first = one_layer(sequence, tuple((member[0] for member in stacked)))
    passed = low_back(low(first))
    return one_layer(passed, tuple((member[1] for member in stacked)))

def reference(inputs, cotangent, gain_one, shift_one, attend_in, attend_bias, attend_out, out_bias, gain_two, shift_two, expand_in, expand_bias, reduce_out, reduce_bias):
    params = tuple((member.astype(jnp.float32) for member in (gain_one, shift_one, attend_in, attend_bias, attend_out, out_bias, gain_two, shift_two, expand_in, expand_bias, reduce_out, reduce_bias)))
    flat_in = inputs.astype(jnp.float32).reshape(MICRO * SEQS, SEQ, D)
    flat_cot = cotangent.astype(jnp.float32).reshape(MICRO * SEQS, SEQ, D)

    def forward(tokens_in, stacked):

        def per_sequence(sequence):
            return two_layers(sequence, stacked)
        return lax.map(jax.checkpoint(per_sequence), tokens_in)
    results, pullback = jax.vjp(forward, flat_in, params)
    grad_in, grads = pullback(flat_cot)
    shape = (MICRO, SEQS, SEQ, D)
    return (results.reshape(shape).astype(jnp.bfloat16), grad_in.reshape(shape).astype(jnp.bfloat16), grads[0], grads[1], grads[2], grads[3], grads[4], grads[5], grads[6], grads[7], grads[8], grads[9], grads[10], grads[11])
```

```python
import functools

import jax
import jax.numpy as jnp
import numpy as np
from jax import lax
from jax.experimental import pallas as pl
from jax.experimental.pallas import tpu as pltpu
from jax.sharding import Mesh
from jax.sharding import PartitionSpec as P

HEAD = 64
DEPTH = 12
BRANCH = DEPTH ** (-0.5)
EPSILON = 1e-05
NEGATIVE = -1e30
LANES = 128
AXES = ("pipe", "y", "core", "tensor")
F32 = jnp.float32
BF16 = jnp.bfloat16


def ring_order(count):
    return list(range(0, count, 2)) + list(range(1, count, 2))[::-1]


def ring(value):
    order = ring_order(lax.axis_size("tensor"))
    return lax.ppermute(value, "tensor", list(zip(order, order[1:] + order[:1])))


def swap(value, axis):
    return lax.ppermute(value, axis, [(0, 1), (1, 0)])


def along_pipe(value, by):
    return lax.ppermute(value, "pipe", [(0, 1)] if by > 0 else [(1, 0)])


def routes(section, large):
    count = lax.axis_size("tensor")

    def index(x, y, c, z):
        return ((x * 2 + y) * 2 + c) * count + z

    pairs = []
    for micro in range(2):
        for y in range(2):
            for c in range(2):
                for core in range(2):
                    block = 3 - core if large else core
                    pairs.append((index(micro, y, c, block), index(section, y, core, 2 * micro + c)))
    return pairs


def fetch(block, section):
    return [lax.ppermute(block, AXES, routes(section, large)) for large in (False, True)]


def give_back(small, large, section):
    pieces = []
    for rows, is_large in ((small, False), (large, True)):
        pairs = [(b, a) for a, b in routes(section, is_large)]
        pieces.append(lax.ppermute(rows, AXES, pairs))
    return jnp.where(lax.axis_index("tensor") < 2, pieces[0], pieces[1])


def nt(left, right):
    return lax.dot_general(left, right, (((1,), (1,)), ((), ())), preferred_element_type=F32)


def tn(left, right):
    return lax.dot_general(left, right, (((0,), (0,)), ((), ())), preferred_element_type=F32)


def tk(left, right):
    turned = right.astype(F32).T.astype(BF16)
    return nn(turned, left).T


def nn(left, right):
    return lax.dot_general(left, right, (((1,), (0,)), ((), ())), preferred_element_type=F32)


def head_mask(rows, head):
    lanes = lax.broadcasted_iota(jnp.int32, (rows, LANES), 1)
    return (lanes >= head * HEAD) & (lanes < (head + 1) * HEAD)


def only(mask, value, factor=1.0):
    return jnp.where(mask, value.astype(F32) * factor, 0.0).astype(BF16)


def attend_kernel(keep_weights, core_ref, q_ref, k_ref, v_ref, ko_ref, vo_ref, o_ref, *p_refs):
    rows = q_ref.shape[0] // 2
    second = core_ref[0] == 1
    keys = lax.broadcasted_iota(jnp.int32, (rows, rows), 0)
    places = lax.broadcasted_iota(jnp.int32, (rows, rows), 1)
    allowed = keys <= places
    factor = HEAD ** (-0.5)
    small = pl.ds(0, rows)
    large = pl.ds(rows, rows)
    k5 = jnp.where(second, ko_ref[small, :].astype(F32), ko_ref[large, :].astype(F32)).astype(BF16)
    v5 = jnp.where(second, vo_ref[small, :].astype(F32), vo_ref[large, :].astype(F32))
    out_small = None
    out_large = None
    for head in range(LANES // HEAD):
        mask = head_mask(rows, head)

        def query(value):
            return only(mask, value, factor)

        qs, ql = query(q_ref[small, :]), query(q_ref[large, :])
        qf = query(jnp.where(second, q_ref[small, :].astype(F32), q_ref[large, :].astype(F32)))
        s1 = jnp.where(allowed, nt(k_ref[small, :], qs), NEGATIVE)
        s2 = nt(k_ref[small, :], ql)
        s3 = jnp.where(allowed, nt(k_ref[large, :], ql), NEGATIVE)
        s4 = nt(ko_ref[small, :], ql)
        s5 = nt(k5, qf)

        def peak(value):
            return jnp.max(value, axis=0, keepdims=True)

        def total(value):
            return jnp.sum(value, axis=0, keepdims=True)

        m5 = peak(s5)
        ms = peak(s1)
        ml = jnp.maximum(jnp.maximum(peak(s2), peak(s3)), peak(s4))
        ms = jnp.where(second, jnp.maximum(ms, m5), ms)
        ml = jnp.where(second, ml, jnp.maximum(ml, m5))
        mf = jnp.where(second, ms, ml)
        e1 = jnp.exp(s1 - ms)
        e2 = jnp.exp(s2 - ml)
        e3 = jnp.exp(s3 - ml)
        e4 = jnp.exp(s4 - ml)
        e5 = jnp.exp(s5 - mf)
        t5 = total(e5)
        rs = total(e1)
        rl = total(e2) + total(e3) + total(e4)
        rs = 1.0 / jnp.where(second, rs + t5, rs)
        rl = 1.0 / jnp.where(second, rl, rl + t5)
        rf = jnp.where(second, rs, rl)
        p1 = (e1 * rs).astype(BF16)
        p2 = (e2 * rl).astype(BF16)
        p3 = (e3 * rl).astype(BF16)
        p4 = (e4 * rl).astype(BF16)
        p5 = (e5 * rf).astype(BF16)
        if keep_weights:
            for place, value in enumerate((p1, p2, p3, p4, p5)):
                p_refs[0][head, place] = value
        vs = only(mask, v_ref[small, :])
        o5 = tk(p5, only(mask, v5))
        os = tk(p1, vs) + jnp.where(second, o5, 0.0)
        ol = (
            tk(p2, vs)
            + tk(p3, only(mask, v_ref[large, :]))
            + tk(p4, only(mask, vo_ref[small, :]))
            + jnp.where(second, 0.0, o5)
        )
        out_small = os if out_small is None else out_small + os
        out_large = ol if out_large is None else out_large + ol
    o_ref[small, :] = out_small.astype(BF16)
    o_ref[large, :] = out_large.astype(BF16)


def attend_back_kernel(
    core_ref, q_ref, k_ref, v_ref, ko_ref, vo_ref, go_ref, o_ref, p_ref, gq_ref, own_ref, other_ref, sums_ref
):
    rows = q_ref.shape[0] // 2
    second = core_ref[0] == 1
    factor = HEAD ** (-0.5)
    small = pl.ds(0, rows)
    large = pl.ds(rows, rows)

    def fifth(ref, first, last):
        return jnp.where(second, ref[first, :].astype(F32), ref[last, :].astype(F32))

    k5 = fifth(ko_ref, small, large)
    v5 = fifth(vo_ref, small, large).astype(BF16)
    q5 = fifth(q_ref, small, large)
    g5 = fifth(go_ref, small, large)
    product = go_ref[...].astype(F32) * o_ref[...].astype(F32)
    high = product.astype(BF16)
    low = (product - high.astype(F32)).astype(BF16)
    totals = {}

    def add(name, value):
        totals[name] = value if name not in totals else totals[name] + value

    for head in range(LANES // HEAD):
        mask = head_mask(rows, head)
        ones = jnp.where(head_mask(16, head), 1.0, 0.0).astype(BF16)
        inner = (nt(ones, high) + nt(ones, low))[0:1]
        ds_, dl_ = inner[:, :rows], inner[:, rows:]
        df_ = jnp.where(second, ds_, dl_)

        def weight(place):
            return p_ref[head, place]

        qs, ql, qf = (only(mask, value, factor) for value in (q_ref[small, :], q_ref[large, :], q5))
        gs, gl, gf = (only(mask, value) for value in (go_ref[small, :], go_ref[large, :], g5))

        def score_grad(place, values, rows_grad, shift):
            return (weight(place).astype(F32) * (nt(values, rows_grad) - shift)).astype(BF16)

        z1 = score_grad(0, v_ref[small, :], gs, ds_)
        z2 = score_grad(1, v_ref[small, :], gl, dl_)
        z3 = score_grad(2, v_ref[large, :], gl, dl_)
        z4 = score_grad(3, vo_ref[small, :], gl, dl_)
        z5 = score_grad(4, v5, gf, df_)
        k_small = only(mask, k_ref[small, :])
        gq5 = tk(z5, only(mask, k5))
        add("qs", tk(z1, k_small) + jnp.where(second, gq5, 0.0))
        add(
            "ql",
            tk(z2, k_small)
            + tk(z3, only(mask, k_ref[large, :]))
            + tk(z4, only(mask, ko_ref[small, :]))
            + jnp.where(second, 0.0, gq5),
        )
        add("ks", nn(z1, qs) + nn(z2, ql))
        add("kl", nn(z3, ql))
        add("k4", nn(z4, ql))
        add("k5", nn(z5, qf))
        add("vs", nn(weight(0), gs) + nn(weight(1), gl))
        add("vl", nn(weight(2), gl))
        add("v4", nn(weight(3), gl))
        add("v5", nn(weight(4), gf))
    gqs, gql = totals["qs"] * factor, totals["ql"] * factor
    gq_ref[small, :] = gqs.astype(BF16)
    gq_ref[large, :] = gql.astype(BF16)
    for place, name in enumerate("kv"):
        own_ref[place, small, :] = totals[name + "s"]
        own_ref[place, large, :] = totals[name + "l"]
        four, five = totals[name + "4"], totals[name + "5"]
        other_ref[place, small, :] = (four + jnp.where(second, five, 0.0)).astype(BF16)
        other_ref[place, large, :] = jnp.where(second, 0.0, five).astype(BF16)
    sum_q = jnp.sum(gqs, axis=0, keepdims=True) + jnp.sum(gql, axis=0, keepdims=True)
    sum_v = jnp.sum(totals["vs"] + totals["vl"] + totals["v4"] + totals["v5"], axis=0, keepdims=True)
    row = lax.broadcasted_iota(jnp.int32, (8, LANES), 0)
    sums_ref[...] = jnp.where(row == 0, sum_q, jnp.where(row == 1, sum_v, 0.0))


def attend(core, qkv, kv_other, keep_weights):
    length, triple = qkv.shape
    width = triple // 3
    pairs = width // LANES
    rows = length // 2

    def at(shift):
        return pl.BlockSpec((length, LANES), lambda i: (0, i + shift))

    shapes = [jax.ShapeDtypeStruct((length, width), BF16)]
    outs = [at(0)]
    if keep_weights:
        shapes.append(jax.ShapeDtypeStruct((width // HEAD, 5, rows, rows), BF16))
        outs.append(pl.BlockSpec((2, 5, rows, rows), lambda i: (i, 0, 0, 0)))
    return pl.pallas_call(
        functools.partial(attend_kernel, keep_weights),
        grid=(pairs,),
        out_shape=shapes,
        in_specs=[
            pl.BlockSpec(memory_space=pltpu.SMEM),
            at(0),
            at(pairs),
            at(2 * pairs),
            at(0),
            at(pairs),
        ],
        out_specs=outs,
        compiler_params=pltpu.CompilerParams(vmem_limit_bytes=48 * 1024 * 1024),
        cost_estimate=pl.CostEstimate(
            flops=20 * rows * rows * width * 2, bytes_accessed=16 * length * width, transcendentals=5 * rows * rows * 12
        ),
        name="attend",
    )(core, qkv, qkv, qkv, kv_other, kv_other)


def attend_back(core, qkv, kv_other, grad_mixed, mixed, weights):
    length, triple = qkv.shape
    width = triple // 3
    pairs = width // LANES
    rows = length // 2

    def at(shift):
        return pl.BlockSpec((length, LANES), lambda i: (0, i + shift))

    double = pl.BlockSpec((2, length, LANES), lambda i: (0, 0, i))
    return pl.pallas_call(
        attend_back_kernel,
        grid=(pairs,),
        out_shape=[
            jax.ShapeDtypeStruct((length, width), BF16),
            jax.ShapeDtypeStruct((2, length, width), F32),
            jax.ShapeDtypeStruct((2, length, width), BF16),
            jax.ShapeDtypeStruct((8, width), F32),
        ],
        in_specs=[
            pl.BlockSpec(memory_space=pltpu.SMEM),
            at(0),
            at(pairs),
            at(2 * pairs),
            at(0),
            at(pairs),
            at(0),
            at(0),
            pl.BlockSpec((2, 5, rows, rows), lambda i: (i, 0, 0, 0)),
        ],
        out_specs=[at(0), double, double, pl.BlockSpec((8, LANES), lambda i: (0, i))],
        compiler_params=pltpu.CompilerParams(vmem_limit_bytes=48 * 1024 * 1024),
        cost_estimate=pl.CostEstimate(
            flops=40 * rows * rows * width * 2, bytes_accessed=40 * length * width, transcendentals=0
        ),
        name="attend_back",
    )(core, qkv, qkv, qkv, kv_other, kv_other, grad_mixed, mixed, weights)


def gelu_and_slope(values):
    root = float(np.sqrt(2 / np.pi))
    cubic = 0.044715 * root
    square = values * values
    bend = jnp.tanh(values * (root + cubic * square))
    half = 0.5 + 0.5 * bend
    gate = values * half
    slope = half + gate * ((1.0 - bend) * (root + (3 * cubic) * square))
    return (gate, slope)


def tiles_of(units):
    return units // 512 if units % 512 == 0 else 1


def expand_kernel(rows_ref, expand_ref, bias_ref, reduce_ref, start_ref, total_ref, hidden_ref, slope_ref):
    units = expand_ref.shape[0]
    piece = 256 if units % 256 == 0 else units
    rows = rows_ref[...]
    total = None
    for offset in range(0, units, piece):
        part = pl.ds(offset, piece)
        gate, slope = gelu_and_slope(nt(rows, expand_ref[part, :]) + bias_ref[:, part])
        hidden = gate.astype(BF16)
        hidden_ref[:, part] = hidden
        slope_ref[:, part] = slope.astype(BF16)
        term = nn(hidden, reduce_ref[part, :])
        total = term if total is None else total + term

    @pl.when(pl.program_id(0) == 0)
    def _():
        total_ref[...] = start_ref[...] + total

    @pl.when(pl.program_id(0) > 0)
    def _():
        total_ref[...] += total


def contract_kernel(grad_ref, expand_ref, slope_ref, reduce_ref, start_ref, total_ref, pre_ref, sums_ref):
    units = expand_ref.shape[0]
    piece = 256 if units % 256 == 0 else units
    grad = grad_ref[...]
    total = None
    for offset in range(0, units, piece):
        part = pl.ds(offset, piece)
        pre = nt(grad, reduce_ref[part, :]) * slope_ref[:, part].astype(F32)
        sums_ref[:, part] = jnp.broadcast_to(jnp.sum(pre, axis=0, keepdims=True), (8, piece))
        rounded = pre.astype(BF16)
        pre_ref[:, part] = rounded
        term = nn(rounded, expand_ref[part, :])
        total = term if total is None else total + term

    @pl.when(pl.program_id(0) == 0)
    def _():
        total_ref[...] = start_ref[...] + total

    @pl.when(pl.program_id(0) > 0)
    def _():
        total_ref[...] += total


def feed_half(rows, expand_w, bias, reduce_w, start):
    length, width = rows.shape
    units = expand_w.shape[0]
    steps = tiles_of(units)
    tile = units // steps
    whole = pl.BlockSpec((length, width), lambda i: (0, 0))
    weight = pl.BlockSpec((tile, width), lambda i: (i, 0))
    across = pl.BlockSpec((length, tile), lambda i: (0, i))
    return pl.pallas_call(
        expand_kernel,
        grid=(steps,),
        out_shape=[
            jax.ShapeDtypeStruct((length, width), F32),
            jax.ShapeDtypeStruct((length, units), BF16),
            jax.ShapeDtypeStruct((length, units), BF16),
        ],
        in_specs=[whole, weight, pl.BlockSpec((1, tile), lambda i: (0, i)), weight, whole],
        out_specs=[whole, across, across],
        compiler_params=pltpu.CompilerParams(vmem_limit_bytes=40 * 1024 * 1024),
        cost_estimate=pl.CostEstimate(
            flops=4 * length * width * units, bytes_accessed=4 * width * units, transcendentals=length * units
        ),
        name="feed_half",
    )(rows, expand_w, bias.reshape(1, units), reduce_w, start)


def feed_half_back(grad, expand_w, slope, reduce_w, start):
    length, width = grad.shape
    units = expand_w.shape[0]
    steps = tiles_of(units)
    tile = units // steps
    whole = pl.BlockSpec((length, width), lambda i: (0, 0))
    weight = pl.BlockSpec((tile, width), lambda i: (i, 0))
    across = pl.BlockSpec((length, tile), lambda i: (0, i))
    return pl.pallas_call(
        contract_kernel,
        grid=(steps,),
        out_shape=[
            jax.ShapeDtypeStruct((length, width), F32),
            jax.ShapeDtypeStruct((length, units), BF16),
            jax.ShapeDtypeStruct((8, units), F32),
        ],
        in_specs=[whole, weight, across, weight, whole],
        out_specs=[whole, across, pl.BlockSpec((8, tile), lambda i: (0, i))],
        compiler_params=pltpu.CompilerParams(vmem_limit_bytes=40 * 1024 * 1024),
        cost_estimate=pl.CostEstimate(
            flops=4 * length * width * units, bytes_accessed=4 * width * units, transcendentals=0
        ),
        name="feed_half_back",
    )(grad, expand_w, slope, reduce_w, start)


def tie(value, *others):
    return lax.optimization_barrier((value, *others))[0]


def normalize_rows(rows):
    centred = rows - jnp.mean(rows, axis=-1, keepdims=True)
    inverse = lax.rsqrt(jnp.mean(centred * centred, axis=-1, keepdims=True) + EPSILON)
    return (centred * inverse, inverse)


def norm_backward(grad_normed, normed, inverse, gain):
    scaled = grad_normed * gain
    centred = scaled - jnp.mean(scaled, axis=-1, keepdims=True)
    return inverse * (centred - normed * jnp.mean(scaled * normed, axis=-1, keepdims=True))


def attention_forward(core, rows_in, weights, keep, after_projection=None):
    gain_a, shift_a, proj_in, proj_bias, proj_out, bias_out = weights
    normed_one, inverse_one = normalize_rows(rows_in)
    ready_one = (normed_one * gain_a + shift_a).astype(BF16)
    qkv = (nt(ready_one, proj_in) + proj_bias).astype(BF16)
    width = rows_in.shape[1]
    kv_other = swap(qkv[:, width:], "core")
    mixed, *kept_weights = attend(core, qkv, kv_other, keep)
    middle = rows_in + BRANCH * (nn(mixed, proj_out) + bias_out)
    kept = (normed_one, inverse_one, ready_one, qkv, kv_other, mixed, *kept_weights)
    return middle, kept


def feed_forward(middle, weights):
    gain_b, shift_b, halves, reduce_b = weights
    normed_two, inverse_two = normalize_rows(middle)
    ready_two = (normed_two * gain_b + shift_b).astype(BF16)
    total = jnp.broadcast_to(reduce_b, middle.shape)
    hidden, slope = [], []
    for expand_w, expand_b, reduce_w in halves:
        total, hidden_part, slope_part = feed_half(ready_two, expand_w, expand_b, reduce_w, total)
        hidden.append(hidden_part)
        slope.append(slope_part)
    return middle + BRANCH * total, (normed_two, inverse_two, ready_two, hidden, slope)


def feed_backward(kept, grad_result, weights):
    gain_b, _, halves, _ = weights
    normed_two, inverse_two, ready_two, hidden, slope = kept
    grad_outcome = BRANCH * grad_result
    rounded_outcome = grad_outcome.astype(BF16)
    total = jnp.zeros_like(grad_result)
    rounded_pre, sums = [], []
    for (expand_w, _, reduce_w), slope_part in zip(halves, slope):
        total, pre, sum_part = feed_half_back(rounded_outcome, expand_w, slope_part, reduce_w, total)
        rounded_pre.append(pre)
        sums.append(sum_part[0])
    grad_middle = grad_result + norm_backward(total, normed_two, inverse_two, gain_b)
    shared = [total * normed_two, total, grad_outcome]
    return grad_middle, rounded_outcome, rounded_pre, sums, shared


def attention_backward(core, kept, grad_middle, weights, last=()):
    gain_a, _, proj_in, _, proj_out, _ = weights
    normed_one, inverse_one, ready_one, qkv, kv_other, mixed, attention = kept
    width = normed_one.shape[1]
    grad_attended = BRANCH * grad_middle
    rounded_attended = grad_attended.astype(BF16)
    grad_mixed = nt(rounded_attended, proj_out).astype(BF16)
    grad_q, own, other, sums = attend_back(core, qkv, kv_other, grad_mixed, mixed, attention)
    other = tie(other, *last)
    grad_kv = (own + swap(other, "core").astype(F32)).astype(BF16)
    grad_normed_one = (
        nn(grad_q, proj_in[:width]) + nn(grad_kv[0], proj_in[width : 2 * width]) + nn(grad_kv[1], proj_in[2 * width :])
    )
    grad_in = grad_middle + norm_backward(grad_normed_one, normed_one, inverse_one, gain_a)
    shared = [grad_normed_one * normed_one, grad_normed_one, grad_attended]
    return grad_in, rounded_attended, (grad_q, grad_kv[0], grad_kv[1]), sums[:2], shared


def narrow(value):
    return value.astype(BF16)


def wide_add(left, right):
    return narrow(left.astype(F32) + right.astype(F32))


def over_groups(value):
    return lax.psum(value, "outer") if lax.axis_size("outer") > 1 else value


def ring_add(parts):
    count = len(parts)
    total = parts[1 % count]
    for step in range(1, count):
        total = wide_add(ring(total), parts[(step + 1) % count])
    return total


def thirds(values):
    pieces = []
    for _ in range(3):
        piece = lax.reduce_precision(values, 8, 7)
        pieces.append(narrow(piece))
        values = values - piece
    return jnp.stack(pieces)


def shards(
    inputs, cotangent, gain_one, shift_one, attend_in, attend_bias, attend_out, out_bias,
    gain_two, shift_two, expand_in, expand_bias, reduce_out, reduce_bias,
):
    count = lax.axis_size("tensor")
    x, y, c, z = (lax.axis_index(axis) for axis in AXES)
    is_first = x == 0
    core = c.reshape(1).astype(jnp.int32)
    width = attend_in.shape[1]
    local = attend_in.shape[3]
    units = expand_in.shape[2]
    half = local // 2
    part = units // 4
    spare = 16

    def either(index, pair):
        first, second = pair
        return jnp.where(index == 0, first, second), jnp.where(index == 0, second, first)

    def quarters(value, axis):
        blocks = jnp.split(value, 4, axis)
        rows = [either(y, blocks[:2]), either(y, blocks[2:])]
        return list(zip(*(either(c, pair) for pair in zip(*rows))))

    rows_in = jnp.concatenate(fetch(inputs[0, 0], 0))
    own = jnp.concatenate([attend_in[0].transpose(1, 2, 0), attend_out])
    mine = jnp.where(c == 0, own[:2], own[2:])
    biases = thirds(jnp.concatenate([attend_bias[0].reshape(2 * local), expand_bias[0]])).reshape(-1)
    biases = jnp.pad(biases, (0, spare * width - biases.size)).reshape(spare, width)
    piece = jnp.where(y == 0, mine[:, :half], mine[:, half:]).reshape(local, width)
    piece = jnp.concatenate([piece, biases])
    bias_rows = [biases]
    pieces = []
    for _ in range(count - 1):
        piece = ring(piece)
        pieces.append(piece)
    expand_own = quarters(expand_in[0].T, 0)
    reduce_own = quarters(reduce_out[0], 0)
    feed = [jnp.stack([expand_own[0][0], reduce_own[0][0]])]
    feed_y = [jnp.stack([expand_own[0][1], reduce_own[0][1]])]
    moving = ring(tie(feed[0], pieces[0]))
    moving = tie(moving, pieces[-1])
    feed.append(moving)
    feed_y.append(swap(moving, "y"))
    moving = ring(moving)
    halves = []
    for piece in pieces:
        bias_rows.append(piece[local:])
        piece = piece[:local]
        pair = [value.reshape(2, half, width) for value in either(y, (piece, swap(piece, "y")))]
        halves.append(jnp.concatenate(pair, axis=1))
    halves = jnp.concatenate(halves, axis=1)
    first, second = either(c, (halves, swap(halves, "core")))
    both = [jnp.concatenate([own[kind], (first, second)[kind // 2][kind % 2]]) for kind in range(4)]
    proj_in = jnp.concatenate(both[:3])
    proj_out = both[3]
    biases = jnp.stack(bias_rows).reshape(count, -1)[:, : 3 * (2 * local + units)].reshape(count, 3, 2 * local + units)
    biases = biases.astype(F32)
    biases = biases[:, 0] + (biases[:, 1] + biases[:, 2])
    bias_q, bias_v = biases[:, :local].reshape(width), biases[:, local : 2 * local].reshape(width)
    proj_bias = jnp.concatenate([bias_q, jnp.zeros_like(bias_q), bias_v])
    expand_b = quarters(biases[:, 2 * local :], 1)
    expand_b = [jnp.concatenate([value.reshape(count * part) for value in pair]) for pair in expand_b]
    attention_weights = (gain_one[0], shift_one[0], proj_in, proj_bias, proj_out, out_bias[0])

    block = rows_in.shape[0] // 2
    middle, parts = attention_forward(core, rows_in.astype(F32), attention_weights, False)
    last = fetch(cotangent[0, 0], 1)
    moving = tie(moving, parts[3])
    feed.append(moving)
    feed_y.append(swap(moving, "y"))
    moving = ring(moving)
    moving = tie(moving, parts[5], *last)
    feed.append(moving)
    feed_y.append(swap(moving, "y"))
    last = jnp.concatenate(last)
    own_half = [jnp.concatenate([value[kind] for value in feed + feed_y]) for kind in range(2)]
    other_half = [swap(value, "core") for value in own_half]
    feed_weights = (
        gain_two[0],
        shift_two[0],
        [(own_half[0], expand_b[0], own_half[1]), (other_half[0], expand_b[1], other_half[1])],
        reduce_bias[0],
    )
    result = narrow(feed_forward(middle, feed_weights)[0])
    passed = jnp.concatenate([along_pipe(result[:block], 1), along_pipe(result[block:], 1)])
    rows_in = jnp.where(is_first, rows_in, passed)
    middle, kept_attention = attention_forward(core, rows_in.astype(F32), attention_weights, True)
    result, kept_feed = feed_forward(middle, feed_weights)
    result = narrow(result)
    outputs = give_back(result[:block], result[block:], 1)
    grad_middle = feed_backward(kept_feed, last.astype(F32), feed_weights)[0]
    grad_in = attention_backward(core, kept_attention, grad_middle, attention_weights, (outputs,))[0]
    grad_in = narrow(grad_in)
    returned = jnp.concatenate([along_pipe(grad_in[:block], -1), along_pipe(grad_in[block:], -1)])
    grad_result = jnp.where(is_first, returned, last)

    def unit_grads(units_of, rows_of, core_half, y_half):
        piece = units_of[core_half]
        span = piece.shape[1] // 2
        return tn(piece[:, y_half * span : (y_half + 1) * span], rows_of)

    rounded_outcome = narrow(BRANCH * grad_result.astype(F32))
    hidden = kept_feed[3]
    send = [unit_grads(hidden, rounded_outcome, 1, i) for i in range(2)]
    keep = [unit_grads(hidden, rounded_outcome, 0, i) for i in range(2)]
    send = [narrow(value) for value in send]
    reduce_arrived = [swap(value, "core") for value in send]
    grad_result, *keep = lax.optimization_barrier((grad_result, *keep, *send))[:3]
    grad_middle, _, rounded_pre, sums_pre, shared_feed = feed_backward(kept_feed, grad_result.astype(F32), feed_weights)
    reduce_sums = [wide_add(a, tie(b, grad_middle)) for a, b in zip(keep, reduce_arrived)]
    reduce_sums = jnp.stack(reduce_sums).reshape(2, count, part, width)
    reduce_total = ring_add([reduce_sums[:, slot] for slot in range(count)])
    ready_two = kept_feed[2]
    send = [unit_grads(rounded_pre, ready_two, 1, i) for i in (1, 0)]
    keep = [unit_grads(rounded_pre, ready_two, 0, i) for i in (1, 0)]
    send = [narrow(value) for value in send]
    grad_middle, *keep = lax.optimization_barrier((grad_middle, *keep, *send))[:3]
    expand_sums = [wide_add(a, swap(b, "core")).reshape(count, part, width) for a, b in zip(keep, send)]
    expand_parts = [None] * count
    for slot in list(range(1, count)) + [0]:
        expand_parts[slot] = wide_add(expand_sums[1][slot], swap(expand_sums[0][slot], "y"))
    expand_total = ring_add(expand_parts)
    grad_in, rounded_attended, grad_qkv, sums_qv, shared_attention = attention_backward(
        core, kept_attention, grad_middle, attention_weights
    )
    grad_in = narrow(grad_in)
    mixed, ready_one = kept_attention[5], kept_attention[2]
    typed_grads = [narrow(tn(value, ready_one)) for value in grad_qkv] + [narrow(tn(mixed, rounded_attended))]
    typed_grads = jnp.stack(typed_grads).reshape(2, 2, count, 2, half, width)
    typed_grads = typed_grads.transpose(0, 3, 2, 1, 4, 5).reshape(2, 2, count, local, width)
    shared = shared_attention[:2] + [shared_attention[2]] + shared_feed
    shared = jnp.stack([jnp.sum(value, axis=0) for value in shared])
    sums_qv = jnp.pad(sums_qv.reshape(2, count, local), ((0, 0), (0, 0), (0, 0)))
    sums_qv = jnp.concatenate([sums_qv[0], sums_qv[1], jnp.zeros((count, width - 2 * local), F32)], axis=1)[:, None]
    sums_pre = [[value.reshape(count, part) for value in jnp.split(half_sums, 2)] for half_sums in sums_pre]
    sums_pre = quarters(jnp.concatenate(sums_pre[0] + sums_pre[1], axis=1), 1)
    sums_pre = jnp.concatenate(sums_pre[0] + sums_pre[1], axis=1)[:, None]
    vectors = jnp.concatenate([jnp.broadcast_to(shared, (count,) + shared.shape), sums_qv, sums_pre], axis=1)
    vectors = narrow(vectors).reshape(count, 2, 2, 2, width).transpose(1, 2, 0, 3, 4)
    vectors = jnp.pad(vectors, ((0, 0), (0, 0), (0, 0), (0, spare - 2), (0, 0)))
    typed_grads = jnp.concatenate([typed_grads, vectors], axis=3)
    keep, send = either(c, (typed_grads[0], typed_grads[1]))
    typed_sums = wide_add(keep, swap(send, "core"))
    keep, send = either(y, (typed_sums[0], typed_sums[1]))
    typed_parts = [None] * count
    for slot in list(range(1, count)) + [0]:
        typed_parts[slot] = wide_add(keep[slot], swap(send[slot], "y"))
    typed_total = ring_add(typed_parts)
    input_grad = give_back(grad_in[:block], grad_in[block:], 0)
    def gathered(pair):
        pair = jnp.concatenate(pair)
        blocks = quarters(jnp.concatenate([pair, swap(pair, "core")]), 0)
        return jnp.concatenate(blocks[0] + blocks[1])

    reduce_other = swap(reduce_total, "y")
    grad_reduce = [over_groups(wide_add(reduce_total[i], reduce_other[1 - i])) for i in range(2)]
    grad_reduce = gathered(grad_reduce).astype(F32)
    expand_total = over_groups(expand_total)
    grad_expand = gathered([expand_total, swap(expand_total, "y")]).T.astype(F32)
    typed_total = over_groups(typed_total)
    pair = jnp.stack(either(y, (typed_total, swap(typed_total, "y"))))
    whole = either(c, (pair, swap(pair, "core")))
    vectors = jnp.stack([value[:, local : local + 2] for value in whole]).reshape(8, width).astype(F32)
    whole = [value[:, :local].reshape(2, 2, half, width).transpose(1, 0, 2, 3).reshape(2, local, width) for value in whole]
    grad_attend_in = jnp.concatenate([whole[0], whole[1][:1]]).transpose(2, 0, 1).astype(F32)
    grad_attend_out = whole[1][1].astype(F32)
    return (
        outputs[None, None],
        input_grad[None, None],
        vectors[0][None],
        vectors[1][None],
        grad_attend_in[None],
        vectors[6, : 2 * local].reshape(1, 2, local),
        grad_attend_out[None],
        vectors[2][None],
        vectors[3][None],
        vectors[4][None],
        grad_expand[None],
        vectors[7, :units][None],
        grad_reduce[None],
        vectors[5][None],
    )


def solution(mesh):
    pipe, groups, count = mesh.devices.shape
    split = Mesh(mesh.devices.reshape(pipe, groups // 4, 2, 2, count), ("pipe", "outer", "y", "core", "tensor"))
    dp = ("outer", "y", "core")
    rows = P("pipe", dp, "tensor", None)
    vector = P("pipe", None)
    placed = (
        rows,
        rows,
        vector,
        vector,
        P("pipe", None, None, "tensor"),
        P("pipe", None, "tensor"),
        P("pipe", "tensor", None),
        vector,
        vector,
        vector,
        P("pipe", None, "tensor"),
        P("pipe", "tensor"),
        P("pipe", "tensor", None),
        vector,
    )
    return jax.shard_map(shards, mesh=split, in_specs=placed, out_specs=(rows, rows) + placed[2:], check_vma=False)
```

```python
import functools

import jax
import jax.numpy as jnp
import numpy as np
from jax import lax
from jax.experimental import pallas as pl
from jax.experimental.pallas import tpu as pltpu
from jax.sharding import Mesh
from jax.sharding import PartitionSpec as P

HEAD = 64
DEPTH = 12
BRANCH = DEPTH ** (-0.5)
EPSILON = 1e-05
NEGATIVE = -1e30
LANES = 128
AXES = ("pipe", "y", "core", "tensor")
F32 = jnp.float32
BF16 = jnp.bfloat16


def ring_order(count):
    return list(range(0, count, 2)) + list(range(1, count, 2))[::-1]


def ring(value):
    order = ring_order(lax.axis_size("tensor"))
    return lax.ppermute(value, "tensor", list(zip(order, order[1:] + order[:1])))


def swap(value, axis):
    return lax.ppermute(value, axis, [(0, 1), (1, 0)])


def along_pipe(value, by):
    return lax.ppermute(value, "pipe", [(0, 1)] if by > 0 else [(1, 0)])


def routes(section, large):
    count = lax.axis_size("tensor")

    def index(x, y, c, z):
        return ((x * 2 + y) * 2 + c) * count + z

    pairs = []
    for micro in range(2):
        for y in range(2):
            for c in range(2):
                for core in range(2):
                    block = 3 - core if large else core
                    pairs.append((index(micro, y, c, block), index(section, y, core, 2 * micro + c)))
    return pairs


def fetch(block, section):
    return [lax.ppermute(block, AXES, routes(section, large)) for large in (False, True)]


def give_back(small, large, section):
    pieces = []
    for rows, is_large in ((small, False), (large, True)):
        pairs = [(b, a) for a, b in routes(section, is_large)]
        pieces.append(lax.ppermute(rows, AXES, pairs))
    return jnp.where(lax.axis_index("tensor") < 2, pieces[0], pieces[1])


def nt(left, right):
    return lax.dot_general(left, right, (((1,), (1,)), ((), ())), preferred_element_type=F32)


def tn(left, right):
    return lax.dot_general(left, right, (((0,), (0,)), ((), ())), preferred_element_type=F32)


def tk(left, right):
    turned = right.astype(F32).T.astype(BF16)
    return nn(turned, left).T


def nn(left, right):
    return lax.dot_general(left, right, (((1,), (0,)), ((), ())), preferred_element_type=F32)


def head_mask(rows, head):
    lanes = lax.broadcasted_iota(jnp.int32, (rows, LANES), 1)
    return (lanes >= head * HEAD) & (lanes < (head + 1) * HEAD)


def only(mask, value, factor=1.0):
    return jnp.where(mask, value.astype(F32) * factor, 0.0).astype(BF16)


def attend_kernel(keep_weights, core_ref, q_ref, k_ref, v_ref, ko_ref, vo_ref, o_ref, *p_refs):
    rows = q_ref.shape[0] // 2
    second = core_ref[0] == 1
    keys = lax.broadcasted_iota(jnp.int32, (rows, rows), 0)
    places = lax.broadcasted_iota(jnp.int32, (rows, rows), 1)
    allowed = keys <= places
    factor = HEAD ** (-0.5)
    small = pl.ds(0, rows)
    large = pl.ds(rows, rows)
    k5 = jnp.where(second, ko_ref[small, :].astype(F32), ko_ref[large, :].astype(F32)).astype(BF16)
    v5 = jnp.where(second, vo_ref[small, :].astype(F32), vo_ref[large, :].astype(F32))
    out_small = None
    out_large = None
    for head in range(LANES // HEAD):
        mask = head_mask(rows, head)

        def query(value):
            return only(mask, value, factor)

        qs, ql = query(q_ref[small, :]), query(q_ref[large, :])
        qf = query(jnp.where(second, q_ref[small, :].astype(F32), q_ref[large, :].astype(F32)))
        s1 = jnp.where(allowed, nt(k_ref[small, :], qs), NEGATIVE)
        s2 = nt(k_ref[small, :], ql)
        s3 = jnp.where(allowed, nt(k_ref[large, :], ql), NEGATIVE)
        s4 = nt(ko_ref[small, :], ql)
        s5 = nt(k5, qf)

        def peak(value):
            return jnp.max(value, axis=0, keepdims=True)

        def total(value):
            return jnp.sum(value, axis=0, keepdims=True)

        m5 = peak(s5)
        ms = peak(s1)
        ml = jnp.maximum(jnp.maximum(peak(s2), peak(s3)), peak(s4))
        ms = jnp.where(second, jnp.maximum(ms, m5), ms)
        ml = jnp.where(second, ml, jnp.maximum(ml, m5))
        mf = jnp.where(second, ms, ml)
        e1 = jnp.exp(s1 - ms)
        e2 = jnp.exp(s2 - ml)
        e3 = jnp.exp(s3 - ml)
        e4 = jnp.exp(s4 - ml)
        e5 = jnp.exp(s5 - mf)
        t5 = total(e5)
        rs = total(e1)
        rl = total(e2) + total(e3) + total(e4)
        rs = 1.0 / jnp.where(second, rs + t5, rs)
        rl = 1.0 / jnp.where(second, rl, rl + t5)
        rf = jnp.where(second, rs, rl)
        p1 = (e1 * rs).astype(BF16)
        p2 = (e2 * rl).astype(BF16)
        p3 = (e3 * rl).astype(BF16)
        p4 = (e4 * rl).astype(BF16)
        p5 = (e5 * rf).astype(BF16)
        if keep_weights:
            for place, value in enumerate((p1, p2, p3, p4, p5)):
                p_refs[0][head, place] = value
        vs = only(mask, v_ref[small, :])
        o5 = tk(p5, only(mask, v5))
        os = tk(p1, vs) + jnp.where(second, o5, 0.0)
        ol = (
            tk(p2, vs)
            + tk(p3, only(mask, v_ref[large, :]))
            + tk(p4, only(mask, vo_ref[small, :]))
            + jnp.where(second, 0.0, o5)
        )
        out_small = os if out_small is None else out_small + os
        out_large = ol if out_large is None else out_large + ol
    o_ref[small, :] = out_small.astype(BF16)
    o_ref[large, :] = out_large.astype(BF16)


def attend_back_kernel(
    core_ref, q_ref, k_ref, v_ref, ko_ref, vo_ref, go_ref, o_ref, p_ref, gq_ref, own_ref, other_ref, sums_ref
):
    rows = q_ref.shape[0] // 2
    second = core_ref[0] == 1
    factor = HEAD ** (-0.5)
    small = pl.ds(0, rows)
    large = pl.ds(rows, rows)

    def fifth(ref, first, last):
        return jnp.where(second, ref[first, :].astype(F32), ref[last, :].astype(F32))

    k5 = fifth(ko_ref, small, large)
    v5 = fifth(vo_ref, small, large).astype(BF16)
    q5 = fifth(q_ref, small, large)
    g5 = fifth(go_ref, small, large)
    product = go_ref[...].astype(F32) * o_ref[...].astype(F32)
    high = product.astype(BF16)
    low = (product - high.astype(F32)).astype(BF16)
    totals = {}

    def add(name, value):
        totals[name] = value if name not in totals else totals[name] + value

    for head in range(LANES // HEAD):
        mask = head_mask(rows, head)
        ones = jnp.where(head_mask(16, head), 1.0, 0.0).astype(BF16)
        inner = (nt(ones, high) + nt(ones, low))[0:1]
        ds_, dl_ = inner[:, :rows], inner[:, rows:]
        df_ = jnp.where(second, ds_, dl_)

        def weight(place):
            return p_ref[head, place]

        qs, ql, qf = (only(mask, value, factor) for value in (q_ref[small, :], q_ref[large, :], q5))
        gs, gl, gf = (only(mask, value) for value in (go_ref[small, :], go_ref[large, :], g5))

        def score_grad(place, values, rows_grad, shift):
            return (weight(place).astype(F32) * (nt(values, rows_grad) - shift)).astype(BF16)

        z1 = score_grad(0, v_ref[small, :], gs, ds_)
        z2 = score_grad(1, v_ref[small, :], gl, dl_)
        z3 = score_grad(2, v_ref[large, :], gl, dl_)
        z4 = score_grad(3, vo_ref[small, :], gl, dl_)
        z5 = score_grad(4, v5, gf, df_)
        k_small = only(mask, k_ref[small, :])
        gq5 = tk(z5, only(mask, k5))
        add("qs", tk(z1, k_small) + jnp.where(second, gq5, 0.0))
        add(
            "ql",
            tk(z2, k_small)
            + tk(z3, only(mask, k_ref[large, :]))
            + tk(z4, only(mask, ko_ref[small, :]))
            + jnp.where(second, 0.0, gq5),
        )
        add("ks", nn(z1, qs) + nn(z2, ql))
        add("kl", nn(z3, ql))
        add("k4", nn(z4, ql))
        add("k5", nn(z5, qf))
        add("vs", nn(weight(0), gs) + nn(weight(1), gl))
        add("vl", nn(weight(2), gl))
        add("v4", nn(weight(3), gl))
        add("v5", nn(weight(4), gf))
    gqs, gql = totals["qs"] * factor, totals["ql"] * factor
    gq_ref[small, :] = gqs.astype(BF16)
    gq_ref[large, :] = gql.astype(BF16)
    for place, name in enumerate("kv"):
        own_ref[place, small, :] = totals[name + "s"]
        own_ref[place, large, :] = totals[name + "l"]
        four, five = totals[name + "4"], totals[name + "5"]
        other_ref[place, small, :] = (four + jnp.where(second, five, 0.0)).astype(BF16)
        other_ref[place, large, :] = jnp.where(second, 0.0, five).astype(BF16)
    sum_q = jnp.sum(gqs, axis=0, keepdims=True) + jnp.sum(gql, axis=0, keepdims=True)
    sum_v = jnp.sum(totals["vs"] + totals["vl"] + totals["v4"] + totals["v5"], axis=0, keepdims=True)
    row = lax.broadcasted_iota(jnp.int32, (8, LANES), 0)
    sums_ref[...] = jnp.where(row == 0, sum_q, jnp.where(row == 1, sum_v, 0.0))


def attend(core, q, k, v, k_other, v_other, keep_weights):
    length, width = q.shape
    rows = length // 2
    column = pl.BlockSpec((length, LANES), lambda i: (0, i))
    shapes = [jax.ShapeDtypeStruct((length, width), BF16)]
    outs = [column]
    if keep_weights:
        shapes.append(pltpu.HBM((width // HEAD, 5, rows, rows), BF16))
        outs.append(pl.BlockSpec((2, 5, rows, rows), lambda i: (i, 0, 0, 0)))
    return pl.pallas_call(
        functools.partial(attend_kernel, keep_weights),
        grid=(width // LANES,),
        out_shape=shapes,
        in_specs=[pl.BlockSpec(memory_space=pltpu.SMEM)] + [column] * 5,
        out_specs=outs,
        compiler_params=pltpu.CompilerParams(vmem_limit_bytes=40 * 1024 * 1024),
        cost_estimate=pl.CostEstimate(
            flops=20 * rows * rows * width * 2, bytes_accessed=16 * length * width, transcendentals=0
        ),
        name="attend",
    )(core, q, k, v, k_other, v_other)


def attend_back(core, q, k, v, k_other, v_other, grad_mixed, mixed, weights):
    length, width = q.shape
    rows = length // 2
    column = pl.BlockSpec((length, LANES), lambda i: (0, i))
    double = pl.BlockSpec((2, length, LANES), lambda i: (0, 0, i))
    return pl.pallas_call(
        attend_back_kernel,
        grid=(width // LANES,),
        out_shape=[
            jax.ShapeDtypeStruct((length, width), BF16),
            jax.ShapeDtypeStruct((2, length, width), F32),
            jax.ShapeDtypeStruct((2, length, width), BF16),
            jax.ShapeDtypeStruct((8, width), F32),
        ],
        in_specs=[pl.BlockSpec(memory_space=pltpu.SMEM)]
        + [column] * 7
        + [pl.BlockSpec((2, 5, rows, rows), lambda i: (i, 0, 0, 0))],
        out_specs=[column, double, double, pl.BlockSpec((8, LANES), lambda i: (0, i))],
        compiler_params=pltpu.CompilerParams(vmem_limit_bytes=40 * 1024 * 1024),
        cost_estimate=pl.CostEstimate(
            flops=40 * rows * rows * width * 2, bytes_accessed=40 * length * width, transcendentals=0
        ),
        name="attend_back",
    )(core, q, k, v, k_other, v_other, grad_mixed, mixed, weights)


def gelu_and_slope(values):
    root = float(np.sqrt(2 / np.pi))
    cubic = 0.044715 * root
    square = values * values
    bend = jnp.tanh(values * (root + cubic * square))
    half = 0.5 + 0.5 * bend
    gate = values * half
    slope = half + gate * ((1.0 - bend) * (root + (3 * cubic) * square))
    return (gate, slope)


def tiles_of(units):
    return units // 512 if units % 512 == 0 else 1


def expand_kernel(rows_ref, expand_ref, bias_ref, reduce_ref, start_ref, total_ref):
    units = expand_ref.shape[0]
    piece = 256 if units % 256 == 0 else units
    rows = rows_ref[...]
    total = None
    for offset in range(0, units, piece):
        part = pl.ds(offset, piece)
        gate, _ = gelu_and_slope(nt(rows, expand_ref[part, :]) + bias_ref[:, part])
        term = nn(gate.astype(BF16), reduce_ref[part, :])
        total = term if total is None else total + term

    @pl.when(pl.program_id(0) == 0)
    def _():
        total_ref[...] = start_ref[...] + total

    @pl.when(pl.program_id(0) > 0)
    def _():
        total_ref[...] += total


def feed_half(rows, expand_w, bias, reduce_w, start, row_part=None):
    length, width = rows.shape
    units = expand_w.shape[0]
    steps = tiles_of(units)
    tile = units // steps
    if row_part is not None:
        length = length // 2
    place = row_part or 0
    whole = pl.BlockSpec((length, width), lambda i: (0, 0))
    taken = pl.BlockSpec((length, width), lambda i: (place, 0))
    weight = pl.BlockSpec((tile, width), lambda i: (i, 0))
    return pl.pallas_call(
        expand_kernel,
        grid=(steps,),
        out_shape=jax.ShapeDtypeStruct((length, width), F32),
        in_specs=[taken, weight, pl.BlockSpec((1, tile), lambda i: (0, i)), weight, taken],
        out_specs=whole,
        compiler_params=pltpu.CompilerParams(vmem_limit_bytes=40 * 1024 * 1024),
        cost_estimate=pl.CostEstimate(
            flops=4 * length * width * units, bytes_accessed=4 * width * units, transcendentals=0
        ),
        name="feed_half",
    )(rows, expand_w, bias.reshape(1, units), reduce_w, start)


def both_kernel(
    steps, rows_ref, grad_ref, e0_ref, e1_ref, b0_ref, b1_ref, r0_ref, r1_ref,
    total_ref, grad_total_ref, h0_ref, h1_ref, s0_ref, s1_ref,
):
    place = pl.program_id(0)

    @pl.when(place == 0)
    def _():
        total_ref[...] = jnp.zeros_like(total_ref)
        grad_total_ref[...] = jnp.zeros_like(grad_total_ref)

    def tile(expand_ref, bias_ref, reduce_ref, hidden_ref, slope_ref):
        gate, slope = gelu_and_slope(nt(rows_ref[...], expand_ref[...]) + bias_ref[...])
        hidden = gate.astype(BF16)
        slope = slope.astype(BF16)
        hidden_ref[...] = hidden
        slope_ref[...] = slope
        total_ref[...] += nn(hidden, reduce_ref[...])
        pre = nt(grad_ref[...], reduce_ref[...]) * slope.astype(F32)
        grad_total_ref[...] += nn(pre.astype(BF16), expand_ref[...])

    @pl.when(place < steps)
    def _():
        tile(e0_ref, b0_ref, r0_ref, h0_ref, s0_ref)

    @pl.when(place >= steps)
    def _():
        tile(e1_ref, b1_ref, r1_ref, h1_ref, s1_ref)


def back_kernel(
    steps, grad_ref, e0_ref, e1_ref, r0_ref, r1_ref, s0_ref, s1_ref,
    total_ref, p0_ref, p1_ref, sums0_ref, sums1_ref,
):
    place = pl.program_id(0)

    @pl.when(place == 0)
    def _():
        total_ref[...] = jnp.zeros_like(total_ref)

    def tile(expand_ref, reduce_ref, slope_ref, pre_ref, sums_ref):
        pre = nt(grad_ref[...], reduce_ref[...]) * slope_ref[...].astype(F32)
        sums_ref[...] = jnp.broadcast_to(jnp.sum(pre, axis=0, keepdims=True), sums_ref.shape)
        rounded = pre.astype(BF16)
        pre_ref[...] = rounded
        total_ref[...] += nn(rounded, expand_ref[...])

    @pl.when(place < steps)
    def _():
        tile(e0_ref, r0_ref, s0_ref, p0_ref, sums0_ref)

    @pl.when(place >= steps)
    def _():
        tile(e1_ref, r1_ref, s1_ref, p1_ref, sums1_ref)


def feed_specs(length, width, units):
    steps = tiles_of(units)
    tile = units // steps
    whole = pl.BlockSpec((length, width), lambda i: (0, 0))

    def early(i):
        return jnp.minimum(i, steps - 1)

    def late(i):
        return jnp.maximum(i - steps, 0)

    weight = [pl.BlockSpec((tile, width), lambda i, f=f: (f(i), 0)) for f in (early, late)]
    across = [pl.BlockSpec((length, tile), lambda i, f=f: (0, f(i))) for f in (early, late)]
    row = [pl.BlockSpec((1, tile), lambda i, f=f: (0, f(i))) for f in (early, late)]
    rows = [pl.BlockSpec((8, tile), lambda i, f=f: (0, f(i))) for f in (early, late)]
    return steps, whole, weight, across, row, rows


def feed_both(rows, grad, halves):
    length, width = rows.shape
    units = halves[0][0].shape[0]
    steps, whole, weight, across, row, _ = feed_specs(length, width, units)
    total = jax.ShapeDtypeStruct((length, width), F32)
    kept = jax.ShapeDtypeStruct((length, units), BF16)
    (e0, b0, r0), (e1, b1, r1) = halves
    return pl.pallas_call(
        functools.partial(both_kernel, steps),
        grid=(2 * steps,),
        out_shape=[total, total, kept, kept, kept, kept],
        in_specs=[whole, whole, *weight, *row, *weight],
        out_specs=[whole, whole, *across, *across],
        compiler_params=pltpu.CompilerParams(vmem_limit_bytes=40 * 1024 * 1024),
        cost_estimate=pl.CostEstimate(
            flops=16 * length * width * units, bytes_accessed=8 * width * units, transcendentals=0
        ),
        name="feed_both",
    )(rows, grad, e0, e1, b0.reshape(1, units), b1.reshape(1, units), r0, r1)


def feed_back(grad, halves, slope):
    length, width = grad.shape
    units = halves[0][0].shape[0]
    steps, whole, weight, across, _, rows = feed_specs(length, width, units)
    kept = jax.ShapeDtypeStruct((length, units), BF16)
    sums = jax.ShapeDtypeStruct((8, units), F32)
    (e0, _, r0), (e1, _, r1) = halves
    return pl.pallas_call(
        functools.partial(back_kernel, steps),
        grid=(2 * steps,),
        out_shape=[jax.ShapeDtypeStruct((length, width), F32), kept, kept, sums, sums],
        in_specs=[whole, *weight, *weight, *across],
        out_specs=[whole, *across, *rows],
        compiler_params=pltpu.CompilerParams(vmem_limit_bytes=40 * 1024 * 1024),
        cost_estimate=pl.CostEstimate(
            flops=8 * length * width * units, bytes_accessed=8 * width * units, transcendentals=0
        ),
        name="feed_back",
    )(grad, e0, e1, r0, r1, *slope)


def tie(value, *others):
    return lax.optimization_barrier((value, *others))[0]


def normalize_rows(rows):
    centred = rows - jnp.mean(rows, axis=-1, keepdims=True)
    inverse = lax.rsqrt(jnp.mean(centred * centred, axis=-1, keepdims=True) + EPSILON)
    return (centred * inverse, inverse)


def norm_backward(grad_normed, normed, inverse, gain):
    scaled = grad_normed * gain
    centred = scaled - jnp.mean(scaled, axis=-1, keepdims=True)
    return inverse * (centred - normed * jnp.mean(scaled * normed, axis=-1, keepdims=True))


def attention_forward(core, rows_in, weights, keep, before=(), after=()):
    gain_a, shift_a, proj, bias_q, bias_v, bias_out = weights
    normed_one, inverse_one = normalize_rows(rows_in)
    ready_one = narrow(normed_one * gain_a + shift_a)
    k = narrow(nt(ready_one, proj[1]))
    k_other = swap(k, "core")
    v = narrow(nt(ready_one, proj[2]) + bias_v)
    v_other = swap(v, "core")
    q = narrow(nt(ready_one, proj[0]) + bias_q)
    if before:
        q, *before = lax.optimization_barrier((q, *before))
        after = [*after[:-2], *after[-1](before)]
    mixed, *kept_weights = attend(core, q, k, v, k_other, v_other, keep)
    mixed, *after = lax.optimization_barrier((mixed, *after))
    middle = rows_in + BRANCH * (nn(mixed, proj[3]) + bias_out)
    kept = (normed_one, inverse_one, ready_one, (q, k, v, k_other, v_other), mixed, *kept_weights)
    return middle, kept, after


def feed_start(middle, weights):
    gain_b, shift_b, _, _ = weights
    normed_two, inverse_two = normalize_rows(middle)
    return normed_two, inverse_two, narrow(normed_two * gain_b + shift_b)


def feed_forward_only(middle, weights):
    ready_two = feed_start(middle, weights)[2]
    first, second = weights[2]
    total = feed_half(ready_two, *first, jnp.broadcast_to(weights[3], middle.shape))
    block = middle.shape[0] // 2
    results = []
    for part in range(2):
        rows = slice(part * block, (part + 1) * block)
        piece = feed_half(ready_two, *second, tie(total, *results), part)
        results.append(narrow(middle[rows] + BRANCH * piece))
    return results


def feed_forward_and_back(middle, grad_result, weights):
    normed_two, inverse_two, ready_two = feed_start(middle, weights)
    rounded = narrow(BRANCH * grad_result)
    total, grad_total, *kept = feed_both(ready_two, rounded, weights[2])
    result = narrow(middle + BRANCH * (total + weights[3]))
    grad_middle = grad_result + norm_backward(grad_total, normed_two, inverse_two, weights[0])
    return result, grad_middle, (normed_two, inverse_two, ready_two, kept[:2], kept[2:])


def attention_backward(core, kept, grad_middle, weights, before=(), after=()):
    gain_a, _, proj, _, _, _ = weights
    normed_one, inverse_one, ready_one, projected, mixed, attention = kept
    grad_attended = BRANCH * grad_middle
    rounded_attended = narrow(grad_attended)
    grad_mixed = narrow(nt(tie(rounded_attended, *before), proj[3]))
    grad_q, own, other, sums = attend_back(core, *projected, grad_mixed, mixed, attention)
    other, *after = lax.optimization_barrier((other, *after))
    grad_kv = narrow(own + swap(other, "core").astype(F32))
    grad_normed_one = nn(grad_q, proj[0]) + nn(grad_kv[0], proj[1]) + nn(grad_kv[1], proj[2])
    grad_in = grad_middle + norm_backward(grad_normed_one, normed_one, inverse_one, gain_a)
    shared = [grad_normed_one * normed_one, grad_normed_one, grad_attended]
    return grad_in, rounded_attended, (grad_q, grad_kv[0], grad_kv[1]), sums[:2], shared, after


def narrow(value):
    return value.astype(BF16)


def wide_add(left, right):
    return narrow(left.astype(F32) + right.astype(F32))


def over_groups(value):
    return lax.psum(value, "outer") if lax.axis_size("outer") > 1 else value


def ring_add(parts):
    count = len(parts)
    total = parts[1 % count]
    for step in range(1, count):
        total = wide_add(ring(total), parts[(step + 1) % count])
    return total


def thirds(values):
    pieces = []
    for _ in range(3):
        piece = lax.reduce_precision(values, 8, 7)
        pieces.append(narrow(piece))
        values = values - piece
    return jnp.stack(pieces)


def shards(
    inputs, cotangent, gain_one, shift_one, attend_in, attend_bias, attend_out, out_bias,
    gain_two, shift_two, expand_in, expand_bias, reduce_out, reduce_bias,
):
    count = lax.axis_size("tensor")
    x, y, c, z = (lax.axis_index(axis) for axis in AXES)
    is_first = x == 0
    core = c.reshape(1).astype(jnp.int32)
    width = attend_in.shape[1]
    local = attend_in.shape[3]
    units = expand_in.shape[2]
    part = units // 4
    spare = 16

    def either(index, pair):
        first, second = pair
        return jnp.where(index == 0, first, second), jnp.where(index == 0, second, first)

    def relative(blocks):
        rows = [either(y, blocks[:2]), either(y, blocks[2:])]
        return list(zip(*(either(c, pair) for pair in zip(*rows))))

    def quarters(value, axis):
        return relative(jnp.split(value, 4, axis))

    typed = [*attend_in[0].transpose(1, 2, 0), attend_out[0]]
    (mine, mine_y), _ = relative(typed)
    biases = thirds(jnp.concatenate([attend_bias[0].reshape(2 * local), expand_bias[0]])).reshape(-1)
    biases = jnp.pad(biases, (0, spare * width - biases.size)).reshape(spare, width)
    piece = jnp.concatenate([mine, biases])
    bias_rows = [biases]
    own_parts = [quarters(expand_in[0].T, 0), quarters(reduce_out[0], 0)]
    feed = [jnp.concatenate([value[0][0] for value in own_parts])]
    feed_y = [jnp.concatenate([value[0][1] for value in own_parts])]
    pieces, pieces_y = [ring(piece)], []
    arrived = fetch(inputs[0, 0], 0)
    while len(pieces) < count - 1:
        pieces_y.append(swap(pieces[-1][:local], "y"))
        pieces.append(ring(pieces[-1]))
        pieces[-1], pieces_y[-1], feed[0], *arrived = lax.optimization_barrier(
            (pieces[-1], pieces_y[-1], feed[0], *arrived)
        )
        if len(pieces) == count - 1:
            feed.append(ring(feed[0]))
    pieces_y.append(swap(pieces[-1][:local], "y"))
    feed[1], pieces_y[-1] = lax.optimization_barrier((feed[1], pieces_y[-1]))
    feed_y.append(swap(feed[1], "y"))
    feed.append(ring(feed[1]))
    before = (feed[2], feed_y[1])
    bias_rows += [value[local:] for value in pieces]
    pieces = [mine] + [value[:local] for value in pieces]
    pieces_y = [mine_y] + pieces_y
    pieces = jnp.concatenate(pieces)
    pieces_y = jnp.concatenate(pieces_y)
    proj = relative([pieces, pieces_y, swap(pieces, "core"), swap(pieces_y, "core")])
    proj = [*proj[0], *proj[1]]
    biases = jnp.stack(bias_rows).reshape(count, -1)[:, : 3 * (2 * local + units)].reshape(count, 3, 2 * local + units)
    biases = biases.astype(F32)
    biases = biases[:, 0] + (biases[:, 1] + biases[:, 2])
    bias_q, bias_v = biases[:, :local].reshape(width), biases[:, local : 2 * local].reshape(width)
    expand_b = quarters(biases[:, 2 * local :], 1)
    expand_b = [jnp.concatenate([value.reshape(count * part) for value in pair]) for pair in expand_b]
    attention_weights = (gain_one[0], shift_one[0], proj, bias_q, bias_v, out_bias[0])

    rows_in = jnp.concatenate(arrived)
    middle, _, after = attention_forward(
        core, rows_in.astype(F32), attention_weights, False, before,
        (before, lambda ready: (ring(ready[0]), swap(ready[0], "y"))),
    )
    feed.append(after[0])
    feed_y += [after[1], swap(after[0], "y")]
    own_half = [
        jnp.concatenate([value[kind * part : (kind + 1) * part] for value in feed + feed_y]) for kind in range(2)
    ]
    other_half = [swap(value, "core") for value in own_half]
    feed_weights = (
        gain_two[0],
        shift_two[0],
        [(own_half[0], expand_b[0], own_half[1]), (other_half[0], expand_b[1], other_half[1])],
        reduce_bias[0],
    )
    passed = jnp.concatenate([along_pipe(rows, 1) for rows in feed_forward_only(middle, feed_weights)])
    last = jnp.concatenate(fetch(tie(cotangent[0, 0], passed), 1))
    rows_in = jnp.where(is_first, rows_in, passed)
    middle, kept_attention, _ = attention_forward(core, rows_in.astype(F32), attention_weights, True)
    result, grad_middle, kept_feed = feed_forward_and_back(middle, last.astype(F32), feed_weights)
    block = result.shape[0] // 2
    outputs = give_back(result[:block], result[block:], 1)
    grad_in, _, _, _, _, (outputs,) = attention_backward(
        core, kept_attention, grad_middle, attention_weights, (), (outputs,)
    )
    grad_in = narrow(grad_in)
    returned = jnp.concatenate([along_pipe(grad_in[:block], -1), along_pipe(grad_in[block:], -1)])
    grad_result = jnp.where(is_first, returned, last).astype(F32)
    grad_outcome = BRANCH * grad_result
    rounded_outcome = narrow(grad_outcome)
    normed_two, inverse_two, ready_two, hidden, slope = kept_feed
    span = count * part

    def by_slot(value):
        return [value[slot * part : (slot + 1) * part] for slot in range(count)]

    def steps_of(parts):
        state = [parts[1 % count]]

        def start():
            state.append(ring(state[-1]))
            return state[-1]

        def finish(arrived, step):
            state.append(wide_add(arrived, parts[(step + 1) % count]))
            return state[-1]

        return start, finish

    send = narrow(tn(hidden[1], rounded_outcome))
    arrived = swap(send, "core")
    keep = tn(hidden[0], tie(rounded_outcome, send))
    total, pre_own, pre_other, sums_own, sums_other = feed_back(tie(rounded_outcome, keep), feed_weights[2], slope)
    reduce_sums = wide_add(keep, tie(arrived, total))
    reduce_y = swap(reduce_sums[span:], "y")
    total = tie(total, reduce_sums)
    grad_middle = grad_result + norm_backward(total, normed_two, inverse_two, gain_two[0])
    shared_feed = [total * normed_two, total, grad_outcome]
    send = narrow(tn(tie(pre_other, grad_middle), ready_two))
    arrived = swap(send, "core")
    keep = tn(pre_own, tie(ready_two, send))
    expand_sums = wide_add(keep, tie(arrived, keep))
    expand_parts = [jnp.concatenate(pair) for pair in zip(by_slot(expand_sums[:span]), by_slot(expand_sums[span:]))]
    expand_start, expand_finish = steps_of(expand_parts)
    grad_in, rounded_attended, grad_qkv, sums_qv, shared_attention, after = attention_backward(
        core, kept_attention, grad_middle, attention_weights, expand_parts, (expand_start(), reduce_y)
    )
    expand_step = expand_finish(after[0], 1)
    reduce_parts = by_slot(wide_add(reduce_sums[:span], after[1]))
    reduce_start, reduce_finish = steps_of(reduce_parts)
    grad_qkv = lax.optimization_barrier((*grad_qkv, expand_step, *reduce_parts))[:3]
    grad_in = narrow(grad_in)
    expand_step = expand_start()
    mixed, ready_one = kept_attention[4], kept_attention[2]
    left = jnp.stack([*grad_qkv, mixed])
    index = 2 * c + y

    def typed_grad(shift):
        right = jnp.where((index ^ shift) == 3, rounded_attended, ready_one)
        return tn(lax.dynamic_index_in_dim(left, index ^ shift, 0, False), right)

    send = [narrow(typed_grad(shift)) for shift in (3, 2)]
    arrived = [swap(value, "core") for value in send]
    left = tie(left, *send)
    keep = [typed_grad(shift) for shift in (1, 0)]
    expand_step, keep[1] = lax.optimization_barrier((expand_step, keep[1]))
    expand_step = expand_finish(expand_step, 2)
    shared = shared_attention + shared_feed
    shared = jnp.stack([jnp.sum(value, axis=0) for value in shared])
    sums_qv = sums_qv.reshape(2, count, local)
    sums_qv = jnp.concatenate([sums_qv[0], sums_qv[1], jnp.zeros((count, width - 2 * local), F32)], axis=1)[:, None]
    sums_pre = [value.reshape(count, part) for half in (sums_own[0], sums_other[0]) for value in jnp.split(half, 2)]
    sums_pre = quarters(jnp.concatenate(sums_pre, axis=1), 1)
    sums_pre = jnp.concatenate(sums_pre[0] + sums_pre[1], axis=1)[:, None]
    vectors = jnp.concatenate([jnp.broadcast_to(shared, (count,) + shared.shape), sums_qv, sums_pre], axis=1)
    vectors = jnp.pad(vectors, ((0, 0), (0, spare - 8), (0, 0)))
    vectors = vectors + swap(vectors, "core")

    sums = [wide_add(a, b) for a, b in zip(keep, arrived)]
    to_y, to_keep = by_slot(sums[0]), by_slot(sums[1])
    typed_parts = [None] * count

    def typed_swap(slot):
        return swap(to_y[slot], "y")

    moving_y, moving_e, vectors_y = typed_swap(1), expand_start(), swap(vectors, "y")
    moving_y, vectors_y, to_y[2] = lax.optimization_barrier((moving_y, vectors_y, to_y[2]))
    typed_parts[1] = wide_add(to_keep[1], moving_y)
    vectors = narrow(vectors + vectors_y)
    reduce_parts = [jnp.concatenate([a, b]) for a, b in zip(reduce_parts, vectors)]
    reduce_start, reduce_finish = steps_of(reduce_parts)
    typed_start, typed_finish = steps_of(typed_parts)
    moving_t, moving_y, moving_r = typed_start(), typed_swap(2), reduce_start()
    moving_t, moving_y, moving_e = lax.optimization_barrier((moving_t, moving_y, moving_e))
    typed_parts[2] = wide_add(to_keep[2], moving_y)
    typed_finish(moving_t, 1)
    expand_total = expand_finish(moving_e, 3).reshape(2, part, width)
    moving_t, moving_y, expand_other = typed_start(), typed_swap(3), swap(expand_total, "y")
    moving_t, moving_y, moving_r = lax.optimization_barrier((moving_t, moving_y, moving_r))
    typed_parts[3] = wide_add(to_keep[3], moving_y)
    typed_finish(moving_t, 2)
    reduce_finish(moving_r, 1)
    moving_t, moving_y, moving_r = typed_start(), typed_swap(0), reduce_start()
    moving_t, moving_y, moving_r, expand_other = lax.optimization_barrier((moving_t, moving_y, moving_r, expand_other))
    typed_parts[0] = wide_add(to_keep[0], moving_y)
    typed_total = typed_finish(moving_t, 3)
    reduce_finish(moving_r, 2)
    reduce_total = reduce_finish(reduce_start(), 3)
    grad_in = tie(grad_in, moving_t)
    input_grad = give_back(grad_in[:block], grad_in[block:], 0)
    def gathered(pair):
        pair = jnp.concatenate(pair)
        blocks = quarters(jnp.concatenate([pair, swap(pair, "core")]), 0)
        return jnp.concatenate(blocks[0] + blocks[1])

    grad_expand = [over_groups(wide_add(expand_total[i], expand_other[1 - i])) for i in range(2)]
    grad_expand = gathered(grad_expand).T.astype(F32)
    typed_total = over_groups(typed_total)
    pair = jnp.concatenate([typed_total, swap(typed_total, "y")])
    pair_other = swap(pair, "core")
    whole = relative([pair[:local], pair[local:], pair_other[:local], pair_other[local:]])
    whole = [*whole[0], *whole[1]]
    grad_attend_in = jnp.stack(whole[:3]).transpose(2, 0, 1).astype(F32)
    grad_attend_out = whole[3].astype(F32)
    reduce_total = over_groups(reduce_total)
    vectors = reduce_total[part : part + 8].astype(F32)
    reduce_total = reduce_total[:part]
    grad_reduce = gathered([reduce_total, swap(reduce_total, "y")]).astype(F32)
    return (
        outputs[None, None],
        input_grad[None, None],
        vectors[0][None],
        vectors[1][None],
        grad_attend_in[None],
        vectors[6, : 2 * local].reshape(1, 2, local),
        grad_attend_out[None],
        vectors[2][None],
        vectors[3][None],
        vectors[4][None],
        grad_expand[None],
        vectors[7, :units][None],
        grad_reduce[None],
        vectors[5][None],
    )


def solution(mesh):
    pipe, groups, count = mesh.devices.shape
    split = Mesh(mesh.devices.reshape(pipe, groups // 4, 2, 2, count), ("pipe", "outer", "y", "core", "tensor"))
    dp = ("outer", "y", "core")
    rows = P("pipe", dp, "tensor", None)
    vector = P("pipe", None)
    placed = (
        rows,
        rows,
        vector,
        vector,
        P("pipe", None, None, "tensor"),
        P("pipe", None, "tensor"),
        P("pipe", "tensor", None),
        vector,
        vector,
        vector,
        P("pipe", None, "tensor"),
        P("pipe", "tensor"),
        P("pipe", "tensor", None),
        vector,
    )
    return jax.shard_map(shards, mesh=split, in_specs=placed, out_specs=(rows, rows) + placed[2:], check_vma=False)
```

```python
import functools

import jax
import jax.numpy as jnp
import numpy as np
from jax import lax
from jax.experimental import pallas as pl
from jax.experimental.pallas import tpu as pltpu
from jax.sharding import Mesh
from jax.sharding import PartitionSpec as P

HEAD = 64
DEPTH = 12
BRANCH = DEPTH ** (-0.5)
EPSILON = 1e-05
NEGATIVE = -1e30
LANES = 128
AXES = ("pipe", "y", "core", "tensor")
F32 = jnp.float32
BF16 = jnp.bfloat16


def ring_order(count):
    return list(range(0, count, 2)) + list(range(1, count, 2))[::-1]


def ring(value):
    order = ring_order(lax.axis_size("tensor"))
    return lax.ppermute(value, "tensor", list(zip(order, order[1:] + order[:1])))


def swap(value, axis):
    return lax.ppermute(value, axis, [(0, 1), (1, 0)])


def along_pipe(value, by):
    return lax.ppermute(value, "pipe", [(0, 1)] if by > 0 else [(1, 0)])


def routes(section, large):
    count = lax.axis_size("tensor")

    def index(x, y, c, z):
        return ((x * 2 + y) * 2 + c) * count + z

    pairs = []
    for micro in range(2):
        for y in range(2):
            for c in range(2):
                for core in range(2):
                    block = 3 - core if large else core
                    pairs.append((index(micro, y, c, block), index(section, y, core, 2 * micro + c)))
    return pairs


def fetch(block, section):
    return [lax.ppermute(block, AXES, routes(section, large)) for large in (False, True)]


def give_back(small, large, section):
    pieces = []
    for rows, is_large in ((small, False), (large, True)):
        pairs = [(b, a) for a, b in routes(section, is_large)]
        pieces.append(lax.ppermute(rows, AXES, pairs))
    return jnp.where(lax.axis_index("tensor") < 2, pieces[0], pieces[1])


def nt(left, right):
    return lax.dot_general(left, right, (((1,), (1,)), ((), ())), preferred_element_type=F32)


def tn(left, right):
    return lax.dot_general(left, right, (((0,), (0,)), ((), ())), preferred_element_type=F32)


def tk(left, right):
    turned = right.astype(F32).T.astype(BF16)
    return nn(turned, left).T


def nn(left, right):
    return lax.dot_general(left, right, (((1,), (0,)), ((), ())), preferred_element_type=F32)


def estimate(flops, size):
    return pl.CostEstimate(flops=flops, bytes_accessed=size, transcendentals=0)


def head_mask(rows, head):
    lanes = lax.broadcasted_iota(jnp.int32, (rows, LANES), 1)
    return (lanes >= head * HEAD) & (lanes < (head + 1) * HEAD)


def only(mask, value, factor=1.0):
    return jnp.where(mask, value.astype(F32) * factor, 0.0).astype(BF16)


def attend_kernel(keep_weights, core_ref, q_ref, k_ref, v_ref, ko_ref, vo_ref, o_ref, *p_refs):
    rows = q_ref.shape[0] // 2
    second = core_ref[0] == 1
    keys = lax.broadcasted_iota(jnp.int32, (rows, rows), 0)
    places = lax.broadcasted_iota(jnp.int32, (rows, rows), 1)
    allowed = keys <= places
    factor = HEAD ** (-0.5)
    small = pl.ds(0, rows)
    large = pl.ds(rows, rows)
    k5 = jnp.where(second, ko_ref[small, :].astype(F32), ko_ref[large, :].astype(F32)).astype(BF16)
    v5 = jnp.where(second, vo_ref[small, :].astype(F32), vo_ref[large, :].astype(F32))
    out_small = None
    out_large = None
    for head in range(LANES // HEAD):
        mask = head_mask(rows, head)

        def query(value):
            return only(mask, value, factor)

        qs, ql = query(q_ref[small, :]), query(q_ref[large, :])
        qf = query(jnp.where(second, q_ref[small, :].astype(F32), q_ref[large, :].astype(F32)))
        s1 = jnp.where(allowed, nt(k_ref[small, :], qs), NEGATIVE)
        s2 = nt(k_ref[small, :], ql)
        s3 = jnp.where(allowed, nt(k_ref[large, :], ql), NEGATIVE)
        s4 = nt(ko_ref[small, :], ql)
        s5 = nt(k5, qf)

        def peak(value):
            return jnp.max(value, axis=0, keepdims=True)

        def total(value):
            return jnp.sum(value, axis=0, keepdims=True)

        m5 = peak(s5)
        ms = peak(s1)
        ml = jnp.maximum(jnp.maximum(peak(s2), peak(s3)), peak(s4))
        ms = jnp.where(second, jnp.maximum(ms, m5), ms)
        ml = jnp.where(second, ml, jnp.maximum(ml, m5))
        mf = jnp.where(second, ms, ml)
        e1 = jnp.exp(s1 - ms)
        e2 = jnp.exp(s2 - ml)
        e3 = jnp.exp(s3 - ml)
        e4 = jnp.exp(s4 - ml)
        e5 = jnp.exp(s5 - mf)
        t5 = total(e5)
        rs = total(e1)
        rl = total(e2) + total(e3) + total(e4)
        rs = 1.0 / jnp.where(second, rs + t5, rs)
        rl = 1.0 / jnp.where(second, rl, rl + t5)
        rf = jnp.where(second, rs, rl)
        p1 = (e1 * rs).astype(BF16)
        p2 = (e2 * rl).astype(BF16)
        p3 = (e3 * rl).astype(BF16)
        p4 = (e4 * rl).astype(BF16)
        p5 = (e5 * rf).astype(BF16)
        if keep_weights:
            for place, value in enumerate((p1, p2, p3, p4, p5)):
                p_refs[0][head, place] = value
        vs = only(mask, v_ref[small, :])
        o5 = tk(p5, only(mask, v5))
        os = tk(p1, vs) + jnp.where(second, o5, 0.0)
        ol = (
            tk(p2, vs)
            + tk(p3, only(mask, v_ref[large, :]))
            + tk(p4, only(mask, vo_ref[small, :]))
            + jnp.where(second, 0.0, o5)
        )
        out_small = os if out_small is None else out_small + os
        out_large = ol if out_large is None else out_large + ol
    o_ref[small, :] = out_small.astype(BF16)
    o_ref[large, :] = out_large.astype(BF16)


def attend_back_kernel(
    core_ref, q_ref, k_ref, v_ref, ko_ref, vo_ref, go_ref, o_ref, p_ref, gq_ref, own_ref, other_ref, sums_ref
):
    rows = q_ref.shape[0] // 2
    second = core_ref[0] == 1
    factor = HEAD ** (-0.5)
    small = pl.ds(0, rows)
    large = pl.ds(rows, rows)

    def fifth(ref, first, last):
        return jnp.where(second, ref[first, :].astype(F32), ref[last, :].astype(F32))

    k5 = fifth(ko_ref, small, large)
    v5 = fifth(vo_ref, small, large).astype(BF16)
    q5 = fifth(q_ref, small, large)
    g5 = fifth(go_ref, small, large)
    product = go_ref[...].astype(F32) * o_ref[...].astype(F32)
    high = product.astype(BF16)
    low = (product - high.astype(F32)).astype(BF16)
    totals = {}

    def add(name, value):
        totals[name] = value if name not in totals else totals[name] + value

    for head in range(LANES // HEAD):
        mask = head_mask(rows, head)
        ones = jnp.where(head_mask(16, head), 1.0, 0.0).astype(BF16)
        inner = (nt(ones, high) + nt(ones, low))[0:1]
        ds_, dl_ = inner[:, :rows], inner[:, rows:]
        df_ = jnp.where(second, ds_, dl_)

        def weight(place):
            return p_ref[head, place]

        qs, ql, qf = (only(mask, value, factor) for value in (q_ref[small, :], q_ref[large, :], q5))
        gs, gl, gf = (only(mask, value) for value in (go_ref[small, :], go_ref[large, :], g5))

        def score_grad(place, values, rows_grad, shift):
            return (weight(place).astype(F32) * (nt(values, rows_grad) - shift)).astype(BF16)

        z1 = score_grad(0, v_ref[small, :], gs, ds_)
        z2 = score_grad(1, v_ref[small, :], gl, dl_)
        z3 = score_grad(2, v_ref[large, :], gl, dl_)
        z4 = score_grad(3, vo_ref[small, :], gl, dl_)
        z5 = score_grad(4, v5, gf, df_)
        k_small = only(mask, k_ref[small, :])
        gq5 = tk(z5, only(mask, k5))
        add("qs", tk(z1, k_small) + jnp.where(second, gq5, 0.0))
        add(
            "ql",
            tk(z2, k_small)
            + tk(z3, only(mask, k_ref[large, :]))
            + tk(z4, only(mask, ko_ref[small, :]))
            + jnp.where(second, 0.0, gq5),
        )
        add("ks", nn(z1, qs) + nn(z2, ql))
        add("kl", nn(z3, ql))
        add("k4", nn(z4, ql))
        add("k5", nn(z5, qf))
        add("vs", nn(weight(0), gs) + nn(weight(1), gl))
        add("vl", nn(weight(2), gl))
        add("v4", nn(weight(3), gl))
        add("v5", nn(weight(4), gf))
    gqs, gql = totals["qs"] * factor, totals["ql"] * factor
    gq_ref[small, :] = gqs.astype(BF16)
    gq_ref[large, :] = gql.astype(BF16)
    for place, name in enumerate("kv"):
        own_ref[place, small, :] = totals[name + "s"]
        own_ref[place, large, :] = totals[name + "l"]
        four, five = totals[name + "4"], totals[name + "5"]
        other_ref[place, small, :] = (four + jnp.where(second, five, 0.0)).astype(BF16)
        other_ref[place, large, :] = jnp.where(second, 0.0, five).astype(BF16)
    sum_q = jnp.sum(gqs, axis=0, keepdims=True) + jnp.sum(gql, axis=0, keepdims=True)
    sum_v = jnp.sum(totals["vs"] + totals["vl"] + totals["v4"] + totals["v5"], axis=0, keepdims=True)
    row = lax.broadcasted_iota(jnp.int32, (8, LANES), 0)
    sums_ref[...] = jnp.where(row == 0, sum_q, jnp.where(row == 1, sum_v, 0.0))


def attend(core, q, k, v, k_other, v_other, keep_weights):
    length, width = q.shape
    rows = length // 2
    column = pl.BlockSpec((length, LANES), lambda i: (0, i))
    shapes = [jax.ShapeDtypeStruct((length, width), BF16)]
    outs = [column]
    if keep_weights:
        shapes.append(pltpu.HBM((width // HEAD, 5, rows, rows), BF16))
        outs.append(pl.BlockSpec((2, 5, rows, rows), lambda i: (i, 0, 0, 0)))
    return pl.pallas_call(
        functools.partial(attend_kernel, keep_weights),
        grid=(width // LANES,),
        out_shape=shapes,
        in_specs=[pl.BlockSpec(memory_space=pltpu.SMEM)] + [column] * 5,
        out_specs=outs,
        compiler_params=pltpu.CompilerParams(vmem_limit_bytes=40 * 1024 * 1024),
        cost_estimate=estimate(20 * rows * rows * width * 2, 16 * length * width),
        name="attend",
    )(core, q, k, v, k_other, v_other)


def attend_back(core, q, k, v, k_other, v_other, grad_mixed, mixed, weights):
    length, width = q.shape
    rows = length // 2
    column = pl.BlockSpec((length, LANES), lambda i: (0, i))
    double = pl.BlockSpec((2, length, LANES), lambda i: (0, 0, i))
    return pl.pallas_call(
        attend_back_kernel,
        grid=(width // LANES,),
        out_shape=[
            jax.ShapeDtypeStruct((length, width), BF16),
            jax.ShapeDtypeStruct((2, length, width), F32),
            jax.ShapeDtypeStruct((2, length, width), BF16),
            jax.ShapeDtypeStruct((8, width), F32),
        ],
        in_specs=[pl.BlockSpec(memory_space=pltpu.SMEM)]
        + [column] * 7
        + [pl.BlockSpec((2, 5, rows, rows), lambda i: (i, 0, 0, 0))],
        out_specs=[column, double, double, pl.BlockSpec((8, LANES), lambda i: (0, i))],
        compiler_params=pltpu.CompilerParams(vmem_limit_bytes=40 * 1024 * 1024),
        cost_estimate=estimate(40 * rows * rows * width * 2, 40 * length * width),
        name="attend_back",
    )(core, q, k, v, k_other, v_other, grad_mixed, mixed, weights)


def gelu_and_slope(values):
    root = float(np.sqrt(2 / np.pi))
    cubic = 0.044715 * root
    square = values * values
    bend = jnp.tanh(values * (root + cubic * square))
    half = 0.5 + 0.5 * bend
    gate = values * half
    slope = half + gate * ((1.0 - bend) * (root + (3 * cubic) * square))
    return (gate, slope)


def tiles_of(units):
    return units // 512 if units % 512 == 0 else 1


def expand_kernel(rows_ref, expand_ref, bias_ref, reduce_ref, start_ref, total_ref):
    units = expand_ref.shape[0]
    piece = 256 if units % 256 == 0 else units
    rows = rows_ref[...]
    total = None
    for offset in range(0, units, piece):
        part = pl.ds(offset, piece)
        gate, _ = gelu_and_slope(nt(rows, expand_ref[part, :]) + bias_ref[:, part])
        term = nn(gate.astype(BF16), reduce_ref[part, :])
        total = term if total is None else total + term

    @pl.when(pl.program_id(0) == 0)
    def _():
        total_ref[...] = start_ref[...] + total

    @pl.when(pl.program_id(0) > 0)
    def _():
        total_ref[...] += total


def feed_half(rows, expand_w, bias, reduce_w, start, row_part=None):
    length, width = rows.shape
    units = expand_w.shape[0]
    steps = tiles_of(units)
    tile = units // steps
    if row_part is not None:
        length = length // 2
    place = row_part or 0
    whole = pl.BlockSpec((length, width), lambda i: (0, 0))
    taken = pl.BlockSpec((length, width), lambda i: (place, 0))
    weight = pl.BlockSpec((tile, width), lambda i: (i, 0))
    return pl.pallas_call(
        expand_kernel,
        grid=(steps,),
        out_shape=jax.ShapeDtypeStruct((length, width), F32),
        in_specs=[taken, weight, pl.BlockSpec((1, tile), lambda i: (0, i)), weight, taken],
        out_specs=whole,
        compiler_params=pltpu.CompilerParams(vmem_limit_bytes=40 * 1024 * 1024),
        cost_estimate=estimate(4 * length * width * units, 4 * width * units),
        name="feed_half",
    )(rows, expand_w, bias.reshape(1, units), reduce_w, start)


def both_kernel(
    steps, rows_ref, grad_ref, e0_ref, e1_ref, b0_ref, b1_ref, r0_ref, r1_ref,
    total_ref, grad_total_ref, h0_ref, h1_ref, s0_ref, s1_ref,
):
    place = pl.program_id(0)

    @pl.when(place == 0)
    def _():
        total_ref[...] = jnp.zeros_like(total_ref)
        grad_total_ref[...] = jnp.zeros_like(grad_total_ref)

    def tile(expand_ref, bias_ref, reduce_ref, hidden_ref, slope_ref):
        gate, slope = gelu_and_slope(nt(rows_ref[...], expand_ref[...]) + bias_ref[...])
        hidden = gate.astype(BF16)
        slope = slope.astype(BF16)
        hidden_ref[...] = hidden
        slope_ref[...] = slope
        total_ref[...] += nn(hidden, reduce_ref[...])
        pre = nt(grad_ref[...], reduce_ref[...]) * slope.astype(F32)
        grad_total_ref[...] += nn(pre.astype(BF16), expand_ref[...])

    @pl.when(place < steps)
    def _():
        tile(e0_ref, b0_ref, r0_ref, h0_ref, s0_ref)

    @pl.when(place >= steps)
    def _():
        tile(e1_ref, b1_ref, r1_ref, h1_ref, s1_ref)


def back_kernel(
    steps, grad_ref, e0_ref, e1_ref, r0_ref, r1_ref, s0_ref, s1_ref,
    total_ref, p0_ref, p1_ref, sums0_ref, sums1_ref,
):
    place = pl.program_id(0)

    @pl.when(place == 0)
    def _():
        total_ref[...] = jnp.zeros_like(total_ref)

    def tile(expand_ref, reduce_ref, slope_ref, pre_ref, sums_ref):
        pre = nt(grad_ref[...], reduce_ref[...]) * slope_ref[...].astype(F32)
        sums_ref[...] = jnp.broadcast_to(jnp.sum(pre, axis=0, keepdims=True), sums_ref.shape)
        rounded = pre.astype(BF16)
        pre_ref[...] = rounded
        total_ref[...] += nn(rounded, expand_ref[...])

    @pl.when(place < steps)
    def _():
        tile(e0_ref, r0_ref, s0_ref, p0_ref, sums0_ref)

    @pl.when(place >= steps)
    def _():
        tile(e1_ref, r1_ref, s1_ref, p1_ref, sums1_ref)


def feed_specs(length, width, units):
    steps = tiles_of(units)
    tile = units // steps
    whole = pl.BlockSpec((length, width), lambda i: (0, 0))

    def early(i):
        return jnp.minimum(i, steps - 1)

    def late(i):
        return jnp.maximum(i - steps, 0)

    weight = [pl.BlockSpec((tile, width), lambda i, f=f: (f(i), 0)) for f in (early, late)]
    across = [pl.BlockSpec((length, tile), lambda i, f=f: (0, f(i))) for f in (early, late)]
    row = [pl.BlockSpec((1, tile), lambda i, f=f: (0, f(i))) for f in (early, late)]
    rows = [pl.BlockSpec((8, tile), lambda i, f=f: (0, f(i))) for f in (early, late)]
    return steps, whole, weight, across, row, rows


def feed_both(rows, grad, halves):
    length, width = rows.shape
    units = halves[0][0].shape[0]
    steps, whole, weight, across, row, _ = feed_specs(length, width, units)
    total = jax.ShapeDtypeStruct((length, width), F32)
    kept = jax.ShapeDtypeStruct((length, units), BF16)
    (e0, b0, r0), (e1, b1, r1) = halves
    return pl.pallas_call(
        functools.partial(both_kernel, steps),
        grid=(2 * steps,),
        out_shape=[total, total, kept, kept, kept, kept],
        in_specs=[whole, whole, *weight, *row, *weight],
        out_specs=[whole, whole, *across, *across],
        compiler_params=pltpu.CompilerParams(vmem_limit_bytes=40 * 1024 * 1024),
        cost_estimate=estimate(16 * length * width * units, 8 * width * units),
        name="feed_both",
    )(rows, grad, e0, e1, b0.reshape(1, units), b1.reshape(1, units), r0, r1)


def feed_back(grad, halves, slope):
    length, width = grad.shape
    units = halves[0][0].shape[0]
    steps, whole, weight, across, _, rows = feed_specs(length, width, units)
    kept = jax.ShapeDtypeStruct((length, units), BF16)
    sums = jax.ShapeDtypeStruct((8, units), F32)
    (e0, _, r0), (e1, _, r1) = halves
    return pl.pallas_call(
        functools.partial(back_kernel, steps),
        grid=(2 * steps,),
        out_shape=[jax.ShapeDtypeStruct((length, width), F32), kept, kept, sums, sums],
        in_specs=[whole, *weight, *weight, *across],
        out_specs=[whole, *across, *rows],
        compiler_params=pltpu.CompilerParams(vmem_limit_bytes=40 * 1024 * 1024),
        cost_estimate=estimate(8 * length * width * units, 8 * width * units),
        name="feed_back",
    )(grad, e0, e1, r0, r1, *slope)


def tie(value, *others):
    return lax.optimization_barrier((value, *others))[0]


def normalize_rows(rows):
    centred = rows - jnp.mean(rows, axis=-1, keepdims=True)
    inverse = lax.rsqrt(jnp.mean(centred * centred, axis=-1, keepdims=True) + EPSILON)
    return (centred * inverse, inverse)


def norm_backward(grad_normed, normed, inverse, gain):
    scaled = grad_normed * gain
    centred = scaled - jnp.mean(scaled, axis=-1, keepdims=True)
    return inverse * (centred - normed * jnp.mean(scaled * normed, axis=-1, keepdims=True))


def attention_forward(core, rows_in, weights, keep, before=(), after=()):
    gain_a, shift_a, proj, bias_q, bias_v, bias_out = weights
    normed_one, inverse_one = normalize_rows(rows_in)
    ready_one = narrow(normed_one * gain_a + shift_a)
    k = narrow(nt(ready_one, proj[1]))
    k_other = swap(k, "core")
    v = narrow(nt(ready_one, proj[2]) + bias_v)
    v_other = swap(v, "core")
    q = narrow(nt(ready_one, proj[0]) + bias_q)
    if before:
        q, *before = lax.optimization_barrier((q, *before))
        after = after(before)
    mixed, *kept_weights = attend(core, q, k, v, k_other, v_other, keep)
    mixed, *after = lax.optimization_barrier((mixed, *after))
    middle = rows_in + BRANCH * (nn(mixed, proj[3]) + bias_out)
    kept = (normed_one, inverse_one, ready_one, (q, k, v, k_other, v_other), mixed, *kept_weights)
    return middle, kept, after


def feed_start(middle, weights):
    gain_b, shift_b, _, _ = weights
    normed_two, inverse_two = normalize_rows(middle)
    return normed_two, inverse_two, narrow(normed_two * gain_b + shift_b)


def feed_forward_only(middle, weights):
    ready_two = feed_start(middle, weights)[2]
    first, second = weights[2]
    total = feed_half(ready_two, *first, jnp.broadcast_to(weights[3], middle.shape))
    block = middle.shape[0] // 2
    results = []
    for part in range(2):
        rows = slice(part * block, (part + 1) * block)
        piece = feed_half(ready_two, *second, tie(total, *results), part)
        results.append(narrow(middle[rows] + BRANCH * piece))
    return results


def feed_forward_and_back(middle, grad_result, weights):
    normed_two, inverse_two, ready_two = feed_start(middle, weights)
    rounded = narrow(BRANCH * grad_result)
    total, grad_total, *kept = feed_both(ready_two, rounded, weights[2])
    result = narrow(middle + BRANCH * (total + weights[3]))
    grad_middle = grad_result + norm_backward(grad_total, normed_two, inverse_two, weights[0])
    return result, grad_middle, (normed_two, inverse_two, ready_two, kept[:2], kept[2:])


def attention_backward(core, kept, grad_middle, weights, before=(), after=()):
    gain_a, _, proj, _, _, _ = weights
    normed_one, inverse_one, ready_one, projected, mixed, attention = kept
    grad_attended = BRANCH * grad_middle
    rounded_attended = narrow(grad_attended)
    grad_mixed = narrow(nt(tie(rounded_attended, *before), proj[3]))
    grad_q, own, other, sums = attend_back(core, *projected, grad_mixed, mixed, attention)
    other, *after = lax.optimization_barrier((other, *after))
    grad_kv = narrow(own + swap(other, "core").astype(F32))
    grad_normed_one = nn(grad_q, proj[0]) + nn(grad_kv[0], proj[1]) + nn(grad_kv[1], proj[2])
    grad_in = grad_middle + norm_backward(grad_normed_one, normed_one, inverse_one, gain_a)
    shared = [grad_normed_one * normed_one, grad_normed_one, grad_attended]
    return grad_in, rounded_attended, (grad_q, grad_kv[0], grad_kv[1]), sums[:2], shared, after


def narrow(value):
    return value.astype(BF16)


def wide_add(left, right):
    return narrow(left.astype(F32) + right.astype(F32))


def over_groups(value):
    return lax.psum(value, "outer") if lax.axis_size("outer") > 1 else value


def ring_add(parts):
    count = len(parts)
    total = parts[1 % count]
    for step in range(1, count):
        total = wide_add(ring(total), parts[(step + 1) % count])
    return total


def thirds(values):
    pieces = []
    for _ in range(3):
        piece = lax.reduce_precision(values, 8, 7)
        pieces.append(narrow(piece))
        values = values - piece
    return jnp.stack(pieces)


def shards(
    inputs, cotangent, gain_one, shift_one, attend_in, attend_bias, attend_out, out_bias,
    gain_two, shift_two, expand_in, expand_bias, reduce_out, reduce_bias,
):
    count = lax.axis_size("tensor")
    x, y, c, z = (lax.axis_index(axis) for axis in AXES)
    is_first = x == 0
    core = c.reshape(1).astype(jnp.int32)
    width = attend_in.shape[1]
    local = attend_in.shape[3]
    units = expand_in.shape[2]
    part = units // 4
    spare = 16

    def either(index, pair):
        first, second = pair
        return jnp.where(index == 0, first, second), jnp.where(index == 0, second, first)

    def relative(blocks):
        rows = [either(y, blocks[:2]), either(y, blocks[2:])]
        return list(zip(*(either(c, pair) for pair in zip(*rows))))

    def quarters(value, axis):
        return relative(jnp.split(value, 4, axis))

    typed = [*attend_in[0].transpose(1, 2, 0), attend_out[0]]
    (mine, mine_y), _ = relative(typed)
    biases = thirds(jnp.concatenate([attend_bias[0].reshape(2 * local), expand_bias[0]])).reshape(-1)
    biases = jnp.pad(biases, (0, spare * width - biases.size)).reshape(spare, width)
    piece = jnp.concatenate([mine, biases])
    bias_rows = [biases]
    own_parts = [quarters(expand_in[0].T, 0), quarters(reduce_out[0], 0)]
    feed = [jnp.concatenate([value[0][0] for value in own_parts])]
    feed_y = [jnp.concatenate([value[0][1] for value in own_parts])]
    pieces, pieces_y = [ring(piece)], []
    arrived = fetch(inputs[0, 0], 0)
    while len(pieces) < count - 1:
        pieces_y.append(swap(pieces[-1][:local], "y"))
        pieces.append(ring(pieces[-1]))
        if len(pieces) < count - 1:
            pieces[-1], pieces_y[-1], feed[0], *arrived = lax.optimization_barrier(
                (pieces[-1], pieces_y[-1], feed[0], *arrived)
            )
    feed.append(ring(feed[0]))
    pieces[-1], pieces_y[-1] = lax.optimization_barrier((pieces[-1], pieces_y[-1]))
    pieces_y.append(swap(pieces[-1][:local], "y"))
    feed[1], pieces_y[-1] = lax.optimization_barrier((feed[1], pieces_y[-1]))
    feed_y.append(swap(feed[1], "y"))
    feed.append(ring(feed[1]))
    feed[2], feed_y[1] = lax.optimization_barrier((feed[2], feed_y[1]))
    feed_y.append(swap(feed[2], "y"))
    before = (ring(feed[2]), feed_y[2])
    bias_rows += [value[local:] for value in pieces]
    pieces = [mine] + [value[:local] for value in pieces]
    pieces_y = [mine_y] + pieces_y
    pieces = jnp.concatenate(pieces)
    pieces_y = jnp.concatenate(pieces_y)
    proj = relative([pieces, pieces_y, swap(pieces, "core"), swap(pieces_y, "core")])
    proj = [*proj[0], *proj[1]]
    biases = jnp.stack(bias_rows).reshape(count, -1)[:, : 3 * (2 * local + units)].reshape(count, 3, 2 * local + units)
    biases = biases.astype(F32)
    biases = biases[:, 0] + (biases[:, 1] + biases[:, 2])
    bias_q, bias_v = biases[:, :local].reshape(width), biases[:, local : 2 * local].reshape(width)
    expand_b = quarters(biases[:, 2 * local :], 1)
    expand_b = [jnp.concatenate([value.reshape(count * part) for value in pair]) for pair in expand_b]
    attention_weights = (gain_one[0], shift_one[0], proj, bias_q, bias_v, out_bias[0])

    rows_in = jnp.concatenate(arrived)
    middle, _, after = attention_forward(
        core, rows_in.astype(F32), attention_weights, False, before,
        lambda ready: (*ready, swap(ready[0], "y")),
    )
    feed.append(after[0])
    feed_y[2:] = after[1:]
    own_half = [
        jnp.concatenate([value[kind * part : (kind + 1) * part] for value in feed + feed_y]) for kind in range(2)
    ]
    other_half = [swap(value, "core") for value in own_half]
    feed_weights = (
        gain_two[0],
        shift_two[0],
        [(own_half[0], expand_b[0], own_half[1]), (other_half[0], expand_b[1], other_half[1])],
        reduce_bias[0],
    )
    passed = jnp.concatenate([along_pipe(rows, 1) for rows in feed_forward_only(middle, feed_weights)])
    last = fetch(tie(cotangent[0, 0], passed), 1)
    rows_in = jnp.where(is_first, rows_in, passed)
    middle, kept_attention, last = attention_forward(
        core, rows_in.astype(F32), attention_weights, True, (), last
    )
    last = jnp.concatenate(last)
    result, grad_middle, kept_feed = feed_forward_and_back(middle, last.astype(F32), feed_weights)
    block = result.shape[0] // 2
    outputs = give_back(result[:block], result[block:], 1)
    grad_in, _, _, _, _, (outputs,) = attention_backward(
        core, kept_attention, grad_middle, attention_weights, (), (outputs,)
    )
    grad_in = narrow(grad_in)
    returned = jnp.concatenate([along_pipe(grad_in[:block], -1), along_pipe(grad_in[block:], -1)])
    grad_result = jnp.where(is_first, returned, last).astype(F32)
    grad_outcome = BRANCH * grad_result
    rounded_outcome = narrow(grad_outcome)
    normed_two, inverse_two, ready_two, hidden, slope = kept_feed
    span = count * part

    def by_slot(value):
        return [value[slot * part : (slot + 1) * part] for slot in range(count)]

    def steps_of(parts):
        state = [parts[1 % count]]

        def start():
            state.append(ring(state[-1]))
            return state[-1]

        def finish(arrived, step):
            state.append(wide_add(arrived, parts[(step + 1) % count]))
            return state[-1]

        return start, finish

    send = narrow(tn(hidden[1], rounded_outcome))
    arrived = swap(send, "core")
    keep = tn(hidden[0], tie(rounded_outcome, send))
    reduce_sums = wide_add(keep, tie(arrived, keep))
    reduce_y = swap(reduce_sums[span:], "y")
    total, pre_own, pre_other, sums_own, sums_other = feed_back(
        tie(rounded_outcome, reduce_sums), feed_weights[2], slope
    )
    grad_middle = grad_result + norm_backward(total, normed_two, inverse_two, gain_two[0])
    shared_feed = [total * normed_two, total, grad_outcome]
    send = narrow(tn(tie(pre_other, grad_middle), ready_two))
    arrived = swap(send, "core")
    keep = tn(pre_own, tie(ready_two, send))
    expand_sums = wide_add(keep, tie(arrived, keep))
    expand_parts = [jnp.concatenate(pair) for pair in zip(by_slot(expand_sums[:span]), by_slot(expand_sums[span:]))]
    expand_start, expand_finish = steps_of(expand_parts)
    grad_in, rounded_attended, grad_qkv, sums_qv, shared_attention, after = attention_backward(
        core, kept_attention, grad_middle, attention_weights, expand_parts, (expand_start(), reduce_y)
    )
    expand_step = expand_finish(after[0], 1)
    reduce_parts = by_slot(wide_add(reduce_sums[:span], after[1]))
    reduce_start, reduce_finish = steps_of(reduce_parts)
    grad_qkv = lax.optimization_barrier((*grad_qkv, expand_step, *reduce_parts))[:3]
    grad_in = narrow(grad_in)
    moving_e, moving_r = expand_start(), reduce_start()
    mixed, ready_one = kept_attention[4], kept_attention[2]
    left = jnp.stack([*grad_qkv, mixed])
    index = 2 * c + y

    def typed_grad(shift):
        right = jnp.where((index ^ shift) == 3, rounded_attended, ready_one)
        return tn(lax.dynamic_index_in_dim(left, index ^ shift, 0, False), right)

    send = [narrow(typed_grad(shift)) for shift in (3, 2)]
    arrived = [swap(value, "core") for value in send]
    left = tie(left, *send)
    keep = [typed_grad(shift) for shift in (1, 0)]
    moving_e, moving_r, *keep = lax.optimization_barrier((moving_e, moving_r, *keep))
    expand_finish(moving_e, 2)
    reduce_finish(moving_r, 1)
    shared = shared_attention + shared_feed
    shared = jnp.stack([jnp.sum(value, axis=0) for value in shared])
    sums_qv = sums_qv.reshape(2, count, local)
    sums_qv = jnp.concatenate([sums_qv[0], sums_qv[1], jnp.zeros((count, width - 2 * local), F32)], axis=1)[:, None]
    sums_pre = [value.reshape(count, part) for half in (sums_own[0], sums_other[0]) for value in jnp.split(half, 2)]
    sums_pre = quarters(jnp.concatenate(sums_pre, axis=1), 1)
    sums_pre = jnp.concatenate(sums_pre[0] + sums_pre[1], axis=1)[:, None]
    vectors = jnp.concatenate([jnp.broadcast_to(shared, (count,) + shared.shape), sums_qv, sums_pre], axis=1)
    vectors = jnp.pad(vectors, ((0, 0), (0, spare - 8), (0, 0)))
    vectors = vectors + swap(vectors, "core")

    sums = [wide_add(a, b) for a, b in zip(keep, arrived)]
    to_y, to_keep = by_slot(sums[0]), by_slot(sums[1])
    typed_parts = [None] * count

    def typed_swap(slot):
        return swap(to_y[slot], "y")

    moving_y, moving_z, vectors_y = typed_swap(1), typed_swap(2), swap(vectors, "y")
    moving_e, moving_r = expand_start(), reduce_start()
    moving_y, vectors_y, to_y[3], to_y[0] = lax.optimization_barrier((moving_y, vectors_y, to_y[3], to_y[0]))
    vectors = narrow(vectors + vectors_y)

    def typed_part(slot, arrived):
        typed_parts[slot] = jnp.concatenate([wide_add(to_keep[slot], arrived), vectors[slot]])

    typed_part(1, moving_y)
    typed_start, typed_finish = steps_of(typed_parts)
    moving_t, moving_y = typed_start(), typed_swap(3)
    moving_t, moving_z, moving_e, moving_r = lax.optimization_barrier((moving_t, moving_z, moving_e, moving_r))
    typed_part(2, moving_z)
    typed_finish(moving_t, 1)
    reduce_finish(moving_r, 2)
    expand_total = expand_finish(moving_e, 3).reshape(2, part, width)
    moving_t, moving_z, moving_r = typed_start(), typed_swap(0), reduce_start()
    moving_t, moving_y, moving_r = lax.optimization_barrier((moving_t, moving_y, moving_r))
    typed_part(3, moving_y)
    typed_finish(moving_t, 2)
    reduce_total = over_groups(reduce_finish(moving_r, 3))
    moving_t, expand_other = typed_start(), swap(expand_total, "y")
    moving_t, moving_z, grad_in, expand_other = lax.optimization_barrier((moving_t, moving_z, grad_in, expand_other))
    typed_part(0, moving_z)
    typed_total = over_groups(typed_finish(moving_t, 3))
    typed_other, reduce_other = swap(typed_total[:local], "y"), swap(reduce_total, "y")
    input_grad = give_back(grad_in[:block], grad_in[block:], 0)
    typed_other, reduce_other = lax.optimization_barrier((typed_other, reduce_other))
    def gathered(pair):
        pair = jnp.concatenate(pair)
        blocks = quarters(jnp.concatenate([pair, swap(pair, "core")]), 0)
        return jnp.concatenate(blocks[0] + blocks[1])

    pair = jnp.concatenate([typed_total[:local], typed_other])
    pair_other = swap(pair, "core")
    grad_expand = [over_groups(wide_add(expand_total[i], expand_other[1 - i])) for i in range(2)]
    grad_expand = gathered(grad_expand).T.astype(F32)
    grad_reduce = gathered([reduce_total, reduce_other]).astype(F32)
    whole = relative([pair[:local], pair[local:], pair_other[:local], pair_other[local:]])
    whole = [*whole[0], *whole[1]]
    grad_attend_in = jnp.stack(whole[:3]).transpose(2, 0, 1).astype(F32)
    grad_attend_out = whole[3].astype(F32)
    vectors = typed_total[local : local + 8].astype(F32)
    return (
        outputs[None, None],
        input_grad[None, None],
        vectors[0][None],
        vectors[1][None],
        grad_attend_in[None],
        vectors[6, : 2 * local].reshape(1, 2, local),
        grad_attend_out[None],
        vectors[2][None],
        vectors[3][None],
        vectors[4][None],
        grad_expand[None],
        vectors[7, :units][None],
        grad_reduce[None],
        vectors[5][None],
    )


def solution(mesh):
    pipe, groups, count = mesh.devices.shape
    split = Mesh(mesh.devices.reshape(pipe, groups // 4, 2, 2, count), ("pipe", "outer", "y", "core", "tensor"))
    dp = ("outer", "y", "core")
    rows = P("pipe", dp, "tensor", None)
    vector = P("pipe", None)
    placed = (
        rows,
        rows,
        vector,
        vector,
        P("pipe", None, None, "tensor"),
        P("pipe", None, "tensor"),
        P("pipe", "tensor", None),
        vector,
        vector,
        vector,
        P("pipe", None, "tensor"),
        P("pipe", "tensor"),
        P("pipe", "tensor", None),
        vector,
    )
    return jax.shard_map(shards, mesh=split, in_specs=placed, out_specs=(rows, rows) + placed[2:], check_vma=False)
```

```python
import functools

import jax
import jax.numpy as jnp
import numpy as np
from jax import lax
from jax.experimental import pallas as pl
from jax.experimental.pallas import tpu as pltpu
from jax.sharding import Mesh
from jax.sharding import PartitionSpec as P

HEAD = 64
DEPTH = 12
BRANCH = DEPTH ** (-0.5)
EPSILON = 1e-05
NEGATIVE = -1e30
LANES = 128
AXES = ("pipe", "y", "core", "tensor")
F32 = jnp.float32
BF16 = jnp.bfloat16


def ring_order(count):
    return list(range(0, count, 2)) + list(range(1, count, 2))[::-1]


def ring(value):
    order = ring_order(lax.axis_size("tensor"))
    return lax.ppermute(value, "tensor", list(zip(order, order[1:] + order[:1])))


def swap(value, axis):
    return lax.ppermute(value, axis, [(0, 1), (1, 0)])


def along_pipe(value, by):
    return lax.ppermute(value, "pipe", [(0, 1)] if by > 0 else [(1, 0)])


def routes(section, large):
    count = lax.axis_size("tensor")

    def index(x, y, c, z):
        return ((x * 2 + y) * 2 + c) * count + z

    pairs = []
    for micro in range(2):
        for y in range(2):
            for c in range(2):
                for core in range(2):
                    block = 3 - core if large else core
                    pairs.append((index(micro, y, c, block), index(section, y, core, 2 * c + micro)))
    return pairs


def fetch(block, section):
    return [lax.ppermute(block, AXES, routes(section, large)) for large in (False, True)]


def give_back(small, large, section):
    pieces = []
    for rows, is_large in ((small, False), (large, True)):
        pairs = [(b, a) for a, b in routes(section, is_large)]
        pieces.append(lax.ppermute(rows, AXES, pairs))
    return jnp.where(lax.axis_index("tensor") < 2, pieces[0], pieces[1])


def nt(left, right):
    return lax.dot_general(left, right, (((1,), (1,)), ((), ())), preferred_element_type=F32)


def tn(left, right):
    return lax.dot_general(left, right, (((0,), (0,)), ((), ())), preferred_element_type=F32)


def nn(left, right):
    return lax.dot_general(left, right, (((1,), (0,)), ((), ())), preferred_element_type=F32)


def estimate(flops, size):
    return pl.CostEstimate(flops=flops, bytes_accessed=size, transcendentals=0)


def head_mask(rows, head):
    lanes = lax.broadcasted_iota(jnp.int32, (rows, LANES), 1)
    return (lanes >= head * HEAD) & (lanes < (head + 1) * HEAD)


def only(mask, value, factor=1.0):
    return jnp.where(mask, value.astype(F32) * factor, 0.0).astype(BF16)


def turned(value):
    return value.astype(F32).T.astype(BF16)


def attend_kernel(keep_weights, core_ref, q_ref, k_ref, v_ref, ko_ref, vo_ref, o_ref, *kept_refs):
    rows = q_ref.shape[0] // 2
    second = core_ref[0] == 1
    keys = lax.broadcasted_iota(jnp.int32, (rows, rows), 0)
    places = lax.broadcasted_iota(jnp.int32, (rows, rows), 1)
    allowed = keys <= places
    factor = HEAD ** (-0.5)
    small = pl.ds(0, rows)
    large = pl.ds(rows, rows)

    def fifth(ref):
        return jnp.where(second, ref[small, :].astype(F32), ref[large, :].astype(F32)).astype(BF16)

    k5, q5 = fifth(ko_ref), fifth(q_ref)
    vs, vl, v4, v5 = turned(v_ref[small, :]), turned(v_ref[large, :]), turned(vo_ref[small, :]), turned(fifth(vo_ref))
    small_parts, large_parts, scales = [], [], []
    for head in range(LANES // HEAD):
        mask = head_mask(rows, head)
        lanes = slice(head * HEAD, (head + 1) * HEAD)
        qs, ql, qf = (only(mask, value, factor) for value in (q_ref[small, :], q_ref[large, :], q5))
        s1 = jnp.where(allowed, nt(k_ref[small, :], qs), NEGATIVE)
        s2 = nt(k_ref[small, :], ql)
        s3 = jnp.where(allowed, nt(k_ref[large, :], ql), NEGATIVE)
        s4 = nt(ko_ref[small, :], ql)
        s5 = nt(k5, qf)

        def peak(value):
            return jnp.max(value, axis=0, keepdims=True)

        def total(value):
            return jnp.sum(value, axis=0, keepdims=True)

        m5 = peak(s5)
        ms = peak(s1)
        ml = jnp.maximum(jnp.maximum(peak(s2), peak(s3)), peak(s4))
        ms = jnp.where(second, jnp.maximum(ms, m5), ms)
        ml = jnp.where(second, ml, jnp.maximum(ml, m5))
        mf = jnp.where(second, ms, ml)
        e1 = jnp.exp(s1 - ms)
        e2 = jnp.exp(s2 - ml)
        e3 = jnp.exp(s3 - ml)
        e4 = jnp.exp(s4 - ml)
        e5 = jnp.exp(s5 - mf)
        t5 = total(e5)
        rs = total(e1)
        rl = total(e2) + total(e3) + total(e4)
        rs = 1.0 / jnp.where(second, rs + t5, rs)
        rl = 1.0 / jnp.where(second, rl, rl + t5)
        e1, e2, e3, e4, e5 = (value.astype(BF16) for value in (e1, e2, e3, e4, e5))
        if keep_weights:
            for place, value in enumerate((e1, e2, e3, e4, e5)):
                kept_refs[0][head, place] = value
            scales.append(jnp.concatenate([rs, rl], axis=1))
        o5 = nn(v5[lanes], e5)
        small_parts.append((nn(vs[lanes], e1) + jnp.where(second, o5, 0.0)) * rs)
        large_parts.append(
            (nn(vs[lanes], e2) + nn(vl[lanes], e3) + nn(v4[lanes], e4) + jnp.where(second, 0.0, o5)) * rl
        )
    o_ref[small, :] = jnp.concatenate(small_parts).T.astype(BF16)
    o_ref[large, :] = jnp.concatenate(large_parts).T.astype(BF16)
    if keep_weights:
        row = lax.broadcasted_iota(jnp.int32, (8, 2 * rows), 0)
        kept_refs[1][...] = jnp.where(row == 0, scales[0], scales[1])


def attend_back_kernel(
    core_ref, q_ref, k_ref, v_ref, ko_ref, vo_ref, go_ref, o_ref, e_ref, scale_ref, gq_ref, own_ref, other_ref, sums_ref
):
    rows = q_ref.shape[0] // 2
    second = core_ref[0] == 1
    factor = HEAD ** (-0.5)
    small = pl.ds(0, rows)
    large = pl.ds(rows, rows)

    def fifth(first, last):
        return jnp.where(second, first.astype(F32), last.astype(F32)).astype(BF16)

    row = lax.broadcasted_iota(jnp.int32, (LANES, 2 * rows), 0)
    scale = jnp.where(row < HEAD, scale_ref[0:1, :], scale_ref[1:2, :]).T
    grads = (go_ref[...].astype(F32) * scale).astype(BF16)
    product = grads.astype(F32) * o_ref[...].astype(F32)
    high = product.astype(BF16)
    low = (product - high.astype(F32)).astype(BF16)
    g_small, g_large = grads[:rows], grads[rows:]
    g5 = fifth(g_small, g_large)
    q5 = fifth(q_ref[small, :], q_ref[large, :])
    v5 = fifth(vo_ref[small, :], vo_ref[large, :])
    ks, kl, k4, k5 = (
        turned(k_ref[small, :]), turned(k_ref[large, :]), turned(ko_ref[small, :]),
        turned(fifth(ko_ref[small, :], ko_ref[large, :])),
    )
    totals = {}
    gq_small, gq_large = [], []

    def add(name, value):
        totals[name] = value if name not in totals else totals[name] + value

    for head in range(LANES // HEAD):
        mask = head_mask(rows, head)
        lanes = slice(head * HEAD, (head + 1) * HEAD)
        ones = jnp.where(head_mask(16, head), 1.0, 0.0).astype(BF16)
        inner = (nt(ones, high) + nt(ones, low))[0:1]
        ds_, dl_ = inner[:, :rows], inner[:, rows:]
        df_ = jnp.where(second, ds_, dl_)
        qs, ql, qf = (only(mask, value, factor) for value in (q_ref[small, :], q_ref[large, :], q5))
        gs, gl, gf = (only(mask, value) for value in (g_small, g_large, g5))

        def score_grad(place, values, rows_grad, shift):
            return (e_ref[head, place].astype(F32) * (nt(values, rows_grad) - shift)).astype(BF16)

        z1 = score_grad(0, v_ref[small, :], gs, ds_)
        z2 = score_grad(1, v_ref[small, :], gl, dl_)
        z3 = score_grad(2, v_ref[large, :], gl, dl_)
        z4 = score_grad(3, vo_ref[small, :], gl, dl_)
        z5 = score_grad(4, v5, gf, df_)
        gq5 = nn(k5[lanes], z5)
        gq_small.append(nn(ks[lanes], z1) + jnp.where(second, gq5, 0.0))
        gq_large.append(nn(ks[lanes], z2) + nn(kl[lanes], z3) + nn(k4[lanes], z4) + jnp.where(second, 0.0, gq5))
        add("ks", nn(z1, qs) + nn(z2, ql))
        add("kl", nn(z3, ql))
        add("k4", nn(z4, ql))
        add("k5", nn(z5, qf))
        add("vs", nn(e_ref[head, 0], gs) + nn(e_ref[head, 1], gl))
        add("vl", nn(e_ref[head, 2], gl))
        add("v4", nn(e_ref[head, 3], gl))
        add("v5", nn(e_ref[head, 4], gf))
    gqs, gql = jnp.concatenate(gq_small).T * factor, jnp.concatenate(gq_large).T * factor
    gq_ref[small, :] = gqs.astype(BF16)
    gq_ref[large, :] = gql.astype(BF16)
    for place, name in enumerate("kv"):
        own_ref[place, small, :] = totals[name + "s"]
        own_ref[place, large, :] = totals[name + "l"]
        four, five = totals[name + "4"], totals[name + "5"]
        other_ref[place, small, :] = (four + jnp.where(second, five, 0.0)).astype(BF16)
        other_ref[place, large, :] = jnp.where(second, 0.0, five).astype(BF16)
    sum_q = jnp.sum(gqs, axis=0, keepdims=True) + jnp.sum(gql, axis=0, keepdims=True)
    sum_v = jnp.sum(totals["vs"] + totals["vl"] + totals["v4"] + totals["v5"], axis=0, keepdims=True)
    row = lax.broadcasted_iota(jnp.int32, (8, LANES), 0)
    sums_ref[...] = jnp.where(row == 0, sum_q, jnp.where(row == 1, sum_v, 0.0))


def attend(core, q, k, v, k_other, v_other, keep_weights):
    length, width = q.shape
    rows = length // 2
    pairs = width // LANES
    column = pl.BlockSpec((length, LANES), lambda i: (0, i))
    shapes = [jax.ShapeDtypeStruct((length, width), BF16)]
    outs = [column]
    if keep_weights:
        shapes.append(pltpu.HBM((width // HEAD, 5, rows, rows), BF16))
        shapes.append(jax.ShapeDtypeStruct((8 * pairs, length), F32))
        outs.append(pl.BlockSpec((2, 5, rows, rows), lambda i: (i, 0, 0, 0)))
        outs.append(pl.BlockSpec((8, length), lambda i: (i, 0)))
    return pl.pallas_call(
        functools.partial(attend_kernel, keep_weights),
        grid=(pairs,),
        out_shape=shapes,
        in_specs=[pl.BlockSpec(memory_space=pltpu.SMEM)] + [column] * 5,
        out_specs=outs,
        compiler_params=pltpu.CompilerParams(vmem_limit_bytes=40 * 1024 * 1024),
        cost_estimate=estimate(20 * rows * rows * width * 2, 16 * length * width),
        name="attend",
    )(core, q, k, v, k_other, v_other)


def attend_back(core, q, k, v, k_other, v_other, grad_mixed, mixed, weights, scales):
    length, width = q.shape
    rows = length // 2
    column = pl.BlockSpec((length, LANES), lambda i: (0, i))
    double = pl.BlockSpec((2, length, LANES), lambda i: (0, 0, i))
    return pl.pallas_call(
        attend_back_kernel,
        grid=(width // LANES,),
        out_shape=[
            jax.ShapeDtypeStruct((length, width), BF16),
            jax.ShapeDtypeStruct((2, length, width), F32),
            jax.ShapeDtypeStruct((2, length, width), BF16),
            jax.ShapeDtypeStruct((8, width), F32),
        ],
        in_specs=[pl.BlockSpec(memory_space=pltpu.SMEM)]
        + [column] * 7
        + [pl.BlockSpec((2, 5, rows, rows), lambda i: (i, 0, 0, 0)), pl.BlockSpec((8, length), lambda i: (i, 0))],
        out_specs=[column, double, double, pl.BlockSpec((8, LANES), lambda i: (0, i))],
        compiler_params=pltpu.CompilerParams(vmem_limit_bytes=40 * 1024 * 1024),
        cost_estimate=estimate(40 * rows * rows * width * 2, 40 * length * width),
        name="attend_back",
    )(core, q, k, v, k_other, v_other, grad_mixed, mixed, weights, scales)


def gelu_and_slope(values):
    root = float(np.sqrt(2 / np.pi))
    cubic = 0.044715 * root
    square = values * values
    bend = jnp.tanh(values * (root + cubic * square))
    half = 0.5 + 0.5 * bend
    gate = values * half
    slope = half + gate * ((1.0 - bend) * (root + (3 * cubic) * square))
    return (gate, slope)


def expand_kernel(rows_ref, expand_ref, bias_ref, reduce_ref, start_ref, total_ref):
    gate, _ = gelu_and_slope(nt(rows_ref[...], expand_ref[...]) + bias_ref[...])
    total_ref[...] = start_ref[...] + nn(gate.astype(BF16), reduce_ref[...])


def feed_half(rows, expand_w, bias, reduce_w, start, row_part=None):
    length, width = rows.shape
    units = expand_w.shape[0]
    if row_part is not None:
        length = length // 2
    place = row_part or 0
    whole = pl.BlockSpec((length, width), lambda i: (0, 0))
    taken = pl.BlockSpec((length, width), lambda i: (place, 0))
    start_place = 0 if start.shape[0] == length else place
    begun = pl.BlockSpec((length, width), lambda i: (start_place, 0))
    weight = pl.BlockSpec((units, width), lambda i: (0, 0))
    return pl.pallas_call(
        expand_kernel,
        grid=(1,),
        out_shape=jax.ShapeDtypeStruct((length, width), F32),
        in_specs=[taken, weight, pl.BlockSpec((1, units), lambda i: (0, 0)), weight, begun],
        out_specs=whole,
        compiler_params=pltpu.CompilerParams(vmem_limit_bytes=40 * 1024 * 1024),
        cost_estimate=estimate(4 * length * width * units, 4 * width * units),
        name="feed_half",
    )(rows, expand_w, bias.reshape(1, units), reduce_w, start)


def both_kernel(
    steps, rows_ref, grad_ref, e0_ref, e1_ref, b0_ref, b1_ref, r0_ref, r1_ref,
    total_ref, grad_total_ref, h0_ref, h1_ref, s0_ref, s1_ref,
):
    place = pl.program_id(0)

    @pl.when(place == 0)
    def _():
        total_ref[...] = jnp.zeros_like(total_ref)
        grad_total_ref[...] = jnp.zeros_like(grad_total_ref)

    def tile(expand_ref, bias_ref, reduce_ref, hidden_ref, slope_ref):
        gate, slope = gelu_and_slope(nt(rows_ref[...], expand_ref[...]) + bias_ref[...])
        hidden = gate.astype(BF16)
        slope = slope.astype(BF16)
        hidden_ref[...] = hidden
        slope_ref[...] = slope
        total_ref[...] += nn(hidden, reduce_ref[...])
        pre = nt(grad_ref[...], reduce_ref[...]) * slope.astype(F32)
        grad_total_ref[...] += nn(pre.astype(BF16), expand_ref[...])

    @pl.when(place < steps)
    def _():
        tile(e0_ref, b0_ref, r0_ref, h0_ref, s0_ref)

    @pl.when(place >= steps)
    def _():
        tile(e1_ref, b1_ref, r1_ref, h1_ref, s1_ref)


def back_kernel(
    steps, grad_ref, e0_ref, e1_ref, r0_ref, r1_ref, s0_ref, s1_ref,
    total_ref, p0_ref, p1_ref, sums0_ref, sums1_ref,
):
    place = pl.program_id(0)

    @pl.when(place == 0)
    def _():
        total_ref[...] = jnp.zeros_like(total_ref)

    def tile(expand_ref, reduce_ref, slope_ref, pre_ref, sums_ref):
        pre = nt(grad_ref[...], reduce_ref[...]) * slope_ref[...].astype(F32)
        sums_ref[...] = jnp.broadcast_to(jnp.sum(pre, axis=0, keepdims=True), sums_ref.shape)
        rounded = pre.astype(BF16)
        pre_ref[...] = rounded
        total_ref[...] += nn(rounded, expand_ref[...])

    @pl.when(place < steps)
    def _():
        tile(e0_ref, r0_ref, s0_ref, p0_ref, sums0_ref)

    @pl.when(place >= steps)
    def _():
        tile(e1_ref, r1_ref, s1_ref, p1_ref, sums1_ref)


def feed_specs(length, width, units, steps):
    tile = units // steps
    whole = pl.BlockSpec((length, width), lambda i: (0, 0))

    def early(i):
        return jnp.minimum(i, steps - 1)

    def late(i):
        return jnp.maximum(i - steps, 0)

    weight = [pl.BlockSpec((tile, width), lambda i, f=f: (f(i), 0)) for f in (early, late)]
    across = [pl.BlockSpec((length, tile), lambda i, f=f: (0, f(i))) for f in (early, late)]
    row = [pl.BlockSpec((1, tile), lambda i, f=f: (0, f(i))) for f in (early, late)]
    rows = [pl.BlockSpec((8, tile), lambda i, f=f: (0, f(i))) for f in (early, late)]
    return steps, whole, weight, across, row, rows


def feed_both(rows, grad, halves):
    length, width = rows.shape
    units = halves[0][0].shape[0]
    steps, whole, weight, across, row, _ = feed_specs(length, width, units, 2)
    total = jax.ShapeDtypeStruct((length, width), F32)
    kept = jax.ShapeDtypeStruct((length, units), BF16)
    (e0, b0, r0), (e1, b1, r1) = halves
    return pl.pallas_call(
        functools.partial(both_kernel, steps),
        grid=(2 * steps,),
        out_shape=[total, total, kept, kept, kept, kept],
        in_specs=[whole, whole, *weight, *row, *weight],
        out_specs=[whole, whole, *across, *across],
        compiler_params=pltpu.CompilerParams(vmem_limit_bytes=40 * 1024 * 1024),
        cost_estimate=estimate(16 * length * width * units, 8 * width * units),
        name="feed_both",
    )(rows, grad, e0, e1, b0.reshape(1, units), b1.reshape(1, units), r0, r1)


def feed_back(grad, halves, slope):
    length, width = grad.shape
    units = halves[0][0].shape[0]
    steps, whole, weight, across, _, rows = feed_specs(length, width, units, 1)
    kept = jax.ShapeDtypeStruct((length, units), BF16)
    sums = jax.ShapeDtypeStruct((8, units), F32)
    (e0, _, r0), (e1, _, r1) = halves
    return pl.pallas_call(
        functools.partial(back_kernel, steps),
        grid=(2 * steps,),
        out_shape=[jax.ShapeDtypeStruct((length, width), F32), kept, kept, sums, sums],
        in_specs=[whole, *weight, *weight, *across],
        out_specs=[whole, *across, *rows],
        compiler_params=pltpu.CompilerParams(vmem_limit_bytes=40 * 1024 * 1024),
        cost_estimate=estimate(8 * length * width * units, 8 * width * units),
        name="feed_back",
    )(grad, e0, e1, r0, r1, *slope)


def tie(value, *others):
    return lax.optimization_barrier((value, *others))[0]


def normalize_rows(rows):
    centred = rows - jnp.mean(rows, axis=-1, keepdims=True)
    inverse = lax.rsqrt(jnp.mean(centred * centred, axis=-1, keepdims=True) + EPSILON)
    return (centred * inverse, inverse)


def norm_backward(grad_normed, normed, inverse, gain):
    scaled = grad_normed * gain
    centred = scaled - jnp.mean(scaled, axis=-1, keepdims=True)
    return inverse * (centred - normed * jnp.mean(scaled * normed, axis=-1, keepdims=True))


def attention_forward(core, rows_in, weights, keep, before=(), after=()):
    gain_a, shift_a, proj, bias_q, bias_v, bias_out = weights
    normed_one, inverse_one = normalize_rows(rows_in)
    ready_one = narrow(normed_one * gain_a + shift_a)
    k = narrow(nt(ready_one, proj[1]))
    k_other = swap(k, "core")
    v = narrow(nt(ready_one, proj[2]) + bias_v)
    v_other = swap(v, "core")
    q = narrow(nt(ready_one, proj[0]) + bias_q)
    if before:
        q, proj_out, *before = lax.optimization_barrier((q, proj[3], *before))
        proj = [*proj[:3], proj_out]
        after = after(before)
    mixed, *kept_weights = attend(core, q, k, v, k_other, v_other, keep)
    mixed, *after = lax.optimization_barrier((mixed, *after))
    middle = rows_in + BRANCH * (nn(mixed, proj[3]) + bias_out)
    kept = (normed_one, inverse_one, ready_one, (q, k, v, k_other, v_other), mixed, *kept_weights)
    return middle, kept, after


def feed_start(middle, weights):
    gain_b, shift_b, _, _ = weights
    normed_two, inverse_two = normalize_rows(middle)
    return normed_two, inverse_two, narrow(normed_two * gain_b + shift_b)


def feed_forward_only(middle, weights):
    ready_two = feed_start(middle, weights)[2]
    first, second = weights[2]
    block = middle.shape[0] // 2
    total = jnp.broadcast_to(weights[3], (block, middle.shape[1]))
    totals = [feed_half(ready_two, *first, total, 0)]
    results = []
    for part in range(2):
        rows = slice(part * block, (part + 1) * block)
        if part:
            totals.append(feed_half(ready_two, *first, tie(total, *results), part))
        piece = feed_half(ready_two, *second, totals[part], part)
        results.append(narrow(middle[rows] + BRANCH * piece))
    return results


def feed_forward_and_back(middle, grad_result, weights):
    normed_two, inverse_two, ready_two = feed_start(middle, weights)
    rounded = narrow(BRANCH * grad_result)
    total, grad_total, *kept = feed_both(ready_two, rounded, weights[2])
    result = narrow(middle + BRANCH * (total + weights[3]))
    grad_middle = grad_result + norm_backward(grad_total, normed_two, inverse_two, weights[0])
    return result, grad_middle, (normed_two, inverse_two, ready_two, kept[:2], kept[2:])


def attention_backward(core, kept, grad_middle, weights, before=(), after=()):
    gain_a, _, proj, _, _, _ = weights
    normed_one, inverse_one, ready_one, projected, mixed, *attention = kept
    grad_attended = BRANCH * grad_middle
    rounded_attended = narrow(grad_attended)
    grad_mixed = narrow(nt(tie(rounded_attended, *before), proj[3]))
    grad_q, own, other, sums = attend_back(core, *projected, grad_mixed, mixed, *attention)
    other, *after = lax.optimization_barrier((other, *after))
    grad_kv = narrow(own + swap(other, "core").astype(F32))
    grad_normed_one = nn(grad_q, proj[0]) + nn(grad_kv[0], proj[1]) + nn(grad_kv[1], proj[2])
    grad_in = grad_middle + norm_backward(grad_normed_one, normed_one, inverse_one, gain_a)
    shared = [grad_normed_one * normed_one, grad_normed_one, grad_attended]
    return grad_in, rounded_attended, (grad_q, grad_kv[0], grad_kv[1]), sums[:2], shared, after


def narrow(value):
    return value.astype(BF16)


def wide_add(left, right):
    return narrow(left.astype(F32) + right.astype(F32))


def over_groups(value):
    return lax.psum(value, "outer") if lax.axis_size("outer") > 1 else value


def ring_add(parts):
    count = len(parts)
    total = parts[1 % count]
    for step in range(1, count):
        total = wide_add(ring(total), parts[(step + 1) % count])
    return total


def thirds(values):
    pieces = []
    for _ in range(3):
        piece = lax.reduce_precision(values, 8, 7)
        pieces.append(narrow(piece))
        values = values - piece
    return jnp.stack(pieces)


def shards(
    inputs, cotangent, gain_one, shift_one, attend_in, attend_bias, attend_out, out_bias,
    gain_two, shift_two, expand_in, expand_bias, reduce_out, reduce_bias,
):
    count = lax.axis_size("tensor")
    x, y, c, z = (lax.axis_index(axis) for axis in AXES)
    is_first = x == 0
    core = c.reshape(1).astype(jnp.int32)
    width = attend_in.shape[1]
    local = attend_in.shape[3]
    units = expand_in.shape[2]
    part = units // 4
    spare = 16

    def either(index, pair):
        first, second = pair
        return jnp.where(index == 0, first, second), jnp.where(index == 0, second, first)

    def relative(blocks):
        rows = [either(y, blocks[:2]), either(y, blocks[2:])]
        return list(zip(*(either(c, pair) for pair in zip(*rows))))

    def quarters(value, axis):
        return relative(jnp.split(value, 4, axis))

    typed = [*attend_in[0].transpose(1, 2, 0), attend_out[0]]
    (mine, mine_y), _ = relative(typed)
    biases = thirds(jnp.concatenate([attend_bias[0].reshape(2 * local), expand_bias[0]])).reshape(-1)
    biases = jnp.pad(biases, (0, spare * width - biases.size)).reshape(spare, width)
    piece = jnp.concatenate([mine, biases])
    bias_rows = [biases]
    own_parts = [quarters(expand_in[0].T, 0), quarters(reduce_out[0], 0)]
    feed = [jnp.concatenate([value[0][0] for value in own_parts])]
    feed_y = [jnp.concatenate([value[0][1] for value in own_parts])]
    pieces, pieces_y = [ring(piece)], []
    arrived = fetch(inputs[0, 0], 0)
    while len(pieces) < count - 1:
        pieces_y.append(swap(pieces[-1][:local], "y"))
        pieces.append(ring(pieces[-1]))
        if len(pieces) < count - 1:
            pieces[-1], pieces_y[-1], feed[0], *arrived = lax.optimization_barrier(
                (pieces[-1], pieces_y[-1], feed[0], *arrived)
            )
    feed.append(ring(feed[0]))
    pieces[-1], pieces_y[-1] = lax.optimization_barrier((pieces[-1], pieces_y[-1]))
    pieces_y.append(swap(pieces[-1][:local], "y"))
    feed[1], pieces_y[-1] = lax.optimization_barrier((feed[1], pieces_y[-1]))
    feed_y.append(swap(feed[1], "y"))
    feed.append(ring(feed[1]))
    feed[2], feed_y[1] = lax.optimization_barrier((feed[2], feed_y[1]))
    feed_y.append(swap(feed[2], "y"))
    before = (ring(feed[2]), feed_y[2])
    bias_rows += [value[local:] for value in pieces]
    pieces = [mine] + [value[:local] for value in pieces]
    pieces_y = [mine_y] + pieces_y
    pieces = jnp.concatenate(pieces)
    pieces_y = jnp.concatenate(pieces_y)
    proj = relative([pieces, pieces_y, swap(pieces, "core"), swap(pieces_y, "core")])
    proj = [*proj[0], *proj[1]]
    biases = jnp.stack(bias_rows).reshape(count, -1)[:, : 3 * (2 * local + units)].reshape(count, 3, 2 * local + units)
    biases = biases.astype(F32)
    biases = biases[:, 0] + (biases[:, 1] + biases[:, 2])
    bias_q, bias_v = biases[:, :local].reshape(width), biases[:, local : 2 * local].reshape(width)
    expand_b = quarters(biases[:, 2 * local :], 1)
    expand_b = [jnp.concatenate([value.reshape(count * part) for value in pair]) for pair in expand_b]
    attention_weights = (gain_one[0], shift_one[0], proj, bias_q, bias_v, out_bias[0])

    rows_in = jnp.concatenate(arrived)
    middle, _, after = attention_forward(
        core, rows_in.astype(F32), attention_weights, False, before,
        lambda ready: (*ready, swap(ready[0], "y")),
    )
    feed.append(after[0])
    feed_y[2:] = after[1:]
    own_half = [
        jnp.concatenate([value[kind * part : (kind + 1) * part] for value in feed + feed_y]) for kind in range(2)
    ]
    other_half = [swap(value, "core") for value in own_half]
    feed_weights = (
        gain_two[0],
        shift_two[0],
        [(own_half[0], expand_b[0], own_half[1]), (other_half[0], expand_b[1], other_half[1])],
        reduce_bias[0],
    )
    passed = jnp.concatenate([along_pipe(rows, 1) for rows in feed_forward_only(middle, feed_weights)])
    last = fetch(tie(cotangent[0, 0], passed), 1)
    rows_in = jnp.where(is_first, rows_in, passed)
    middle, kept_attention, last = attention_forward(
        core, rows_in.astype(F32), attention_weights, True, (), last
    )
    last = jnp.concatenate(last)
    result, grad_middle, kept_feed = feed_forward_and_back(middle, last.astype(F32), feed_weights)
    block = result.shape[0] // 2
    outputs = give_back(result[:block], result[block:], 1)
    grad_in, _, _, _, _, (outputs,) = attention_backward(
        core, kept_attention, grad_middle, attention_weights, (), (outputs,)
    )
    grad_in = narrow(grad_in)
    returned = jnp.concatenate([along_pipe(grad_in[:block], -1), along_pipe(grad_in[block:], -1)])
    grad_result = jnp.where(is_first, returned, last).astype(F32)
    grad_outcome = BRANCH * grad_result
    rounded_outcome = narrow(grad_outcome)
    normed_two, inverse_two, ready_two, hidden, slope = kept_feed
    span = count * part

    def by_slot(value):
        return [value[slot * part : (slot + 1) * part] for slot in range(count)]

    def steps_of(parts):
        state = [parts[1 % count]]

        def start():
            state.append(ring(state[-1]))
            return state[-1]

        def finish(arrived, step):
            state.append(wide_add(arrived, parts[(step + 1) % count]))
            return state[-1]

        return start, finish

    send = narrow(tn(hidden[1], rounded_outcome))
    arrived = swap(send, "core")
    keep = tn(hidden[0], tie(rounded_outcome, send))
    reduce_sums = wide_add(keep, tie(arrived, keep))
    reduce_y = swap(reduce_sums[span:], "y")
    total, pre_own, pre_other, sums_own, sums_other = feed_back(
        tie(rounded_outcome, reduce_sums), feed_weights[2], slope
    )
    grad_middle = grad_result + norm_backward(total, normed_two, inverse_two, gain_two[0])
    shared_feed = [total * normed_two, total, grad_outcome]
    send = narrow(tn(tie(pre_other, grad_middle), ready_two))
    arrived = swap(send, "core")
    keep = tn(pre_own, tie(ready_two, send))
    expand_sums = wide_add(keep, tie(arrived, keep))
    expand_parts = [jnp.concatenate(pair) for pair in zip(by_slot(expand_sums[:span]), by_slot(expand_sums[span:]))]
    expand_start, expand_finish = steps_of(expand_parts)
    grad_in, rounded_attended, grad_qkv, sums_qv, shared_attention, after = attention_backward(
        core, kept_attention, grad_middle, attention_weights, expand_parts, (expand_start(), reduce_y)
    )
    expand_step = expand_finish(after[0], 1)
    reduce_parts = by_slot(wide_add(reduce_sums[:span], after[1]))
    reduce_start, reduce_finish = steps_of(reduce_parts)
    grad_qkv = lax.optimization_barrier((*grad_qkv, expand_step, *reduce_parts))[:3]
    grad_in = narrow(grad_in)
    moving_e, moving_r = expand_start(), reduce_start()
    mixed, ready_one = kept_attention[4], kept_attention[2]
    left = jnp.stack([*grad_qkv, mixed])
    index = 2 * c + y

    def typed_grad(shift):
        right = jnp.where((index ^ shift) == 3, rounded_attended, ready_one)
        return tn(lax.dynamic_index_in_dim(left, index ^ shift, 0, False), right)

    send = [narrow(typed_grad(shift)) for shift in (3, 2)]
    arrived = [swap(value, "core") for value in send]
    left = tie(left, *send)
    keep = [typed_grad(shift) for shift in (1, 0)]
    moving_e, moving_r, *keep = lax.optimization_barrier((moving_e, moving_r, *keep))
    expand_finish(moving_e, 2)
    reduce_finish(moving_r, 1)
    shared = shared_attention + shared_feed
    shared = jnp.stack([jnp.sum(value, axis=0) for value in shared])
    sums_qv = sums_qv.reshape(2, count, local)
    sums_qv = jnp.concatenate([sums_qv[0], sums_qv[1], jnp.zeros((count, width - 2 * local), F32)], axis=1)[:, None]
    sums_pre = [value.reshape(count, part) for half in (sums_own[0], sums_other[0]) for value in jnp.split(half, 2)]
    sums_pre = quarters(jnp.concatenate(sums_pre, axis=1), 1)
    sums_pre = jnp.concatenate(sums_pre[0] + sums_pre[1], axis=1)[:, None]
    vectors = jnp.concatenate([jnp.broadcast_to(shared, (count,) + shared.shape), sums_qv, sums_pre], axis=1)
    vectors = jnp.pad(vectors, ((0, 0), (0, spare - 8), (0, 0)))
    vectors = vectors + swap(vectors, "core")

    sums = [wide_add(a, b) for a, b in zip(keep, arrived)]
    to_y, to_keep = by_slot(sums[0]), by_slot(sums[1])
    typed_parts = [None] * count

    def typed_swap(slot):
        return swap(to_y[slot], "y")

    moving_y, moving_z, vectors_y = typed_swap(1), typed_swap(2), swap(vectors, "y")
    moving_e, moving_r = expand_start(), reduce_start()
    moving_y, vectors_y, to_y[3], to_y[0] = lax.optimization_barrier((moving_y, vectors_y, to_y[3], to_y[0]))
    vectors = narrow(vectors + vectors_y)

    def typed_part(slot, arrived):
        typed_parts[slot] = jnp.concatenate([wide_add(to_keep[slot], arrived), vectors[slot]])

    typed_part(1, moving_y)
    typed_start, typed_finish = steps_of(typed_parts)
    moving_t, moving_y = typed_start(), typed_swap(3)
    moving_t, moving_z, moving_e, moving_r = lax.optimization_barrier((moving_t, moving_z, moving_e, moving_r))
    typed_part(2, moving_z)
    typed_finish(moving_t, 1)
    reduce_finish(moving_r, 2)
    expand_total = expand_finish(moving_e, 3).reshape(2, part, width)
    moving_t, moving_z, moving_r = typed_start(), typed_swap(0), reduce_start()
    moving_t, moving_y, moving_r = lax.optimization_barrier((moving_t, moving_y, moving_r))
    typed_part(3, moving_y)
    typed_finish(moving_t, 2)
    reduce_total = over_groups(reduce_finish(moving_r, 3))
    moving_t, expand_other = typed_start(), swap(expand_total, "y")
    moving_t, moving_z, grad_in, expand_other = lax.optimization_barrier((moving_t, moving_z, grad_in, expand_other))
    typed_part(0, moving_z)
    typed_total = over_groups(typed_finish(moving_t, 3))
    typed_other, reduce_other = swap(typed_total[:local], "y"), swap(reduce_total, "y")
    input_grad = give_back(grad_in[:block], grad_in[block:], 0)
    typed_other, reduce_other = lax.optimization_barrier((typed_other, reduce_other))
    def gathered(pair):
        pair = jnp.concatenate(pair)
        blocks = quarters(jnp.concatenate([pair, swap(pair, "core")]), 0)
        return jnp.concatenate(blocks[0] + blocks[1])

    pair = jnp.concatenate([typed_total[:local], typed_other])
    pair_other = swap(pair, "core")
    grad_expand = [over_groups(wide_add(expand_total[i], expand_other[1 - i])) for i in range(2)]
    grad_expand = gathered(grad_expand).T.astype(F32)
    grad_reduce = gathered([reduce_total, reduce_other]).astype(F32)
    whole = relative([pair[:local], pair[local:], pair_other[:local], pair_other[local:]])
    whole = [*whole[0], *whole[1]]
    grad_attend_in = jnp.stack(whole[:3]).transpose(2, 0, 1).astype(F32)
    grad_attend_out = whole[3].astype(F32)
    vectors = typed_total[local : local + 8].astype(F32)
    return (
        outputs[None, None],
        input_grad[None, None],
        vectors[0][None],
        vectors[1][None],
        grad_attend_in[None],
        vectors[6, : 2 * local].reshape(1, 2, local),
        grad_attend_out[None],
        vectors[2][None],
        vectors[3][None],
        vectors[4][None],
        grad_expand[None],
        vectors[7, :units][None],
        grad_reduce[None],
        vectors[5][None],
    )


def solution(mesh):
    pipe, groups, count = mesh.devices.shape
    split = Mesh(mesh.devices.reshape(pipe, groups // 4, 2, 2, count), ("pipe", "outer", "y", "core", "tensor"))
    dp = ("outer", "y", "core")
    rows = P("pipe", dp, "tensor", None)
    vector = P("pipe", None)
    placed = (
        rows,
        rows,
        vector,
        vector,
        P("pipe", None, None, "tensor"),
        P("pipe", None, "tensor"),
        P("pipe", "tensor", None),
        vector,
        vector,
        vector,
        P("pipe", None, "tensor"),
        P("pipe", "tensor"),
        P("pipe", "tensor", None),
        vector,
    )
    return jax.shard_map(shards, mesh=split, in_specs=placed, out_specs=(rows, rows) + placed[2:], check_vma=False)
```

```python
import functools

import jax
import jax.numpy as jnp
import numpy as np
from jax import lax
from jax.experimental import pallas as pl
from jax.experimental.pallas import tpu as pltpu
from jax.sharding import Mesh
from jax.sharding import PartitionSpec as P

HEAD = 64
DEPTH = 12
BRANCH = DEPTH ** (-0.5)
EPSILON = 1e-05
NEGATIVE = -1e30
LANES = 128
AXES = ("pipe", "y", "core", "tensor")
F32 = jnp.float32
BF16 = jnp.bfloat16


def ring_order(count):
    return list(range(0, count, 2)) + list(range(1, count, 2))[::-1]


def ring(value):
    order = ring_order(lax.axis_size("tensor"))
    return lax.ppermute(value, "tensor", list(zip(order, order[1:] + order[:1])))


def swap(value, axis):
    return lax.ppermute(value, axis, [(0, 1), (1, 0)])


def along_pipe(value, by):
    return lax.ppermute(value, "pipe", [(0, 1)] if by > 0 else [(1, 0)])


def routes(section, large):
    count = lax.axis_size("tensor")

    def index(x, y, c, z):
        return ((x * 2 + y) * 2 + c) * count + z

    pairs = []
    for micro in range(2):
        for y in range(2):
            for c in range(2):
                for core in range(2):
                    block = 3 - core if large else core
                    pairs.append((index(micro, y, c, block), index(section, y, core, 2 * c + micro)))
    return pairs


def fetch(block, section):
    return [lax.ppermute(block, AXES, routes(section, large)) for large in (False, True)]


def give_back(small, large, section):
    pieces = []
    for rows, is_large in ((small, False), (large, True)):
        pairs = [(b, a) for a, b in routes(section, is_large)]
        pieces.append(lax.ppermute(rows, AXES, pairs))
    return jnp.where(lax.axis_index("tensor") < 2, pieces[0], pieces[1])


def nt(left, right):
    return lax.dot_general(left, right, (((1,), (1,)), ((), ())), preferred_element_type=F32)


def tn(left, right):
    return lax.dot_general(left, right, (((0,), (0,)), ((), ())), preferred_element_type=F32)


def nn(left, right):
    return lax.dot_general(left, right, (((1,), (0,)), ((), ())), preferred_element_type=F32)


def estimate(flops, size):
    return pl.CostEstimate(flops=flops, bytes_accessed=size, transcendentals=0)


def head_mask(rows, head):
    lanes = lax.broadcasted_iota(jnp.int32, (rows, LANES), 1)
    return (lanes >= head * HEAD) & (lanes < (head + 1) * HEAD)


def only(mask, value, factor=1.0):
    return jnp.where(mask, value.astype(F32) * factor, 0.0).astype(BF16)


def turned(value):
    return value.astype(F32).T.astype(BF16)


def attend_kernel(keep_weights, core_ref, q_ref, k_ref, v_ref, ko_ref, vo_ref, o_ref, *kept_refs):
    rows = q_ref.shape[0] // 2
    second = core_ref[0] == 1
    keys = lax.broadcasted_iota(jnp.int32, (rows, rows), 0)
    places = lax.broadcasted_iota(jnp.int32, (rows, rows), 1)
    allowed = keys <= places
    factor = HEAD ** (-0.5)
    small = pl.ds(0, rows)
    large = pl.ds(rows, rows)

    def fifth(ref):
        return jnp.where(second, ref[small, :].astype(F32), ref[large, :].astype(F32)).astype(BF16)

    k5, q5 = fifth(ko_ref), fifth(q_ref)
    vs, vl, v4, v5 = turned(v_ref[small, :]), turned(v_ref[large, :]), turned(vo_ref[small, :]), turned(fifth(vo_ref))
    small_parts, large_parts, scales = [], [], []
    for head in range(LANES // HEAD):
        mask = head_mask(rows, head)
        lanes = slice(head * HEAD, (head + 1) * HEAD)
        qs, ql, qf = (only(mask, value, factor) for value in (q_ref[small, :], q_ref[large, :], q5))
        s1 = jnp.where(allowed, nt(k_ref[small, :], qs), NEGATIVE)
        s2 = nt(k_ref[small, :], ql)
        s3 = jnp.where(allowed, nt(k_ref[large, :], ql), NEGATIVE)
        s4 = nt(ko_ref[small, :], ql)
        s5 = nt(k5, qf)

        def peak(value):
            return jnp.max(value, axis=0, keepdims=True)

        def total(value):
            return jnp.sum(value, axis=0, keepdims=True)

        m5 = peak(s5)
        ms = peak(s1)
        ml = jnp.maximum(jnp.maximum(peak(s2), peak(s3)), peak(s4))
        ms = jnp.where(second, jnp.maximum(ms, m5), ms)
        ml = jnp.where(second, ml, jnp.maximum(ml, m5))
        mf = jnp.where(second, ms, ml)
        e1 = jnp.exp(s1 - ms)
        e2 = jnp.exp(s2 - ml)
        e3 = jnp.exp(s3 - ml)
        e4 = jnp.exp(s4 - ml)
        e5 = jnp.exp(s5 - mf)
        t5 = total(e5)
        rs = total(e1)
        rl = total(e2) + total(e3) + total(e4)
        rs = 1.0 / jnp.where(second, rs + t5, rs)
        rl = 1.0 / jnp.where(second, rl, rl + t5)
        e1, e2, e3, e4, e5 = (value.astype(BF16) for value in (e1, e2, e3, e4, e5))
        if keep_weights:
            for place, value in enumerate((e1, e2, e3, e4, e5)):
                kept_refs[0][head, place] = value
            scales.append(jnp.concatenate([rs, rl], axis=1))
        o5 = nn(v5[lanes], e5)
        small_parts.append((nn(vs[lanes], e1) + jnp.where(second, o5, 0.0)) * rs)
        large_parts.append(
            (nn(vs[lanes], e2) + nn(vl[lanes], e3) + nn(v4[lanes], e4) + jnp.where(second, 0.0, o5)) * rl
        )
    o_ref[small, :] = jnp.concatenate(small_parts).T.astype(BF16)
    o_ref[large, :] = jnp.concatenate(large_parts).T.astype(BF16)
    if keep_weights:
        row = lax.broadcasted_iota(jnp.int32, (8, 2 * rows), 0)
        kept_refs[1][...] = jnp.where(row == 0, scales[0], scales[1])


def attend_back_kernel(
    core_ref, q_ref, k_ref, v_ref, ko_ref, vo_ref, go_ref, o_ref, e_ref, scale_ref, gq_ref, own_ref, other_ref, sums_ref
):
    rows = q_ref.shape[0] // 2
    second = core_ref[0] == 1
    factor = HEAD ** (-0.5)
    small = pl.ds(0, rows)
    large = pl.ds(rows, rows)

    def fifth(first, last):
        return jnp.where(second, first.astype(F32), last.astype(F32)).astype(BF16)

    row = lax.broadcasted_iota(jnp.int32, (LANES, 2 * rows), 0)
    scale = jnp.where(row < HEAD, scale_ref[0:1, :], scale_ref[1:2, :]).T
    grads = (go_ref[...].astype(F32) * scale).astype(BF16)
    product = grads.astype(F32) * o_ref[...].astype(F32)
    high = product.astype(BF16)
    low = (product - high.astype(F32)).astype(BF16)
    g_small, g_large = grads[:rows], grads[rows:]
    g5 = fifth(g_small, g_large)
    q5 = fifth(q_ref[small, :], q_ref[large, :])
    v5 = fifth(vo_ref[small, :], vo_ref[large, :])
    ks, kl, k4, k5 = (
        turned(k_ref[small, :]), turned(k_ref[large, :]), turned(ko_ref[small, :]),
        turned(fifth(ko_ref[small, :], ko_ref[large, :])),
    )
    totals = {}
    gq_small, gq_large = [], []

    def add(name, value):
        totals[name] = value if name not in totals else totals[name] + value

    for head in range(LANES // HEAD):
        mask = head_mask(rows, head)
        lanes = slice(head * HEAD, (head + 1) * HEAD)
        ones = jnp.where(head_mask(16, head), 1.0, 0.0).astype(BF16)
        inner = (nt(ones, high) + nt(ones, low))[0:1]
        ds_, dl_ = inner[:, :rows], inner[:, rows:]
        df_ = jnp.where(second, ds_, dl_)
        qs, ql, qf = (only(mask, value, factor) for value in (q_ref[small, :], q_ref[large, :], q5))
        gs, gl, gf = (only(mask, value) for value in (g_small, g_large, g5))

        def score_grad(place, values, rows_grad, shift):
            return (e_ref[head, place].astype(F32) * (nt(values, rows_grad) - shift)).astype(BF16)

        z1 = score_grad(0, v_ref[small, :], gs, ds_)
        z2 = score_grad(1, v_ref[small, :], gl, dl_)
        z3 = score_grad(2, v_ref[large, :], gl, dl_)
        z4 = score_grad(3, vo_ref[small, :], gl, dl_)
        z5 = score_grad(4, v5, gf, df_)
        gq5 = nn(k5[lanes], z5)
        gq_small.append(nn(ks[lanes], z1) + jnp.where(second, gq5, 0.0))
        gq_large.append(nn(ks[lanes], z2) + nn(kl[lanes], z3) + nn(k4[lanes], z4) + jnp.where(second, 0.0, gq5))
        add("ks", nn(z1, qs) + nn(z2, ql))
        add("kl", nn(z3, ql))
        add("k4", nn(z4, ql))
        add("k5", nn(z5, qf))
        add("vs", nn(e_ref[head, 0], gs) + nn(e_ref[head, 1], gl))
        add("vl", nn(e_ref[head, 2], gl))
        add("v4", nn(e_ref[head, 3], gl))
        add("v5", nn(e_ref[head, 4], gf))
    gqs, gql = jnp.concatenate(gq_small).T * factor, jnp.concatenate(gq_large).T * factor
    gq_ref[small, :] = gqs.astype(BF16)
    gq_ref[large, :] = gql.astype(BF16)
    for place, name in enumerate("kv"):
        own_ref[place, small, :] = totals[name + "s"]
        own_ref[place, large, :] = totals[name + "l"]
        four, five = totals[name + "4"], totals[name + "5"]
        other_ref[place, small, :] = (four + jnp.where(second, five, 0.0)).astype(BF16)
        other_ref[place, large, :] = jnp.where(second, 0.0, five).astype(BF16)
    sum_q = jnp.sum(gqs, axis=0, keepdims=True) + jnp.sum(gql, axis=0, keepdims=True)
    sum_v = jnp.sum(totals["vs"] + totals["vl"] + totals["v4"] + totals["v5"], axis=0, keepdims=True)
    row = lax.broadcasted_iota(jnp.int32, (8, LANES), 0)
    sums_ref[...] = jnp.where(row == 0, sum_q, jnp.where(row == 1, sum_v, 0.0))


def attend(core, q, k, v, k_other, v_other, keep_weights):
    length, width = q.shape
    rows = length // 2
    pairs = width // LANES
    column = pl.BlockSpec((length, LANES), lambda i: (0, i))
    shapes = [jax.ShapeDtypeStruct((length, width), BF16)]
    outs = [column]
    if keep_weights:
        shapes.append(pltpu.HBM((width // HEAD, 5, rows, rows), BF16))
        shapes.append(jax.ShapeDtypeStruct((8 * pairs, length), F32))
        outs.append(pl.BlockSpec((2, 5, rows, rows), lambda i: (i, 0, 0, 0)))
        outs.append(pl.BlockSpec((8, length), lambda i: (i, 0)))
    return pl.pallas_call(
        functools.partial(attend_kernel, keep_weights),
        grid=(pairs,),
        out_shape=shapes,
        in_specs=[pl.BlockSpec(memory_space=pltpu.SMEM)] + [column] * 5,
        out_specs=outs,
        compiler_params=pltpu.CompilerParams(vmem_limit_bytes=40 * 1024 * 1024),
        cost_estimate=estimate(20 * rows * rows * width * 2, 16 * length * width),
        name="attend",
    )(core, q, k, v, k_other, v_other)


def attend_back(core, q, k, v, k_other, v_other, grad_mixed, mixed, weights, scales):
    length, width = q.shape
    rows = length // 2
    column = pl.BlockSpec((length, LANES), lambda i: (0, i))
    double = pl.BlockSpec((2, length, LANES), lambda i: (0, 0, i))
    return pl.pallas_call(
        attend_back_kernel,
        grid=(width // LANES,),
        out_shape=[
            jax.ShapeDtypeStruct((length, width), BF16),
            jax.ShapeDtypeStruct((2, length, width), F32),
            jax.ShapeDtypeStruct((2, length, width), BF16),
            jax.ShapeDtypeStruct((8, width), F32),
        ],
        in_specs=[pl.BlockSpec(memory_space=pltpu.SMEM)]
        + [column] * 7
        + [pl.BlockSpec((2, 5, rows, rows), lambda i: (i, 0, 0, 0)), pl.BlockSpec((8, length), lambda i: (i, 0))],
        out_specs=[column, double, double, pl.BlockSpec((8, LANES), lambda i: (0, i))],
        compiler_params=pltpu.CompilerParams(vmem_limit_bytes=40 * 1024 * 1024),
        cost_estimate=estimate(40 * rows * rows * width * 2, 40 * length * width),
        name="attend_back",
    )(core, q, k, v, k_other, v_other, grad_mixed, mixed, weights, scales)


def gelu_and_slope(values):
    root = float(np.sqrt(2 / np.pi))
    cubic = 0.044715 * root
    square = values * values
    bend = jnp.tanh(values * (root + cubic * square))
    half = 0.5 + 0.5 * bend
    gate = values * half
    slope = half + gate * ((1.0 - bend) * (root + (3 * cubic) * square))
    return (gate, slope)


def expand_kernel(rows_ref, expand_ref, bias_ref, reduce_ref, start_ref, total_ref):
    gate, _ = gelu_and_slope(nt(rows_ref[...], expand_ref[...]) + bias_ref[...])
    total_ref[...] = start_ref[...] + nn(gate.astype(BF16), reduce_ref[...])


def feed_half(rows, expand_w, bias, reduce_w, start, row_part=None):
    length, width = rows.shape
    units = expand_w.shape[0]
    if row_part is not None:
        length = length // 2
    place = row_part or 0
    whole = pl.BlockSpec((length, width), lambda i: (0, 0))
    taken = pl.BlockSpec((length, width), lambda i: (place, 0))
    start_place = 0 if start.shape[0] == length else place
    begun = pl.BlockSpec((length, width), lambda i: (start_place, 0))
    weight = pl.BlockSpec((units, width), lambda i: (0, 0))
    return pl.pallas_call(
        expand_kernel,
        grid=(1,),
        out_shape=jax.ShapeDtypeStruct((length, width), F32),
        in_specs=[taken, weight, pl.BlockSpec((1, units), lambda i: (0, 0)), weight, begun],
        out_specs=whole,
        compiler_params=pltpu.CompilerParams(vmem_limit_bytes=40 * 1024 * 1024),
        cost_estimate=estimate(4 * length * width * units, 4 * width * units),
        name="feed_half",
    )(rows, expand_w, bias.reshape(1, units), reduce_w, start)


def both_kernel(
    steps, rows_ref, grad_ref, e0_ref, e1_ref, b0_ref, b1_ref, r0_ref, r1_ref,
    total_ref, grad_total_ref, h0_ref, h1_ref, s0_ref, s1_ref,
):
    place = pl.program_id(0)

    @pl.when(place == 0)
    def _():
        total_ref[...] = jnp.zeros_like(total_ref)
        grad_total_ref[...] = jnp.zeros_like(grad_total_ref)

    def tile(expand_ref, bias_ref, reduce_ref, hidden_ref, slope_ref):
        gate, slope = gelu_and_slope(nt(rows_ref[...], expand_ref[...]) + bias_ref[...])
        hidden = gate.astype(BF16)
        slope = slope.astype(BF16)
        hidden_ref[...] = hidden
        slope_ref[...] = slope
        total_ref[...] += nn(hidden, reduce_ref[...])
        pre = nt(grad_ref[...], reduce_ref[...]) * slope.astype(F32)
        grad_total_ref[...] += nn(pre.astype(BF16), expand_ref[...])

    @pl.when(place < steps)
    def _():
        tile(e0_ref, b0_ref, r0_ref, h0_ref, s0_ref)

    @pl.when(place >= steps)
    def _():
        tile(e1_ref, b1_ref, r1_ref, h1_ref, s1_ref)


def back_kernel(
    steps, grad_ref, e0_ref, e1_ref, r0_ref, r1_ref, s0_ref, s1_ref,
    total_ref, p0_ref, p1_ref, sums0_ref, sums1_ref,
):
    place = pl.program_id(0)

    @pl.when(place == 0)
    def _():
        total_ref[...] = jnp.zeros_like(total_ref)

    def tile(expand_ref, reduce_ref, slope_ref, pre_ref, sums_ref):
        pre = nt(grad_ref[...], reduce_ref[...]) * slope_ref[...].astype(F32)
        sums_ref[...] = jnp.broadcast_to(jnp.sum(pre, axis=0, keepdims=True), sums_ref.shape)
        rounded = pre.astype(BF16)
        pre_ref[...] = rounded
        total_ref[...] += nn(rounded, expand_ref[...])

    @pl.when(place < steps)
    def _():
        tile(e0_ref, r0_ref, s0_ref, p0_ref, sums0_ref)

    @pl.when(place >= steps)
    def _():
        tile(e1_ref, r1_ref, s1_ref, p1_ref, sums1_ref)


def feed_specs(length, width, units, steps):
    tile = units // steps
    whole = pl.BlockSpec((length, width), lambda i: (0, 0))

    def early(i):
        return jnp.minimum(i, steps - 1)

    def late(i):
        return jnp.maximum(i - steps, 0)

    weight = [pl.BlockSpec((tile, width), lambda i, f=f: (f(i), 0)) for f in (early, late)]
    across = [pl.BlockSpec((length, tile), lambda i, f=f: (0, f(i))) for f in (early, late)]
    row = [pl.BlockSpec((1, tile), lambda i, f=f: (0, f(i))) for f in (early, late)]
    rows = [pl.BlockSpec((8, tile), lambda i, f=f: (0, f(i))) for f in (early, late)]
    return steps, whole, weight, across, row, rows


def feed_both(rows, grad, halves):
    length, width = rows.shape
    units = halves[0][0].shape[0]
    steps, whole, weight, across, row, _ = feed_specs(length, width, units, 2)
    total = jax.ShapeDtypeStruct((length, width), F32)
    kept = jax.ShapeDtypeStruct((length, units), BF16)
    (e0, b0, r0), (e1, b1, r1) = halves
    return pl.pallas_call(
        functools.partial(both_kernel, steps),
        grid=(2 * steps,),
        out_shape=[total, total, kept, kept, kept, kept],
        in_specs=[whole, whole, *weight, *row, *weight],
        out_specs=[whole, whole, *across, *across],
        compiler_params=pltpu.CompilerParams(vmem_limit_bytes=40 * 1024 * 1024),
        cost_estimate=estimate(16 * length * width * units, 8 * width * units),
        name="feed_both",
    )(rows, grad, e0, e1, b0.reshape(1, units), b1.reshape(1, units), r0, r1)


def feed_back(grad, halves, slope):
    length, width = grad.shape
    units = halves[0][0].shape[0]
    steps, whole, weight, across, _, rows = feed_specs(length, width, units, 1)
    kept = jax.ShapeDtypeStruct((length, units), BF16)
    sums = jax.ShapeDtypeStruct((8, units), F32)
    (e0, _, r0), (e1, _, r1) = halves
    return pl.pallas_call(
        functools.partial(back_kernel, steps),
        grid=(2 * steps,),
        out_shape=[jax.ShapeDtypeStruct((length, width), F32), kept, kept, sums, sums],
        in_specs=[whole, *weight, *weight, *across],
        out_specs=[whole, *across, *rows],
        compiler_params=pltpu.CompilerParams(vmem_limit_bytes=40 * 1024 * 1024),
        cost_estimate=estimate(8 * length * width * units, 8 * width * units),
        name="feed_back",
    )(grad, e0, e1, r0, r1, *slope)


def tie(value, *others):
    return lax.optimization_barrier((value, *others))[0]


def normalize_rows(rows):
    centred = rows - jnp.mean(rows, axis=-1, keepdims=True)
    inverse = lax.rsqrt(jnp.mean(centred * centred, axis=-1, keepdims=True) + EPSILON)
    return (centred * inverse, inverse)


def norm_backward(grad_normed, normed, inverse, gain):
    scaled = grad_normed * gain
    centred = scaled - jnp.mean(scaled, axis=-1, keepdims=True)
    return inverse * (centred - normed * jnp.mean(scaled * normed, axis=-1, keepdims=True))


def attention_forward(core, rows_in, weights, keep, before=(), after=()):
    gain_a, shift_a, proj, bias_q, bias_v, bias_out = weights
    normed_one, inverse_one = normalize_rows(rows_in)
    ready_one = narrow(normed_one * gain_a + shift_a)
    k = narrow(nt(ready_one, proj[1]))
    k_other = swap(k, "core")
    v = narrow(nt(ready_one, proj[2]) + bias_v)
    v_other = swap(v, "core")
    q = narrow(nt(ready_one, proj[0]) + bias_q)
    if before:
        q, proj_out, *before = lax.optimization_barrier((q, proj[3], *before))
        proj = [*proj[:3], proj_out]
        after = after(before)
    mixed, *kept_weights = attend(core, q, k, v, k_other, v_other, keep)
    mixed, *after = lax.optimization_barrier((mixed, *after))
    middle = rows_in + BRANCH * (nn(mixed, proj[3]) + bias_out)
    kept = (normed_one, inverse_one, ready_one, (q, k, v, k_other, v_other), mixed, *kept_weights)
    return middle, kept, after


def feed_start(middle, weights):
    gain_b, shift_b, _, _ = weights
    normed_two, inverse_two = normalize_rows(middle)
    return normed_two, inverse_two, narrow(normed_two * gain_b + shift_b)


def feed_forward_only(middle, weights):
    ready_two = feed_start(middle, weights)[2]
    first, second = weights[2]
    block = middle.shape[0] // 2
    total = jnp.broadcast_to(weights[3], (block, middle.shape[1]))
    totals = [feed_half(ready_two, *first, total, 0)]
    results = []
    for part in range(2):
        rows = slice(part * block, (part + 1) * block)
        if part:
            totals.append(feed_half(ready_two, *first, tie(total, *results), part))
        piece = feed_half(ready_two, *second, totals[part], part)
        results.append(narrow(middle[rows] + BRANCH * piece))
    return results


def feed_forward_and_back(middle, grad_result, weights):
    normed_two, inverse_two, ready_two = feed_start(middle, weights)
    rounded = narrow(BRANCH * grad_result)
    total, grad_total, *kept = feed_both(ready_two, rounded, weights[2])
    result = narrow(middle + BRANCH * (total + weights[3]))
    grad_middle = grad_result + norm_backward(grad_total, normed_two, inverse_two, weights[0])
    return result, grad_middle, (normed_two, inverse_two, ready_two, kept[:2], kept[2:])


def attention_backward(core, kept, grad_middle, weights, before=(), after=()):
    _, _, _, projected, mixed, *attention = kept
    rounded_attended = narrow(BRANCH * grad_middle)
    grad_mixed = narrow(nt(tie(rounded_attended, *before), weights[2][3]))
    grad_q, own, other, sums = attend_back(core, *projected, grad_mixed, mixed, *attention)
    other, *after = lax.optimization_barrier((other, *after))
    grad_kv = narrow(own + swap(other, "core").astype(F32))
    return rounded_attended, (grad_q, grad_kv[0], grad_kv[1]), sums[:2], after


def attention_input_grad(kept, grad_middle, grad_qkv, weights):
    gain_a, _, proj, _, _, _ = weights
    normed_one, inverse_one, *_ = kept
    grad_normed_one = sum(nn(grad, part) for grad, part in zip(grad_qkv, proj))
    grad_in = grad_middle + norm_backward(grad_normed_one, normed_one, inverse_one, gain_a)
    return grad_in, [grad_normed_one * normed_one, grad_normed_one, BRANCH * grad_middle]


def narrow(value):
    return value.astype(BF16)


def wide_add(left, right):
    return narrow(left.astype(F32) + right.astype(F32))


def over_groups(value):
    return lax.psum(value, "outer") if lax.axis_size("outer") > 1 else value


def ring_add(parts):
    count = len(parts)
    total = parts[1 % count]
    for step in range(1, count):
        total = wide_add(ring(total), parts[(step + 1) % count])
    return total


def thirds(values):
    pieces = []
    for _ in range(3):
        piece = lax.reduce_precision(values, 8, 7)
        pieces.append(narrow(piece))
        values = values - piece
    return jnp.stack(pieces)


def shards(
    inputs, cotangent, gain_one, shift_one, attend_in, attend_bias, attend_out, out_bias,
    gain_two, shift_two, expand_in, expand_bias, reduce_out, reduce_bias,
):
    count = lax.axis_size("tensor")
    x, y, c, z = (lax.axis_index(axis) for axis in AXES)
    is_first = x == 0
    core = c.reshape(1).astype(jnp.int32)
    width = attend_in.shape[1]
    local = attend_in.shape[3]
    units = expand_in.shape[2]
    part = units // 4
    spare = 16

    def either(index, pair):
        first, second = pair
        return jnp.where(index == 0, first, second), jnp.where(index == 0, second, first)

    def relative(blocks):
        rows = [either(y, blocks[:2]), either(y, blocks[2:])]
        return list(zip(*(either(c, pair) for pair in zip(*rows))))

    def quarters(value, axis):
        return relative(jnp.split(value, 4, axis))

    typed = [*attend_in[0].transpose(1, 2, 0), attend_out[0]]
    (mine, mine_y), _ = relative(typed)
    biases = thirds(jnp.concatenate([attend_bias[0].reshape(2 * local), expand_bias[0]])).reshape(-1)
    biases = jnp.pad(biases, (0, spare * width - biases.size)).reshape(spare, width)
    piece = jnp.concatenate([mine, biases])
    bias_rows = [biases]
    own_parts = [quarters(expand_in[0].T, 0), quarters(reduce_out[0], 0)]
    feed = [jnp.concatenate([value[0][0] for value in own_parts])]
    feed_y = [jnp.concatenate([value[0][1] for value in own_parts])]
    pieces, pieces_y = [ring(piece)], []
    arrived = fetch(inputs[0, 0], 0)
    while len(pieces) < count - 1:
        pieces_y.append(swap(pieces[-1][:local], "y"))
        pieces.append(ring(pieces[-1]))
        if len(pieces) < count - 1:
            pieces[-1], pieces_y[-1], feed[0], *arrived = lax.optimization_barrier(
                (pieces[-1], pieces_y[-1], feed[0], *arrived)
            )
    feed.append(ring(feed[0]))
    pieces[-1], pieces_y[-1] = lax.optimization_barrier((pieces[-1], pieces_y[-1]))
    pieces_y.append(swap(pieces[-1][:local], "y"))
    feed[1], pieces_y[-1] = lax.optimization_barrier((feed[1], pieces_y[-1]))
    feed_y.append(swap(feed[1], "y"))
    feed.append(ring(feed[1]))
    feed[2], feed_y[1] = lax.optimization_barrier((feed[2], feed_y[1]))
    feed_y.append(swap(feed[2], "y"))
    before = (ring(feed[2]), feed_y[2])
    bias_rows += [value[local:] for value in pieces]
    pieces = [mine] + [value[:local] for value in pieces]
    pieces_y = [mine_y] + pieces_y
    pieces = jnp.concatenate(pieces)
    pieces_y = jnp.concatenate(pieces_y)
    proj = relative([pieces, pieces_y, swap(pieces, "core"), swap(pieces_y, "core")])
    proj = [*proj[0], *proj[1]]
    biases = jnp.stack(bias_rows).reshape(count, -1)[:, : 3 * (2 * local + units)].reshape(count, 3, 2 * local + units)
    biases = biases.astype(F32)
    biases = biases[:, 0] + (biases[:, 1] + biases[:, 2])
    bias_q, bias_v = biases[:, :local].reshape(width), biases[:, local : 2 * local].reshape(width)
    expand_b = quarters(biases[:, 2 * local :], 1)
    expand_b = [jnp.concatenate([value.reshape(count * part) for value in pair]) for pair in expand_b]
    attention_weights = (gain_one[0], shift_one[0], proj, bias_q, bias_v, out_bias[0])

    rows_in = jnp.concatenate(arrived)
    middle, _, after = attention_forward(
        core, rows_in.astype(F32), attention_weights, False, before,
        lambda ready: (*ready, swap(ready[0], "y")),
    )
    feed.append(after[0])
    feed_y[2:] = after[1:]
    own_half = [
        jnp.concatenate([value[kind * part : (kind + 1) * part] for value in feed + feed_y]) for kind in range(2)
    ]
    other_half = [swap(value, "core") for value in own_half]
    feed_weights = (
        gain_two[0],
        shift_two[0],
        [(own_half[0], expand_b[0], own_half[1]), (other_half[0], expand_b[1], other_half[1])],
        reduce_bias[0],
    )
    passed = jnp.concatenate([along_pipe(rows, 1) for rows in feed_forward_only(middle, feed_weights)])
    last = fetch(tie(cotangent[0, 0], passed), 1)
    rows_in = jnp.where(is_first, rows_in, passed)
    middle, kept_attention, last = attention_forward(
        core, rows_in.astype(F32), attention_weights, True, (), last
    )
    last = jnp.concatenate(last)
    result, grad_middle, kept_feed = feed_forward_and_back(middle, last.astype(F32), feed_weights)
    block = result.shape[0] // 2
    outputs = give_back(result[:block], result[block:], 1)
    _, grad_qkv, _, (outputs,) = attention_backward(
        core, kept_attention, grad_middle, attention_weights, (), (outputs,)
    )
    grad_in = narrow(attention_input_grad(kept_attention, grad_middle, grad_qkv, attention_weights)[0])
    returned = jnp.concatenate([along_pipe(grad_in[:block], -1), along_pipe(grad_in[block:], -1)])
    grad_result = jnp.where(is_first, returned, last).astype(F32)
    grad_outcome = BRANCH * grad_result
    rounded_outcome = narrow(grad_outcome)
    normed_two, inverse_two, ready_two, hidden, slope = kept_feed
    span = count * part

    def by_slot(value):
        return [value[slot * part : (slot + 1) * part] for slot in range(count)]

    def steps_of(parts):
        state = [parts[1 % count]]

        def start():
            state.append(ring(state[-1]))
            return state[-1]

        def finish(arrived, step):
            state.append(wide_add(arrived, parts[(step + 1) % count]))
            return state[-1]

        return start, finish

    send = narrow(tn(hidden[1], rounded_outcome))
    arrived = swap(send, "core")
    keep = tn(hidden[0], tie(rounded_outcome, send))
    reduce_sums = wide_add(keep, tie(arrived, keep))
    to_y = reduce_sums[span:]
    to_y = [to_y[part : 3 * part], jnp.concatenate([to_y[3 * part :], to_y[:part]])]
    reduce_y = [swap(value, "y") for value in to_y]
    total, pre_own, pre_other, sums_own, sums_other = feed_back(
        tie(rounded_outcome, reduce_sums, *to_y), feed_weights[2], slope
    )
    pre_other, reduce_y[0] = lax.optimization_barrier((pre_other, reduce_y[0]))
    reduce_keep = by_slot(reduce_sums[:span])
    reduce_parts = [None, *(wide_add(reduce_keep[i + 1], reduce_y[0][i * part : (i + 1) * part]) for i in range(2)), None]
    reduce_start, reduce_finish = steps_of(reduce_parts)
    grad_middle = grad_result + norm_backward(total, normed_two, inverse_two, gain_two[0])
    shared_feed = [total * normed_two, total, grad_outcome]
    send = narrow(tn(tie(pre_other, grad_middle), ready_two))
    arrived = swap(send, "core")
    keep = tn(pre_own, tie(ready_two, send))
    expand_sums = wide_add(keep, tie(arrived, keep))
    expand_parts = [jnp.concatenate(pair) for pair in zip(by_slot(expand_sums[:span]), by_slot(expand_sums[span:]))]
    expand_start, expand_finish = steps_of(expand_parts)
    rounded_attended, grad_qkv, sums_qv, after = attention_backward(
        core, kept_attention, grad_middle, attention_weights, (*expand_parts, *reduce_parts[1:3]),
        (expand_start(), reduce_start(), reduce_y[1]),
    )
    expand_step, reduce_step = expand_finish(after[0], 1), reduce_finish(after[1], 1)
    reduce_parts[3] = wide_add(reduce_keep[3], after[2][:part])
    reduce_parts[0] = wide_add(reduce_keep[0], after[2][part:])
    moving_e, moving_r = expand_start(), reduce_start()
    grad_qkv = lax.optimization_barrier((*grad_qkv, expand_step, reduce_step))[:3]
    mixed, ready_one = kept_attention[4], kept_attention[2]
    left = jnp.stack([*grad_qkv, mixed])
    index = 2 * c + y

    def typed_grad(shift):
        right = jnp.where((index ^ shift) == 3, rounded_attended, ready_one)
        return tn(lax.dynamic_index_in_dim(left, index ^ shift, 0, False), right)

    send = [narrow(typed_grad(shift)) for shift in (3, 2)]
    arrived = [swap(value, "core") for value in send]
    left = tie(left, *send)
    keep = [typed_grad(shift) for shift in (1, 0)]
    moving_e, *keep = lax.optimization_barrier((moving_e, *keep))
    expand_finish(moving_e, 2)
    moving_e = expand_start()
    sums = [wide_add(a, b) for a, b in zip(keep, arrived)]
    to_y, to_keep = by_slot(sums[0]), by_slot(sums[1])
    typed_parts = [None] * count

    def typed_swap(slot):
        return swap(to_y[slot], "y")

    def typed_part(slot, arrived):
        typed_parts[slot] = wide_add(to_keep[slot], arrived)

    moving_y, moving_z = typed_swap(1), typed_swap(2)
    grad_qkv = lax.optimization_barrier((grad_qkv, sums))[0]
    grad_in, shared_attention = attention_input_grad(kept_attention, grad_middle, grad_qkv, attention_weights)
    grad_in = narrow(grad_in)
    shared = jnp.stack([jnp.sum(value, axis=0) for value in shared_attention + shared_feed])
    sums_qv = sums_qv.reshape(2, count, local)
    sums_qv = jnp.concatenate([sums_qv[0], sums_qv[1], jnp.zeros((count, width - 2 * local), F32)], axis=1)[:, None]
    sums_pre = [value.reshape(count, part) for half in (sums_own[0], sums_other[0]) for value in jnp.split(half, 2)]
    sums_pre = quarters(jnp.concatenate(sums_pre, axis=1), 1)
    sums_pre = jnp.concatenate(sums_pre[0] + sums_pre[1], axis=1)[:, None]
    vectors = jnp.concatenate([jnp.broadcast_to(shared, (count,) + shared.shape), sums_qv, sums_pre], axis=1)
    vectors = vectors + swap(vectors, "core")

    moving_y, moving_r, to_y[3], to_y[0] = lax.optimization_barrier((moving_y, moving_r, to_y[3], to_y[0]))
    typed_part(1, moving_y)
    reduce_finish(moving_r, 2)
    typed_start, typed_finish = steps_of(typed_parts)
    moving_t, moving_y, moving_v, moving_r = typed_start(), typed_swap(3), swap(vectors, "y"), reduce_start()
    moving_t, moving_z, moving_v, moving_e = lax.optimization_barrier((moving_t, moving_z, moving_v, moving_e))
    vectors = vectors + moving_v
    typed_part(2, moving_z)
    typed_finish(moving_t, 1)
    expand_total = expand_finish(moving_e, 3).reshape(2, part, width)
    moving_t, moving_z, moving_v = typed_start(), typed_swap(0), ring(vectors[1])
    moving_t, moving_y, moving_v, moving_r = lax.optimization_barrier((moving_t, moving_y, moving_v, moving_r))
    reduce_total = over_groups(reduce_finish(moving_r, 3))
    typed_part(3, moving_y)
    typed_finish(moving_t, 2)
    moving_v = ring(moving_v + vectors[2])
    moving_t, reduce_other, expand_other = typed_start(), swap(reduce_total, "y"), swap(expand_total, "y")
    moving_t, moving_z, moving_v, reduce_other, grad_in = lax.optimization_barrier(
        (moving_t, moving_z, moving_v, reduce_other, grad_in)
    )
    typed_part(0, moving_z)
    typed_total = over_groups(typed_finish(moving_t, 3))
    moving_v = ring(moving_v + vectors[3])
    typed_other = swap(typed_total, "y")
    input_grad = give_back(grad_in[:block], grad_in[block:], 0)
    typed_other, expand_other, moving_v = lax.optimization_barrier((typed_other, expand_other, moving_v))
    vectors = over_groups(moving_v + vectors[0])
    def gathered(pair):
        pair = jnp.concatenate(pair)
        blocks = quarters(jnp.concatenate([pair, swap(pair, "core")]), 0)
        return jnp.concatenate(blocks[0] + blocks[1])

    pair = jnp.concatenate([typed_total, typed_other])
    pair_other = swap(pair, "core")
    grad_expand = [over_groups(wide_add(expand_total[i], expand_other[1 - i])) for i in range(2)]
    grad_expand = gathered(grad_expand).T.astype(F32)
    grad_reduce = gathered([reduce_total, reduce_other]).astype(F32)
    whole = relative([pair[:local], pair[local:], pair_other[:local], pair_other[local:]])
    whole = [*whole[0], *whole[1]]
    grad_attend_in = jnp.stack(whole[:3]).transpose(2, 0, 1).astype(F32)
    grad_attend_out = whole[3].astype(F32)
    return (
        outputs[None, None],
        input_grad[None, None],
        vectors[0][None],
        vectors[1][None],
        grad_attend_in[None],
        vectors[6, : 2 * local].reshape(1, 2, local),
        grad_attend_out[None],
        vectors[2][None],
        vectors[3][None],
        vectors[4][None],
        grad_expand[None],
        vectors[7, :units][None],
        grad_reduce[None],
        vectors[5][None],
    )


def solution(mesh):
    pipe, groups, count = mesh.devices.shape
    split = Mesh(mesh.devices.reshape(pipe, groups // 4, 2, 2, count), ("pipe", "outer", "y", "core", "tensor"))
    dp = ("outer", "y", "core")
    rows = P("pipe", dp, "tensor", None)
    vector = P("pipe", None)
    placed = (
        rows,
        rows,
        vector,
        vector,
        P("pipe", None, None, "tensor"),
        P("pipe", None, "tensor"),
        P("pipe", "tensor", None),
        vector,
        vector,
        vector,
        P("pipe", None, "tensor"),
        P("pipe", "tensor"),
        P("pipe", "tensor", None),
        vector,
    )
    return jax.shard_map(shards, mesh=split, in_specs=placed, out_specs=(rows, rows) + placed[2:], check_vma=False)
```

```python
import functools

import jax
import jax.numpy as jnp
import numpy as np
from jax import lax
from jax.experimental import pallas as pl
from jax.experimental.pallas import tpu as pltpu
from jax.sharding import Mesh
from jax.sharding import PartitionSpec as P

HEAD = 64
DEPTH = 12
BRANCH = DEPTH ** (-0.5)
EPSILON = 1e-05
NEGATIVE = -1e30
LANES = 128
AXES = ("pipe", "y", "core", "tensor")
F32 = jnp.float32
BF16 = jnp.bfloat16


def ring_order(count):
    return list(range(0, count, 2)) + list(range(1, count, 2))[::-1]


def ring(value):
    order = ring_order(lax.axis_size("tensor"))
    return lax.ppermute(value, "tensor", list(zip(order, order[1:] + order[:1])))


def swap(value, axis):
    return lax.ppermute(value, axis, [(0, 1), (1, 0)])


def along_pipe(value, by):
    return lax.ppermute(value, "pipe", [(0, 1)] if by > 0 else [(1, 0)])


def routes(section, large):
    count = lax.axis_size("tensor")

    def index(x, y, c, z):
        return ((x * 2 + y) * 2 + c) * count + z

    pairs = []
    for micro in range(2):
        for y in range(2):
            for c in range(2):
                for core in range(2):
                    block = 3 - core if large else core
                    pairs.append((index(micro, y, c, block), index(section, y, core, 2 * c + micro)))
    return pairs


def fetch(block, section):
    return [lax.ppermute(block, AXES, routes(section, large)) for large in (False, True)]


def give_back(small, large, section):
    pieces = []
    for rows, is_large in ((small, False), (large, True)):
        pairs = [(b, a) for a, b in routes(section, is_large)]
        pieces.append(lax.ppermute(rows, AXES, pairs))
    return jnp.where(lax.axis_index("tensor") < 2, pieces[0], pieces[1])


def nt(left, right):
    return lax.dot_general(left, right, (((1,), (1,)), ((), ())), preferred_element_type=F32)


def tn(left, right):
    return lax.dot_general(left, right, (((0,), (0,)), ((), ())), preferred_element_type=F32)


def nn(left, right):
    return lax.dot_general(left, right, (((1,), (0,)), ((), ())), preferred_element_type=F32)


def estimate(flops, size):
    return pl.CostEstimate(flops=flops, bytes_accessed=size, transcendentals=0)


def head_mask(rows, head):
    lanes = lax.broadcasted_iota(jnp.int32, (rows, LANES), 1)
    return (lanes >= head * HEAD) & (lanes < (head + 1) * HEAD)


def only(mask, value, factor=1.0):
    return jnp.where(mask, value.astype(F32) * factor, 0.0).astype(BF16)


def turned(value):
    return value.astype(F32).T.astype(BF16)


def attend_kernel(keep_weights, core_ref, *refs):
    @pl.when(core_ref[1] == 1)
    def _():
        attend_pair(keep_weights, core_ref, *refs)


def attend_pair(keep_weights, core_ref, q_ref, k_ref, v_ref, ko_ref, vo_ref, o_ref, *kept_refs):
    rows = q_ref.shape[0] // 2
    second = core_ref[0] == 1
    keys = lax.broadcasted_iota(jnp.int32, (rows, rows), 0)
    places = lax.broadcasted_iota(jnp.int32, (rows, rows), 1)
    allowed = keys <= places
    factor = HEAD ** (-0.5)
    small = pl.ds(0, rows)
    large = pl.ds(rows, rows)

    def fifth(ref):
        return jnp.where(second, ref[small, :].astype(F32), ref[large, :].astype(F32)).astype(BF16)

    k5, q5 = fifth(ko_ref), fifth(q_ref)
    vs, vl, v4, v5 = turned(v_ref[small, :]), turned(v_ref[large, :]), turned(vo_ref[small, :]), turned(fifth(vo_ref))
    small_parts, large_parts, scales = [], [], []
    for head in range(LANES // HEAD):
        mask = head_mask(rows, head)
        lanes = slice(head * HEAD, (head + 1) * HEAD)
        qs, ql, qf = (only(mask, value, factor) for value in (q_ref[small, :], q_ref[large, :], q5))
        s1 = jnp.where(allowed, nt(k_ref[small, :], qs), NEGATIVE)
        s2 = nt(k_ref[small, :], ql)
        s3 = jnp.where(allowed, nt(k_ref[large, :], ql), NEGATIVE)
        s4 = nt(ko_ref[small, :], ql)
        s5 = nt(k5, qf)

        def peak(value):
            return jnp.max(value, axis=0, keepdims=True)

        def total(value):
            return jnp.sum(value, axis=0, keepdims=True)

        m5 = peak(s5)
        ms = peak(s1)
        ml = jnp.maximum(jnp.maximum(peak(s2), peak(s3)), peak(s4))
        ms = jnp.where(second, jnp.maximum(ms, m5), ms)
        ml = jnp.where(second, ml, jnp.maximum(ml, m5))
        mf = jnp.where(second, ms, ml)
        e1 = jnp.exp(s1 - ms)
        e2 = jnp.exp(s2 - ml)
        e3 = jnp.exp(s3 - ml)
        e4 = jnp.exp(s4 - ml)
        e5 = jnp.exp(s5 - mf)
        t5 = total(e5)
        rs = total(e1)
        rl = total(e2) + total(e3) + total(e4)
        rs = 1.0 / jnp.where(second, rs + t5, rs)
        rl = 1.0 / jnp.where(second, rl, rl + t5)
        e1, e2, e3, e4, e5 = (value.astype(BF16) for value in (e1, e2, e3, e4, e5))
        if keep_weights:
            for place, value in enumerate((e1, e2, e3, e4, e5)):
                kept_refs[0][head, place] = value
            scales.append(jnp.concatenate([rs, rl], axis=1))
        o5 = nn(v5[lanes], e5)
        small_parts.append((nn(vs[lanes], e1) + jnp.where(second, o5, 0.0)) * rs)
        large_parts.append(
            (nn(vs[lanes], e2) + nn(vl[lanes], e3) + nn(v4[lanes], e4) + jnp.where(second, 0.0, o5)) * rl
        )
    o_ref[small, :] = jnp.concatenate(small_parts).T.astype(BF16)
    o_ref[large, :] = jnp.concatenate(large_parts).T.astype(BF16)
    if keep_weights:
        row = lax.broadcasted_iota(jnp.int32, (8, 2 * rows), 0)
        kept_refs[1][...] = jnp.where(row == 0, scales[0], scales[1])


def attend_back_kernel(
    core_ref, q_ref, k_ref, v_ref, ko_ref, vo_ref, go_ref, o_ref, e_ref, scale_ref, gq_ref, own_ref, other_ref, sums_ref
):
    rows = q_ref.shape[0] // 2
    second = core_ref[0] == 1
    factor = HEAD ** (-0.5)
    small = pl.ds(0, rows)
    large = pl.ds(rows, rows)

    def fifth(first, last):
        return jnp.where(second, first.astype(F32), last.astype(F32)).astype(BF16)

    row = lax.broadcasted_iota(jnp.int32, (LANES, 2 * rows), 0)
    scale = jnp.where(row < HEAD, scale_ref[0:1, :], scale_ref[1:2, :]).T
    grads = (go_ref[...].astype(F32) * scale).astype(BF16)
    product = grads.astype(F32) * o_ref[...].astype(F32)
    high = product.astype(BF16)
    low = (product - high.astype(F32)).astype(BF16)
    g_small, g_large = grads[:rows], grads[rows:]
    g5 = fifth(g_small, g_large)
    q5 = fifth(q_ref[small, :], q_ref[large, :])
    v5 = fifth(vo_ref[small, :], vo_ref[large, :])
    ks, kl, k4, k5 = (
        turned(k_ref[small, :]), turned(k_ref[large, :]), turned(ko_ref[small, :]),
        turned(fifth(ko_ref[small, :], ko_ref[large, :])),
    )
    totals = {}
    gq_small, gq_large = [], []

    def add(name, value):
        totals[name] = value if name not in totals else totals[name] + value

    for head in range(LANES // HEAD):
        mask = head_mask(rows, head)
        lanes = slice(head * HEAD, (head + 1) * HEAD)
        ones = jnp.where(head_mask(16, head), 1.0, 0.0).astype(BF16)
        inner = (nt(ones, high) + nt(ones, low))[0:1]
        ds_, dl_ = inner[:, :rows], inner[:, rows:]
        df_ = jnp.where(second, ds_, dl_)
        qs, ql, qf = (only(mask, value, factor) for value in (q_ref[small, :], q_ref[large, :], q5))
        gs, gl, gf = (only(mask, value) for value in (g_small, g_large, g5))

        def score_grad(place, values, rows_grad, shift):
            return (e_ref[head, place].astype(F32) * (nt(values, rows_grad) - shift)).astype(BF16)

        z1 = score_grad(0, v_ref[small, :], gs, ds_)
        z2 = score_grad(1, v_ref[small, :], gl, dl_)
        z3 = score_grad(2, v_ref[large, :], gl, dl_)
        z4 = score_grad(3, vo_ref[small, :], gl, dl_)
        z5 = score_grad(4, v5, gf, df_)
        gq5 = nn(k5[lanes], z5)
        gq_small.append(nn(ks[lanes], z1) + jnp.where(second, gq5, 0.0))
        gq_large.append(nn(ks[lanes], z2) + nn(kl[lanes], z3) + nn(k4[lanes], z4) + jnp.where(second, 0.0, gq5))
        add("ks", nn(z1, qs) + nn(z2, ql))
        add("kl", nn(z3, ql))
        add("k4", nn(z4, ql))
        add("k5", nn(z5, qf))
        add("vs", nn(e_ref[head, 0], gs) + nn(e_ref[head, 1], gl))
        add("vl", nn(e_ref[head, 2], gl))
        add("v4", nn(e_ref[head, 3], gl))
        add("v5", nn(e_ref[head, 4], gf))
    gqs, gql = jnp.concatenate(gq_small).T * factor, jnp.concatenate(gq_large).T * factor
    gq_ref[small, :] = gqs.astype(BF16)
    gq_ref[large, :] = gql.astype(BF16)
    for place, name in enumerate("kv"):
        own_ref[place, small, :] = totals[name + "s"]
        own_ref[place, large, :] = totals[name + "l"]
        four, five = totals[name + "4"], totals[name + "5"]
        other_ref[place, small, :] = (four + jnp.where(second, five, 0.0)).astype(BF16)
        other_ref[place, large, :] = jnp.where(second, 0.0, five).astype(BF16)
    sum_q = jnp.sum(gqs, axis=0, keepdims=True) + jnp.sum(gql, axis=0, keepdims=True)
    sum_v = jnp.sum(totals["vs"] + totals["vl"] + totals["v4"] + totals["v5"], axis=0, keepdims=True)
    row = lax.broadcasted_iota(jnp.int32, (8, LANES), 0)
    sums_ref[...] = jnp.where(row == 0, sum_q, jnp.where(row == 1, sum_v, 0.0))


def attend(core, q, k, v, k_other, v_other, keep_weights):
    length, width = q.shape
    rows = length // 2
    pairs = width // LANES
    column = pl.BlockSpec((length, LANES), lambda i: (0, i))
    shapes = [jax.ShapeDtypeStruct((length, width), BF16)]
    outs = [column]
    if keep_weights:
        shapes.append(pltpu.HBM((width // HEAD, 5, rows, rows), BF16))
        shapes.append(jax.ShapeDtypeStruct((8 * pairs, length), F32))
        outs.append(pl.BlockSpec((2, 5, rows, rows), lambda i: (i, 0, 0, 0)))
        outs.append(pl.BlockSpec((8, length), lambda i: (i, 0)))
    return pl.pallas_call(
        functools.partial(attend_kernel, keep_weights),
        grid=(pairs,),
        out_shape=shapes,
        in_specs=[pl.BlockSpec(memory_space=pltpu.SMEM)] + [column] * 5,
        out_specs=outs,
        compiler_params=pltpu.CompilerParams(vmem_limit_bytes=40 * 1024 * 1024),
        cost_estimate=estimate(20 * rows * rows * width * 2, 16 * length * width),
        name="attend",
    )(core, q, k, v, k_other, v_other)


def attend_back(core, q, k, v, k_other, v_other, grad_mixed, mixed, weights, scales):
    length, width = q.shape
    rows = length // 2
    column = pl.BlockSpec((length, LANES), lambda i: (0, i))
    double = pl.BlockSpec((2, length, LANES), lambda i: (0, 0, i))
    return pl.pallas_call(
        attend_back_kernel,
        grid=(width // LANES,),
        out_shape=[
            jax.ShapeDtypeStruct((length, width), BF16),
            jax.ShapeDtypeStruct((2, length, width), F32),
            jax.ShapeDtypeStruct((2, length, width), BF16),
            jax.ShapeDtypeStruct((8, width), F32),
        ],
        in_specs=[pl.BlockSpec(memory_space=pltpu.SMEM)]
        + [column] * 7
        + [pl.BlockSpec((2, 5, rows, rows), lambda i: (i, 0, 0, 0)), pl.BlockSpec((8, length), lambda i: (i, 0))],
        out_specs=[column, double, double, pl.BlockSpec((8, LANES), lambda i: (0, i))],
        compiler_params=pltpu.CompilerParams(vmem_limit_bytes=40 * 1024 * 1024),
        cost_estimate=estimate(40 * rows * rows * width * 2, 40 * length * width),
        name="attend_back",
    )(core, q, k, v, k_other, v_other, grad_mixed, mixed, weights, scales)


def gelu_and_slope(values):
    root = float(np.sqrt(2 / np.pi))
    cubic = 0.044715 * root
    square = values * values
    bend = jnp.tanh(values * (root + cubic * square))
    half = 0.5 + 0.5 * bend
    gate = values * half
    slope = half + gate * ((1.0 - bend) * (root + (3 * cubic) * square))
    return (gate, slope)


def expand_kernel(core_ref, rows_ref, expand_ref, bias_ref, reduce_ref, start_ref, total_ref):
    @pl.when(core_ref[1] == 1)
    def _():
        gate, _ = gelu_and_slope(nt(rows_ref[...], expand_ref[...]) + bias_ref[...])
        total_ref[...] = start_ref[...] + nn(gate.astype(BF16), reduce_ref[...])


def feed_half(core, rows, expand_w, bias, reduce_w, start, row_part=None):
    length, width = rows.shape
    units = expand_w.shape[0]
    if row_part is not None:
        length = length // 2
    place = row_part or 0
    whole = pl.BlockSpec((length, width), lambda i: (0, 0))
    taken = pl.BlockSpec((length, width), lambda i: (place, 0))
    start_place = 0 if start.shape[0] == length else place
    begun = pl.BlockSpec((length, width), lambda i: (start_place, 0))
    weight = pl.BlockSpec((units, width), lambda i: (0, 0))
    return pl.pallas_call(
        expand_kernel,
        grid=(1,),
        out_shape=jax.ShapeDtypeStruct((length, width), F32),
        in_specs=[
            pl.BlockSpec(memory_space=pltpu.SMEM),
            taken, weight, pl.BlockSpec((1, units), lambda i: (0, 0)), weight, begun,
        ],
        out_specs=whole,
        compiler_params=pltpu.CompilerParams(vmem_limit_bytes=40 * 1024 * 1024),
        cost_estimate=estimate(4 * length * width * units, 4 * width * units),
        name="feed_half",
    )(core, rows, expand_w, bias.reshape(1, units), reduce_w, start)


def both_kernel(
    steps, rows_ref, grad_ref, e0_ref, e1_ref, b0_ref, b1_ref, r0_ref, r1_ref,
    total_ref, grad_total_ref, h0_ref, h1_ref, s0_ref, s1_ref,
):
    place = pl.program_id(0)

    @pl.when(place == 0)
    def _():
        total_ref[...] = jnp.zeros_like(total_ref)
        grad_total_ref[...] = jnp.zeros_like(grad_total_ref)

    def tile(expand_ref, bias_ref, reduce_ref, hidden_ref, slope_ref):
        gate, slope = gelu_and_slope(nt(rows_ref[...], expand_ref[...]) + bias_ref[...])
        hidden = gate.astype(BF16)
        slope = slope.astype(BF16)
        hidden_ref[...] = hidden
        slope_ref[...] = slope
        total_ref[...] += nn(hidden, reduce_ref[...])
        pre = nt(grad_ref[...], reduce_ref[...]) * slope.astype(F32)
        grad_total_ref[...] += nn(pre.astype(BF16), expand_ref[...])

    @pl.when(place < steps)
    def _():
        tile(e0_ref, b0_ref, r0_ref, h0_ref, s0_ref)

    @pl.when(place >= steps)
    def _():
        tile(e1_ref, b1_ref, r1_ref, h1_ref, s1_ref)


def back_kernel(
    steps, grad_ref, e0_ref, e1_ref, r0_ref, r1_ref, s0_ref, s1_ref,
    total_ref, p0_ref, p1_ref, sums0_ref, sums1_ref,
):
    place = pl.program_id(0)

    @pl.when(place == 0)
    def _():
        total_ref[...] = jnp.zeros_like(total_ref)

    def tile(expand_ref, reduce_ref, slope_ref, pre_ref, sums_ref):
        pre = nt(grad_ref[...], reduce_ref[...]) * slope_ref[...].astype(F32)
        sums_ref[...] = jnp.broadcast_to(jnp.sum(pre, axis=0, keepdims=True), sums_ref.shape)
        rounded = pre.astype(BF16)
        pre_ref[...] = rounded
        total_ref[...] += nn(rounded, expand_ref[...])

    @pl.when(place < steps)
    def _():
        tile(e0_ref, r0_ref, s0_ref, p0_ref, sums0_ref)

    @pl.when(place >= steps)
    def _():
        tile(e1_ref, r1_ref, s1_ref, p1_ref, sums1_ref)


def feed_specs(length, width, units, steps):
    tile = units // steps
    whole = pl.BlockSpec((length, width), lambda i: (0, 0))

    def early(i):
        return jnp.minimum(i, steps - 1)

    def late(i):
        return jnp.maximum(i - steps, 0)

    weight = [pl.BlockSpec((tile, width), lambda i, f=f: (f(i), 0)) for f in (early, late)]
    across = [pl.BlockSpec((length, tile), lambda i, f=f: (0, f(i))) for f in (early, late)]
    row = [pl.BlockSpec((1, tile), lambda i, f=f: (0, f(i))) for f in (early, late)]
    rows = [pl.BlockSpec((8, tile), lambda i, f=f: (0, f(i))) for f in (early, late)]
    return steps, whole, weight, across, row, rows


def feed_both(rows, grad, halves):
    length, width = rows.shape
    units = halves[0][0].shape[0]
    steps, whole, weight, across, row, _ = feed_specs(length, width, units, 2)
    total = jax.ShapeDtypeStruct((length, width), F32)
    kept = jax.ShapeDtypeStruct((length, units), BF16)
    (e0, b0, r0), (e1, b1, r1) = halves
    return pl.pallas_call(
        functools.partial(both_kernel, steps),
        grid=(2 * steps,),
        out_shape=[total, total, kept, kept, kept, kept],
        in_specs=[whole, whole, *weight, *row, *weight],
        out_specs=[whole, whole, *across, *across],
        compiler_params=pltpu.CompilerParams(vmem_limit_bytes=40 * 1024 * 1024),
        cost_estimate=estimate(16 * length * width * units, 8 * width * units),
        name="feed_both",
    )(rows, grad, e0, e1, b0.reshape(1, units), b1.reshape(1, units), r0, r1)


def feed_back(grad, halves, slope):
    length, width = grad.shape
    units = halves[0][0].shape[0]
    steps, whole, weight, across, _, rows = feed_specs(length, width, units, 1)
    kept = jax.ShapeDtypeStruct((length, units), BF16)
    sums = jax.ShapeDtypeStruct((8, units), F32)
    (e0, _, r0), (e1, _, r1) = halves
    return pl.pallas_call(
        functools.partial(back_kernel, steps),
        grid=(2 * steps,),
        out_shape=[jax.ShapeDtypeStruct((length, width), F32), kept, kept, sums, sums],
        in_specs=[whole, *weight, *weight, *across],
        out_specs=[whole, *across, *rows],
        compiler_params=pltpu.CompilerParams(vmem_limit_bytes=40 * 1024 * 1024),
        cost_estimate=estimate(8 * length * width * units, 8 * width * units),
        name="feed_back",
    )(grad, e0, e1, r0, r1, *slope)


def tie(value, *others):
    return lax.optimization_barrier((value, *others))[0]


def normalize_rows(rows):
    centred = rows - jnp.mean(rows, axis=-1, keepdims=True)
    inverse = lax.rsqrt(jnp.mean(centred * centred, axis=-1, keepdims=True) + EPSILON)
    return (centred * inverse, inverse)


def norm_backward(grad_normed, normed, inverse, gain):
    scaled = grad_normed * gain
    centred = scaled - jnp.mean(scaled, axis=-1, keepdims=True)
    return inverse * (centred - normed * jnp.mean(scaled * normed, axis=-1, keepdims=True))


def attention_forward(core, rows_in, weights, keep, before=(), after=()):
    gain_a, shift_a, proj, bias_q, bias_v, bias_out = weights
    normed_one, inverse_one = normalize_rows(rows_in)
    ready_one = narrow(normed_one * gain_a + shift_a)
    k = narrow(nt(ready_one, proj[1]))
    k_other = swap(k, "core")
    v = narrow(nt(ready_one, proj[2]) + bias_v)
    v_other = swap(v, "core")
    q = narrow(nt(ready_one, proj[0]) + bias_q)
    if before:
        q, proj_out, *before = lax.optimization_barrier((q, proj[3], *before))
        proj = [*proj[:3], proj_out]
        after = after(before)
    mixed, *kept_weights = attend(core, q, k, v, k_other, v_other, keep)
    mixed, *after = lax.optimization_barrier((mixed, *after))
    middle = rows_in + BRANCH * (nn(mixed, proj[3]) + bias_out)
    kept = (normed_one, inverse_one, ready_one, (q, k, v, k_other, v_other), mixed, *kept_weights)
    return middle, kept, after


def feed_start(middle, weights):
    gain_b, shift_b, _, _ = weights
    normed_two, inverse_two = normalize_rows(middle)
    return normed_two, inverse_two, narrow(normed_two * gain_b + shift_b)


def feed_forward_only(core, middle, weights):
    ready_two = feed_start(middle, weights)[2]
    first, second = weights[2]
    block = middle.shape[0] // 2
    total = jnp.broadcast_to(weights[3], (block, middle.shape[1]))
    totals = [feed_half(core, ready_two, *first, total, 0)]
    results = []
    for part in range(2):
        rows = slice(part * block, (part + 1) * block)
        if part:
            totals.append(feed_half(core, ready_two, *first, tie(total, *results), part))
        piece = feed_half(core, ready_two, *second, totals[part], part)
        results.append(narrow(middle[rows] + BRANCH * piece))
    return results


def feed_forward_and_back(middle, grad_result, weights):
    normed_two, inverse_two, ready_two = feed_start(middle, weights)
    rounded = narrow(BRANCH * grad_result)
    total, grad_total, *kept = feed_both(ready_two, rounded, weights[2])
    result = narrow(middle + BRANCH * (total + weights[3]))
    grad_middle = grad_result + norm_backward(grad_total, normed_two, inverse_two, weights[0])
    return result, grad_middle, (normed_two, inverse_two, ready_two, kept[:2], kept[2:])


def attention_backward(core, kept, grad_middle, weights, before=(), after=()):
    _, _, _, projected, mixed, *attention = kept
    rounded_attended = narrow(BRANCH * grad_middle)
    grad_mixed = narrow(nt(tie(rounded_attended, *before), weights[2][3]))
    grad_q, own, other, sums = attend_back(core, *projected, grad_mixed, mixed, *attention)
    other, *after = lax.optimization_barrier((other, *after))
    grad_kv = narrow(own + swap(other, "core").astype(F32))
    return rounded_attended, (grad_q, grad_kv[0], grad_kv[1]), sums[:2], after


def attention_input_grad(kept, grad_middle, grad_qkv, weights):
    gain_a, _, proj, _, _, _ = weights
    normed_one, inverse_one, *_ = kept
    grad_normed_one = sum(nn(grad, part) for grad, part in zip(grad_qkv, proj))
    grad_in = grad_middle + norm_backward(grad_normed_one, normed_one, inverse_one, gain_a)
    return grad_in, [grad_normed_one * normed_one, grad_normed_one, BRANCH * grad_middle]


def narrow(value):
    return value.astype(BF16)


def wide_add(left, right):
    return narrow(left.astype(F32) + right.astype(F32))


def over_groups(value):
    return lax.psum(value, "outer") if lax.axis_size("outer") > 1 else value


def ring_add(parts):
    count = len(parts)
    total = parts[1 % count]
    for step in range(1, count):
        total = wide_add(ring(total), parts[(step + 1) % count])
    return total


def thirds(values):
    pieces = []
    for _ in range(3):
        piece = lax.reduce_precision(values, 8, 7)
        pieces.append(narrow(piece))
        values = values - piece
    return jnp.stack(pieces)


def shards(
    inputs, cotangent, gain_one, shift_one, attend_in, attend_bias, attend_out, out_bias,
    gain_two, shift_two, expand_in, expand_bias, reduce_out, reduce_bias,
):
    count = lax.axis_size("tensor")
    x, y, c, z = (lax.axis_index(axis) for axis in AXES)
    is_first = x == 0
    core = jnp.stack([c, jnp.ones_like(c)]).astype(jnp.int32)
    core_a = jnp.stack([c, 1 - x]).astype(jnp.int32)
    width = attend_in.shape[1]
    local = attend_in.shape[3]
    units = expand_in.shape[2]
    part = units // 4
    spare = 16

    def either(index, pair):
        first, second = pair
        return jnp.where(index == 0, first, second), jnp.where(index == 0, second, first)

    def relative(blocks):
        rows = [either(y, blocks[:2]), either(y, blocks[2:])]
        return list(zip(*(either(c, pair) for pair in zip(*rows))))

    def quarters(value, axis):
        return relative(jnp.split(value, 4, axis))

    typed = [*attend_in[0].transpose(1, 2, 0), attend_out[0]]
    (mine, mine_y), _ = relative(typed)
    biases = thirds(jnp.concatenate([attend_bias[0].reshape(2 * local), expand_bias[0]])).reshape(-1)
    biases = jnp.pad(biases, (0, spare * width - biases.size)).reshape(spare, width)
    piece = jnp.concatenate([mine, biases])
    bias_rows = [biases]
    own_parts = [quarters(expand_in[0].T, 0), quarters(reduce_out[0], 0)]
    feed = [jnp.concatenate([value[0][0] for value in own_parts])]
    feed_y = [jnp.concatenate([value[0][1] for value in own_parts])]
    pieces, pieces_y = [ring(piece)], []
    arrived = fetch(inputs[0, 0], 0)
    while len(pieces) < count - 1:
        pieces_y.append(swap(pieces[-1][:local], "y"))
        pieces.append(ring(pieces[-1]))
        if len(pieces) < count - 1:
            pieces[-1], pieces_y[-1], feed[0], *arrived = lax.optimization_barrier(
                (pieces[-1], pieces_y[-1], feed[0], *arrived)
            )
    feed.append(ring(feed[0]))
    pieces[-1], pieces_y[-1] = lax.optimization_barrier((pieces[-1], pieces_y[-1]))
    pieces_y.append(swap(pieces[-1][:local], "y"))
    feed[1], pieces_y[-1] = lax.optimization_barrier((feed[1], pieces_y[-1]))
    feed_y.append(swap(feed[1], "y"))
    feed.append(ring(feed[1]))
    feed[2], feed_y[1] = lax.optimization_barrier((feed[2], feed_y[1]))
    feed_y.append(swap(feed[2], "y"))
    before = (ring(feed[2]), feed_y[2])
    bias_rows += [value[local:] for value in pieces]
    pieces = [mine] + [value[:local] for value in pieces]
    pieces_y = [mine_y] + pieces_y
    pieces = jnp.concatenate(pieces)
    pieces_y = jnp.concatenate(pieces_y)
    proj = relative([pieces, pieces_y, swap(pieces, "core"), swap(pieces_y, "core")])
    proj = [*proj[0], *proj[1]]
    biases = jnp.stack(bias_rows).reshape(count, -1)[:, : 3 * (2 * local + units)].reshape(count, 3, 2 * local + units)
    biases = biases.astype(F32)
    biases = biases[:, 0] + (biases[:, 1] + biases[:, 2])
    bias_q, bias_v = biases[:, :local].reshape(width), biases[:, local : 2 * local].reshape(width)
    expand_b = quarters(biases[:, 2 * local :], 1)
    expand_b = [jnp.concatenate([value.reshape(count * part) for value in pair]) for pair in expand_b]
    attention_weights = (gain_one[0], shift_one[0], proj, bias_q, bias_v, out_bias[0])

    rows_in = jnp.concatenate(arrived)
    middle, _, after = attention_forward(
        core_a, rows_in.astype(F32), attention_weights, False, before,
        lambda ready: (*ready, swap(ready[0], "y")),
    )
    feed.append(after[0])
    feed_y[2:] = after[1:]
    own_half = [
        jnp.concatenate([value[kind * part : (kind + 1) * part] for value in feed + feed_y]) for kind in range(2)
    ]
    other_half = [swap(value, "core") for value in own_half]
    feed_weights = (
        gain_two[0],
        shift_two[0],
        [(own_half[0], expand_b[0], own_half[1]), (other_half[0], expand_b[1], other_half[1])],
        reduce_bias[0],
    )
    passed = jnp.concatenate([along_pipe(rows, 1) for rows in feed_forward_only(core_a, middle, feed_weights)])
    last = fetch(tie(cotangent[0, 0], passed), 1)
    rows_in = jnp.where(is_first, rows_in, passed)
    middle, kept_attention, last = attention_forward(
        core, rows_in.astype(F32), attention_weights, True, (), last
    )
    last = jnp.concatenate(last)
    result, grad_middle, kept_feed = feed_forward_and_back(middle, last.astype(F32), feed_weights)
    block = result.shape[0] // 2
    outputs = give_back(result[:block], result[block:], 1)
    _, grad_qkv, _, (outputs,) = attention_backward(
        core, kept_attention, grad_middle, attention_weights, (), (outputs,)
    )
    grad_in = narrow(attention_input_grad(kept_attention, grad_middle, grad_qkv, attention_weights)[0])
    returned = jnp.concatenate([along_pipe(grad_in[:block], -1), along_pipe(grad_in[block:], -1)])
    grad_result = jnp.where(is_first, returned, last).astype(F32)
    grad_outcome = BRANCH * grad_result
    rounded_outcome = narrow(grad_outcome)
    normed_two, inverse_two, ready_two, hidden, slope = kept_feed
    span = count * part

    def by_slot(value):
        return [value[slot * part : (slot + 1) * part] for slot in range(count)]

    def steps_of(parts):
        state = [parts[1 % count]]

        def start():
            state.append(ring(state[-1]))
            return state[-1]

        def finish(arrived, step):
            state.append(wide_add(arrived, parts[(step + 1) % count]))
            return state[-1]

        return start, finish

    send = narrow(tn(hidden[1], rounded_outcome))
    arrived = swap(send, "core")
    keep = tn(hidden[0], tie(rounded_outcome, send))
    reduce_sums = wide_add(keep, tie(arrived, keep))
    to_y = reduce_sums[span:]
    to_y = [to_y[part : 3 * part], jnp.concatenate([to_y[3 * part :], to_y[:part]])]
    reduce_y = [swap(value, "y") for value in to_y]
    total, pre_own, pre_other, sums_own, sums_other = feed_back(
        tie(rounded_outcome, reduce_sums, *to_y), feed_weights[2], slope
    )
    pre_other, reduce_y[0] = lax.optimization_barrier((pre_other, reduce_y[0]))
    reduce_keep = by_slot(reduce_sums[:span])
    reduce_parts = [None, *(wide_add(reduce_keep[i + 1], reduce_y[0][i * part : (i + 1) * part]) for i in range(2)), None]
    reduce_start, reduce_finish = steps_of(reduce_parts)
    grad_middle = grad_result + norm_backward(total, normed_two, inverse_two, gain_two[0])
    shared_feed = [total * normed_two, total, grad_outcome]
    send = narrow(tn(tie(pre_other, grad_middle), ready_two))
    arrived = swap(send, "core")
    keep = tn(pre_own, tie(ready_two, send))
    expand_sums = wide_add(keep, tie(arrived, keep))
    expand_parts = [jnp.concatenate(pair) for pair in zip(by_slot(expand_sums[:span]), by_slot(expand_sums[span:]))]
    expand_start, expand_finish = steps_of(expand_parts)
    rounded_attended, grad_qkv, sums_qv, after = attention_backward(
        core, kept_attention, grad_middle, attention_weights, (*expand_parts, *reduce_parts[1:3]),
        (expand_start(), reduce_start(), reduce_y[1]),
    )
    expand_step, reduce_step = expand_finish(after[0], 1), reduce_finish(after[1], 1)
    reduce_parts[3] = wide_add(reduce_keep[3], after[2][:part])
    reduce_parts[0] = wide_add(reduce_keep[0], after[2][part:])
    moving_e, moving_r = expand_start(), reduce_start()
    grad_qkv = lax.optimization_barrier((*grad_qkv, expand_step, reduce_step))[:3]
    mixed, ready_one = kept_attention[4], kept_attention[2]
    left = jnp.stack([*grad_qkv, mixed])
    index = 2 * c + y

    def typed_grad(shift):
        right = jnp.where((index ^ shift) == 3, rounded_attended, ready_one)
        return tn(lax.dynamic_index_in_dim(left, index ^ shift, 0, False), right)

    send = [narrow(typed_grad(shift)) for shift in (3, 2)]
    arrived = [swap(value, "core") for value in send]
    left = tie(left, *send)
    keep = [typed_grad(shift) for shift in (1, 0)]
    moving_e, *keep = lax.optimization_barrier((moving_e, *keep))
    expand_finish(moving_e, 2)
    moving_e = expand_start()
    sums = [wide_add(a, b) for a, b in zip(keep, arrived)]
    to_y, to_keep = by_slot(sums[0]), by_slot(sums[1])
    typed_parts = [None] * count

    def typed_swap(slot):
        return swap(to_y[slot], "y")

    def typed_part(slot, arrived):
        typed_parts[slot] = wide_add(to_keep[slot], arrived)

    moving_y, moving_z = typed_swap(1), typed_swap(2)
    grad_qkv = lax.optimization_barrier((grad_qkv, sums))[0]
    grad_in, shared_attention = attention_input_grad(kept_attention, grad_middle, grad_qkv, attention_weights)
    grad_in = narrow(grad_in)
    shared = jnp.stack([jnp.sum(value, axis=0) for value in shared_attention + shared_feed])
    sums_qv = sums_qv.reshape(2, count, local)
    sums_qv = jnp.concatenate([sums_qv[0], sums_qv[1], jnp.zeros((count, width - 2 * local), F32)], axis=1)[:, None]
    sums_pre = [value.reshape(count, part) for half in (sums_own[0], sums_other[0]) for value in jnp.split(half, 2)]
    sums_pre = quarters(jnp.concatenate(sums_pre, axis=1), 1)
    sums_pre = jnp.concatenate(sums_pre[0] + sums_pre[1], axis=1)[:, None]
    vectors = jnp.concatenate([jnp.broadcast_to(shared, (count,) + shared.shape), sums_qv, sums_pre], axis=1)
    vectors = vectors + swap(vectors, "core")

    moving_y, moving_r, to_y[3], to_y[0] = lax.optimization_barrier((moving_y, moving_r, to_y[3], to_y[0]))
    typed_part(1, moving_y)
    reduce_finish(moving_r, 2)
    typed_start, typed_finish = steps_of(typed_parts)
    moving_t, moving_y, moving_v, moving_r = typed_start(), typed_swap(3), swap(vectors, "y"), reduce_start()
    moving_t, moving_z, moving_v, moving_e = lax.optimization_barrier((moving_t, moving_z, moving_v, moving_e))
    vectors = vectors + moving_v
    typed_part(2, moving_z)
    typed_finish(moving_t, 1)
    expand_total = expand_finish(moving_e, 3).reshape(2, part, width)
    moving_t, moving_z, moving_v = typed_start(), typed_swap(0), ring(vectors[1])
    moving_t, moving_y, moving_v, moving_r = lax.optimization_barrier((moving_t, moving_y, moving_v, moving_r))
    reduce_total = over_groups(reduce_finish(moving_r, 3))
    typed_part(3, moving_y)
    typed_finish(moving_t, 2)
    moving_v = ring(moving_v + vectors[2])
    moving_t, reduce_other, expand_other = typed_start(), swap(reduce_total, "y"), swap(expand_total, "y")
    moving_t, moving_z, moving_v, reduce_other, grad_in = lax.optimization_barrier(
        (moving_t, moving_z, moving_v, reduce_other, grad_in)
    )
    typed_part(0, moving_z)
    typed_total = over_groups(typed_finish(moving_t, 3))
    moving_v = ring(moving_v + vectors[3])
    typed_other = swap(typed_total, "y")
    input_grad = give_back(grad_in[:block], grad_in[block:], 0)
    typed_other, expand_other, moving_v = lax.optimization_barrier((typed_other, expand_other, moving_v))
    vectors = over_groups(moving_v + vectors[0])
    def gathered(pair):
        pair = jnp.concatenate(pair)
        blocks = quarters(jnp.concatenate([pair, swap(pair, "core")]), 0)
        return jnp.concatenate(blocks[0] + blocks[1])

    pair = jnp.concatenate([typed_total, typed_other])
    pair_other = swap(pair, "core")
    grad_expand = [over_groups(wide_add(expand_total[i], expand_other[1 - i])) for i in range(2)]
    grad_expand = gathered(grad_expand).T.astype(F32)
    grad_reduce = gathered([reduce_total, reduce_other]).astype(F32)
    whole = relative([pair[:local], pair[local:], pair_other[:local], pair_other[local:]])
    whole = [*whole[0], *whole[1]]
    grad_attend_in = jnp.stack(whole[:3]).transpose(2, 0, 1).astype(F32)
    grad_attend_out = whole[3].astype(F32)
    return (
        outputs[None, None],
        input_grad[None, None],
        vectors[0][None],
        vectors[1][None],
        grad_attend_in[None],
        vectors[6, : 2 * local].reshape(1, 2, local),
        grad_attend_out[None],
        vectors[2][None],
        vectors[3][None],
        vectors[4][None],
        grad_expand[None],
        vectors[7, :units][None],
        grad_reduce[None],
        vectors[5][None],
    )


def solution(mesh):
    pipe, groups, count = mesh.devices.shape
    split = Mesh(mesh.devices.reshape(pipe, groups // 4, 2, 2, count), ("pipe", "outer", "y", "core", "tensor"))
    dp = ("outer", "y", "core")
    rows = P("pipe", dp, "tensor", None)
    vector = P("pipe", None)
    placed = (
        rows,
        rows,
        vector,
        vector,
        P("pipe", None, None, "tensor"),
        P("pipe", None, "tensor"),
        P("pipe", "tensor", None),
        vector,
        vector,
        vector,
        P("pipe", None, "tensor"),
        P("pipe", "tensor"),
        P("pipe", "tensor", None),
        vector,
    )
    return jax.shard_map(shards, mesh=split, in_specs=placed, out_specs=(rows, rows) + placed[2:], check_vma=False)
```

```python
import functools

import jax
import jax.numpy as jnp
import numpy as np
from jax import lax
from jax.experimental import pallas as pl
from jax.experimental.pallas import tpu as pltpu
from jax.sharding import Mesh
from jax.sharding import PartitionSpec as P

HEAD = 64
DEPTH = 12
BRANCH = DEPTH ** (-0.5)
EPSILON = 1e-05
NEGATIVE = -1e30
LANES = 128
AXES = ("pipe", "y", "core", "tensor")
F32 = jnp.float32
BF16 = jnp.bfloat16


def ring_order(count):
    return list(range(0, count, 2)) + list(range(1, count, 2))[::-1]


def ring(value):
    order = ring_order(lax.axis_size("tensor"))
    return lax.ppermute(value, "tensor", list(zip(order, order[1:] + order[:1])))


def swap(value, axis):
    return lax.ppermute(value, axis, [(0, 1), (1, 0)])


def along_pipe(value, by):
    return lax.ppermute(value, "pipe", [(0, 1)] if by > 0 else [(1, 0)])


def routes(section, large):
    count = lax.axis_size("tensor")

    def index(x, y, c, z):
        return ((x * 2 + y) * 2 + c) * count + z

    pairs = []
    for micro in range(2):
        for y in range(2):
            for c in range(2):
                for core in range(2):
                    block = 3 - core if large else core
                    place = micro if section is None else section
                    pairs.append((index(micro, y, c, block), index(place, y, core, 2 * c + micro)))
    return pairs


def fetch(block, section):
    return [lax.ppermute(block, AXES, routes(section, large)) for large in (False, True)]


def give_back(small, large, section):
    pieces = []
    for rows, is_large in ((small, False), (large, True)):
        pairs = [(b, a) for a, b in routes(section, is_large)]
        pieces.append(lax.ppermute(rows, AXES, pairs))
    return jnp.where(lax.axis_index("tensor") < 2, pieces[0], pieces[1])


def nt(left, right):
    return lax.dot_general(left, right, (((1,), (1,)), ((), ())), preferred_element_type=F32)


def tn(left, right):
    return lax.dot_general(left, right, (((0,), (0,)), ((), ())), preferred_element_type=F32)


def nn(left, right):
    return lax.dot_general(left, right, (((1,), (0,)), ((), ())), preferred_element_type=F32)


def estimate(flops, size):
    return pl.CostEstimate(flops=flops, bytes_accessed=size, transcendentals=0)


def head_mask(rows, head):
    lanes = lax.broadcasted_iota(jnp.int32, (rows, LANES), 1)
    return (lanes >= head * HEAD) & (lanes < (head + 1) * HEAD)


def only(mask, value, factor=1.0):
    return jnp.where(mask, value.astype(F32) * factor, 0.0).astype(BF16)


def turned(value):
    return value.astype(F32).T.astype(BF16)


def attend_kernel(keep_weights, core_ref, *refs):
    @pl.when(core_ref[1] == 1)
    def _():
        attend_pair(keep_weights, core_ref, *refs)


def attend_pair(keep_weights, core_ref, q_ref, k_ref, v_ref, ko_ref, vo_ref, o_ref, *kept_refs):
    rows = q_ref.shape[0] // 2
    second = core_ref[0] == 1
    keys = lax.broadcasted_iota(jnp.int32, (rows, rows), 0)
    places = lax.broadcasted_iota(jnp.int32, (rows, rows), 1)
    allowed = keys <= places
    factor = HEAD ** (-0.5)
    small = pl.ds(0, rows)
    large = pl.ds(rows, rows)

    def fifth(ref):
        return jnp.where(second, ref[small, :].astype(F32), ref[large, :].astype(F32)).astype(BF16)

    k5, q5 = fifth(ko_ref), fifth(q_ref)
    vs, vl, v4, v5 = turned(v_ref[small, :]), turned(v_ref[large, :]), turned(vo_ref[small, :]), turned(fifth(vo_ref))
    small_parts, large_parts, scales = [], [], []
    for head in range(LANES // HEAD):
        mask = head_mask(rows, head)
        lanes = slice(head * HEAD, (head + 1) * HEAD)
        qs, ql, qf = (only(mask, value, factor) for value in (q_ref[small, :], q_ref[large, :], q5))
        s1 = jnp.where(allowed, nt(k_ref[small, :], qs), NEGATIVE)
        s2 = nt(k_ref[small, :], ql)
        s3 = jnp.where(allowed, nt(k_ref[large, :], ql), NEGATIVE)
        s4 = nt(ko_ref[small, :], ql)
        s5 = nt(k5, qf)

        def peak(value):
            return jnp.max(value, axis=0, keepdims=True)

        def total(value):
            return jnp.sum(value, axis=0, keepdims=True)

        m5 = peak(s5)
        ms = peak(s1)
        ml = jnp.maximum(jnp.maximum(peak(s2), peak(s3)), peak(s4))
        ms = jnp.where(second, jnp.maximum(ms, m5), ms)
        ml = jnp.where(second, ml, jnp.maximum(ml, m5))
        mf = jnp.where(second, ms, ml)
        e1 = jnp.exp(s1 - ms)
        e2 = jnp.exp(s2 - ml)
        e3 = jnp.exp(s3 - ml)
        e4 = jnp.exp(s4 - ml)
        e5 = jnp.exp(s5 - mf)
        t5 = total(e5)
        rs = total(e1)
        rl = total(e2) + total(e3) + total(e4)
        rs = 1.0 / jnp.where(second, rs + t5, rs)
        rl = 1.0 / jnp.where(second, rl, rl + t5)
        e1, e2, e3, e4, e5 = (value.astype(BF16) for value in (e1, e2, e3, e4, e5))
        if keep_weights:
            for place, value in enumerate((e1, e2, e3, e4, e5)):
                kept_refs[0][head, place] = value
            scales.append(jnp.concatenate([rs, rl], axis=1))
        o5 = nn(v5[lanes], e5)
        small_parts.append((nn(vs[lanes], e1) + jnp.where(second, o5, 0.0)) * rs)
        large_parts.append(
            (nn(vs[lanes], e2) + nn(vl[lanes], e3) + nn(v4[lanes], e4) + jnp.where(second, 0.0, o5)) * rl
        )
    o_ref[small, :] = jnp.concatenate(small_parts).T.astype(BF16)
    o_ref[large, :] = jnp.concatenate(large_parts).T.astype(BF16)
    if keep_weights:
        row = lax.broadcasted_iota(jnp.int32, (8, 2 * rows), 0)
        kept_refs[1][...] = jnp.where(row == 0, scales[0], scales[1])


def attend_back_kernel(
    core_ref, q_ref, k_ref, v_ref, ko_ref, vo_ref, go_ref, o_ref, e_ref, scale_ref, gq_ref, own_ref, other_ref, sums_ref
):
    rows = q_ref.shape[0] // 2
    second = core_ref[0] == 1
    factor = HEAD ** (-0.5)
    small = pl.ds(0, rows)
    large = pl.ds(rows, rows)

    def fifth(first, last):
        return jnp.where(second, first.astype(F32), last.astype(F32)).astype(BF16)

    row = lax.broadcasted_iota(jnp.int32, (LANES, 2 * rows), 0)
    scale = jnp.where(row < HEAD, scale_ref[0:1, :], scale_ref[1:2, :]).T
    grads = (go_ref[...].astype(F32) * scale).astype(BF16)
    product = grads.astype(F32) * o_ref[...].astype(F32)
    high = product.astype(BF16)
    low = (product - high.astype(F32)).astype(BF16)
    g_small, g_large = grads[:rows], grads[rows:]
    g5 = fifth(g_small, g_large)
    q5 = fifth(q_ref[small, :], q_ref[large, :])
    v5 = fifth(vo_ref[small, :], vo_ref[large, :])
    ks, kl, k4, k5 = (
        turned(k_ref[small, :]), turned(k_ref[large, :]), turned(ko_ref[small, :]),
        turned(fifth(ko_ref[small, :], ko_ref[large, :])),
    )
    totals = {}
    gq_small, gq_large = [], []

    def add(name, value):
        totals[name] = value if name not in totals else totals[name] + value

    for head in range(LANES // HEAD):
        mask = head_mask(rows, head)
        lanes = slice(head * HEAD, (head + 1) * HEAD)
        ones = jnp.where(head_mask(16, head), 1.0, 0.0).astype(BF16)
        inner = (nt(ones, high) + nt(ones, low))[0:1]
        ds_, dl_ = inner[:, :rows], inner[:, rows:]
        df_ = jnp.where(second, ds_, dl_)
        qs, ql, qf = (only(mask, value, factor) for value in (q_ref[small, :], q_ref[large, :], q5))
        gs, gl, gf = (only(mask, value) for value in (g_small, g_large, g5))

        def score_grad(place, values, rows_grad, shift):
            return (e_ref[head, place].astype(F32) * (nt(values, rows_grad) - shift)).astype(BF16)

        z1 = score_grad(0, v_ref[small, :], gs, ds_)
        z2 = score_grad(1, v_ref[small, :], gl, dl_)
        z3 = score_grad(2, v_ref[large, :], gl, dl_)
        z4 = score_grad(3, vo_ref[small, :], gl, dl_)
        z5 = score_grad(4, v5, gf, df_)
        gq5 = nn(k5[lanes], z5)
        gq_small.append(nn(ks[lanes], z1) + jnp.where(second, gq5, 0.0))
        gq_large.append(nn(ks[lanes], z2) + nn(kl[lanes], z3) + nn(k4[lanes], z4) + jnp.where(second, 0.0, gq5))
        add("ks", nn(z1, qs) + nn(z2, ql))
        add("kl", nn(z3, ql))
        add("k4", nn(z4, ql))
        add("k5", nn(z5, qf))
        add("vs", nn(e_ref[head, 0], gs) + nn(e_ref[head, 1], gl))
        add("vl", nn(e_ref[head, 2], gl))
        add("v4", nn(e_ref[head, 3], gl))
        add("v5", nn(e_ref[head, 4], gf))
    gqs, gql = jnp.concatenate(gq_small).T * factor, jnp.concatenate(gq_large).T * factor
    gq_ref[small, :] = gqs.astype(BF16)
    gq_ref[large, :] = gql.astype(BF16)
    for place, name in enumerate("kv"):
        own_ref[place, small, :] = totals[name + "s"]
        own_ref[place, large, :] = totals[name + "l"]
        four, five = totals[name + "4"], totals[name + "5"]
        other_ref[place, small, :] = (four + jnp.where(second, five, 0.0)).astype(BF16)
        other_ref[place, large, :] = jnp.where(second, 0.0, five).astype(BF16)
    sum_q = jnp.sum(gqs, axis=0, keepdims=True) + jnp.sum(gql, axis=0, keepdims=True)
    sum_v = jnp.sum(totals["vs"] + totals["vl"] + totals["v4"] + totals["v5"], axis=0, keepdims=True)
    row = lax.broadcasted_iota(jnp.int32, (8, LANES), 0)
    sums_ref[...] = jnp.where(row == 0, sum_q, jnp.where(row == 1, sum_v, 0.0))


def attend(core, q, k, v, k_other, v_other, keep_weights):
    length, width = q.shape
    rows = length // 2
    pairs = width // LANES
    column = pl.BlockSpec((length, LANES), lambda i: (0, i))
    shapes = [jax.ShapeDtypeStruct((length, width), BF16)]
    outs = [column]
    if keep_weights:
        shapes.append(pltpu.HBM((width // HEAD, 5, rows, rows), BF16))
        shapes.append(jax.ShapeDtypeStruct((8 * pairs, length), F32))
        outs.append(pl.BlockSpec((2, 5, rows, rows), lambda i: (i, 0, 0, 0)))
        outs.append(pl.BlockSpec((8, length), lambda i: (i, 0)))
    return pl.pallas_call(
        functools.partial(attend_pair if keep_weights else attend_kernel, keep_weights),
        grid=(pairs,),
        out_shape=shapes,
        in_specs=[pl.BlockSpec(memory_space=pltpu.SMEM)] + [column] * 5,
        out_specs=outs,
        compiler_params=pltpu.CompilerParams(vmem_limit_bytes=40 * 1024 * 1024),
        cost_estimate=estimate(20 * rows * rows * width * 2, 16 * length * width),
        name="attend",
    )(core, q, k, v, k_other, v_other)


def attend_back(core, q, k, v, k_other, v_other, grad_mixed, mixed, weights, scales):
    length, width = q.shape
    rows = length // 2
    column = pl.BlockSpec((length, LANES), lambda i: (0, i))
    double = pl.BlockSpec((2, length, LANES), lambda i: (0, 0, i))
    return pl.pallas_call(
        attend_back_kernel,
        grid=(width // LANES,),
        out_shape=[
            jax.ShapeDtypeStruct((length, width), BF16),
            jax.ShapeDtypeStruct((2, length, width), F32),
            jax.ShapeDtypeStruct((2, length, width), BF16),
            jax.ShapeDtypeStruct((8, width), F32),
        ],
        in_specs=[pl.BlockSpec(memory_space=pltpu.SMEM)]
        + [column] * 7
        + [pl.BlockSpec((2, 5, rows, rows), lambda i: (i, 0, 0, 0)), pl.BlockSpec((8, length), lambda i: (i, 0))],
        out_specs=[column, double, double, pl.BlockSpec((8, LANES), lambda i: (0, i))],
        compiler_params=pltpu.CompilerParams(vmem_limit_bytes=40 * 1024 * 1024),
        cost_estimate=estimate(40 * rows * rows * width * 2, 40 * length * width),
        name="attend_back",
    )(core, q, k, v, k_other, v_other, grad_mixed, mixed, weights, scales)


def gelu_and_slope(values):
    root = float(np.sqrt(2 / np.pi))
    cubic = 0.044715 * root
    square = values * values
    bend = jnp.tanh(values * (root + cubic * square))
    half = 0.5 + 0.5 * bend
    gate = values * half
    slope = half + gate * ((1.0 - bend) * (root + (3 * cubic) * square))
    return (gate, slope)


def expand_kernel(core_ref, rows_ref, expand_ref, bias_ref, reduce_ref, start_ref, total_ref):
    @pl.when(core_ref[1] == 1)
    def _():
        gate, _ = gelu_and_slope(nt(rows_ref[...], expand_ref[...]) + bias_ref[...])
        total_ref[...] = start_ref[...] + nn(gate.astype(BF16), reduce_ref[...])


def feed_half(core, rows, expand_w, bias, reduce_w, start, row_part=None):
    length, width = rows.shape
    units = expand_w.shape[0]
    if row_part is not None:
        length = length // 2
    place = row_part or 0
    whole = pl.BlockSpec((length, width), lambda i: (0, 0))
    taken = pl.BlockSpec((length, width), lambda i: (place, 0))
    start_place = 0 if start.shape[0] == length else place
    begun = pl.BlockSpec((length, width), lambda i: (start_place, 0))
    weight = pl.BlockSpec((units, width), lambda i: (0, 0))
    return pl.pallas_call(
        expand_kernel,
        grid=(1,),
        out_shape=jax.ShapeDtypeStruct((length, width), F32),
        in_specs=[
            pl.BlockSpec(memory_space=pltpu.SMEM),
            taken, weight, pl.BlockSpec((1, units), lambda i: (0, 0)), weight, begun,
        ],
        out_specs=whole,
        compiler_params=pltpu.CompilerParams(vmem_limit_bytes=40 * 1024 * 1024),
        cost_estimate=estimate(4 * length * width * units, 4 * width * units),
        name="feed_half",
    )(core, rows, expand_w, bias.reshape(1, units), reduce_w, start)


def both_kernel(
    steps, rows_ref, grad_ref, e0_ref, e1_ref, b0_ref, b1_ref, r0_ref, r1_ref,
    total_ref, grad_total_ref, h0_ref, h1_ref, s0_ref, s1_ref,
):
    place = pl.program_id(0)

    @pl.when(place == 0)
    def _():
        total_ref[...] = jnp.zeros_like(total_ref)
        grad_total_ref[...] = jnp.zeros_like(grad_total_ref)

    def tile(expand_ref, bias_ref, reduce_ref, hidden_ref, slope_ref):
        gate, slope = gelu_and_slope(nt(rows_ref[...], expand_ref[...]) + bias_ref[...])
        hidden = gate.astype(BF16)
        slope = slope.astype(BF16)
        hidden_ref[...] = hidden
        slope_ref[...] = slope
        total_ref[...] += nn(hidden, reduce_ref[...])
        pre = nt(grad_ref[...], reduce_ref[...]) * slope.astype(F32)
        grad_total_ref[...] += nn(pre.astype(BF16), expand_ref[...])

    @pl.when(place < steps)
    def _():
        tile(e0_ref, b0_ref, r0_ref, h0_ref, s0_ref)

    @pl.when(place >= steps)
    def _():
        tile(e1_ref, b1_ref, r1_ref, h1_ref, s1_ref)


def back_kernel(
    steps, grad_ref, e0_ref, e1_ref, r0_ref, r1_ref, s0_ref, s1_ref,
    total_ref, p0_ref, p1_ref, sums0_ref, sums1_ref,
):
    place = pl.program_id(0)

    @pl.when(place == 0)
    def _():
        total_ref[...] = jnp.zeros_like(total_ref)

    def tile(expand_ref, reduce_ref, slope_ref, pre_ref, sums_ref):
        pre = nt(grad_ref[...], reduce_ref[...]) * slope_ref[...].astype(F32)
        sums_ref[...] = jnp.broadcast_to(jnp.sum(pre, axis=0, keepdims=True), sums_ref.shape)
        rounded = pre.astype(BF16)
        pre_ref[...] = rounded
        total_ref[...] += nn(rounded, expand_ref[...])

    @pl.when(place < steps)
    def _():
        tile(e0_ref, r0_ref, s0_ref, p0_ref, sums0_ref)

    @pl.when(place >= steps)
    def _():
        tile(e1_ref, r1_ref, s1_ref, p1_ref, sums1_ref)


def feed_specs(length, width, units, steps):
    tile = units // steps
    whole = pl.BlockSpec((length, width), lambda i: (0, 0))

    def early(i):
        return jnp.minimum(i, steps - 1)

    def late(i):
        return jnp.maximum(i - steps, 0)

    weight = [pl.BlockSpec((tile, width), lambda i, f=f: (f(i), 0)) for f in (early, late)]
    across = [pl.BlockSpec((length, tile), lambda i, f=f: (0, f(i))) for f in (early, late)]
    row = [pl.BlockSpec((1, tile), lambda i, f=f: (0, f(i))) for f in (early, late)]
    rows = [pl.BlockSpec((8, tile), lambda i, f=f: (0, f(i))) for f in (early, late)]
    return steps, whole, weight, across, row, rows


def feed_both(rows, grad, halves):
    length, width = rows.shape
    units = halves[0][0].shape[0]
    steps, whole, weight, across, row, _ = feed_specs(length, width, units, 2)
    total = jax.ShapeDtypeStruct((length, width), F32)
    kept = jax.ShapeDtypeStruct((length, units), BF16)
    (e0, b0, r0), (e1, b1, r1) = halves
    return pl.pallas_call(
        functools.partial(both_kernel, steps),
        grid=(2 * steps,),
        out_shape=[total, total, kept, kept, kept, kept],
        in_specs=[whole, whole, *weight, *row, *weight],
        out_specs=[whole, whole, *across, *across],
        compiler_params=pltpu.CompilerParams(vmem_limit_bytes=40 * 1024 * 1024),
        cost_estimate=estimate(16 * length * width * units, 8 * width * units),
        name="feed_both",
    )(rows, grad, e0, e1, b0.reshape(1, units), b1.reshape(1, units), r0, r1)


def feed_back(grad, halves, slope):
    length, width = grad.shape
    units = halves[0][0].shape[0]
    steps, whole, weight, across, _, rows = feed_specs(length, width, units, 1)
    kept = jax.ShapeDtypeStruct((length, units), BF16)
    sums = jax.ShapeDtypeStruct((8, units), F32)
    (e0, _, r0), (e1, _, r1) = halves
    return pl.pallas_call(
        functools.partial(back_kernel, steps),
        grid=(2 * steps,),
        out_shape=[jax.ShapeDtypeStruct((length, width), F32), kept, kept, sums, sums],
        in_specs=[whole, *weight, *weight, *across],
        out_specs=[whole, *across, *rows],
        compiler_params=pltpu.CompilerParams(vmem_limit_bytes=40 * 1024 * 1024),
        cost_estimate=estimate(8 * length * width * units, 8 * width * units),
        name="feed_back",
    )(grad, e0, e1, r0, r1, *slope)


def tie(value, *others):
    return lax.optimization_barrier((value, *others))[0]


def normalize_rows(rows):
    centred = rows - jnp.mean(rows, axis=-1, keepdims=True)
    inverse = lax.rsqrt(jnp.mean(centred * centred, axis=-1, keepdims=True) + EPSILON)
    return (centred * inverse, inverse)


def norm_backward(grad_normed, normed, inverse, gain):
    scaled = grad_normed * gain
    centred = scaled - jnp.mean(scaled, axis=-1, keepdims=True)
    return inverse * (centred - normed * jnp.mean(scaled * normed, axis=-1, keepdims=True))


def attention_forward(core, rows_in, weights, keep, before=(), after=()):
    gain_a, shift_a, proj, bias_q, bias_v, bias_out = weights
    normed_one, inverse_one = normalize_rows(rows_in)
    ready_one = narrow(normed_one * gain_a + shift_a)
    k = narrow(nt(ready_one, proj[1]))
    k_other = swap(k, "core")
    v = narrow(nt(ready_one, proj[2]) + bias_v)
    v_other = swap(v, "core")
    q = narrow(nt(ready_one, proj[0]) + bias_q)
    if before:
        q, proj_out, *before = lax.optimization_barrier((q, proj[3], *before))
        proj = [*proj[:3], proj_out]
        after = after(before)
    mixed, *kept_weights = attend(core, q, k, v, k_other, v_other, keep)
    mixed, *after = lax.optimization_barrier((mixed, *after))
    middle = rows_in + BRANCH * (nn(mixed, proj[3]) + bias_out)
    kept = (normed_one, inverse_one, ready_one, (q, k, v, k_other, v_other), mixed, *kept_weights)
    return middle, kept, after


def feed_start(middle, weights):
    gain_b, shift_b, _, _ = weights
    normed_two, inverse_two = normalize_rows(middle)
    return normed_two, inverse_two, narrow(normed_two * gain_b + shift_b)


def feed_forward_only(core, middle, weights):
    ready_two = feed_start(middle, weights)[2]
    first, second = weights[2]
    block = middle.shape[0] // 2
    total = jnp.broadcast_to(weights[3], (block, middle.shape[1]))
    totals = [feed_half(core, ready_two, *first, total, 0)]
    results = []
    for part in range(2):
        rows = slice(part * block, (part + 1) * block)
        if part:
            totals.append(feed_half(core, ready_two, *first, tie(total, *results), part))
        piece = feed_half(core, ready_two, *second, totals[part], part)
        results.append(narrow(middle[rows] + BRANCH * piece))
    return results


def feed_forward_and_back(middle, grad_result, weights):
    normed_two, inverse_two, ready_two = feed_start(middle, weights)
    rounded = narrow(BRANCH * grad_result)
    total, grad_total, *kept = feed_both(ready_two, rounded, weights[2])
    result = narrow(middle + BRANCH * (total + weights[3]))
    grad_middle = grad_result + norm_backward(grad_total, normed_two, inverse_two, weights[0])
    return result, grad_middle, (normed_two, inverse_two, ready_two, kept[:2], kept[2:])


def attention_backward(core, kept, grad_middle, weights, before=(), after=()):
    _, _, _, projected, mixed, *attention = kept
    rounded_attended = narrow(BRANCH * grad_middle)
    grad_mixed = narrow(nt(tie(rounded_attended, *before), weights[2][3]))
    grad_q, own, other, sums = attend_back(core, *projected, grad_mixed, mixed, *attention)
    other, *after = lax.optimization_barrier((other, *after))
    grad_kv = narrow(own + swap(other, "core").astype(F32))
    return rounded_attended, (grad_q, grad_kv[0], grad_kv[1]), sums[:2], after


def attention_input_grad(kept, grad_middle, grad_qkv, weights):
    gain_a, _, proj, _, _, _ = weights
    normed_one, inverse_one, *_ = kept
    grad_normed_one = sum(nn(grad, part) for grad, part in zip(grad_qkv, proj))
    grad_in = grad_middle + norm_backward(grad_normed_one, normed_one, inverse_one, gain_a)
    return grad_in, [grad_normed_one * normed_one, grad_normed_one, BRANCH * grad_middle]


def narrow(value):
    return value.astype(BF16)


def wide_add(left, right):
    return narrow(left.astype(F32) + right.astype(F32))


def over_groups(value):
    return lax.psum(value, "outer") if lax.axis_size("outer") > 1 else value


def ring_add(parts):
    count = len(parts)
    total = parts[1 % count]
    for step in range(1, count):
        total = wide_add(ring(total), parts[(step + 1) % count])
    return total


def thirds(values):
    pieces = []
    for _ in range(3):
        piece = lax.reduce_precision(values, 8, 7)
        pieces.append(narrow(piece))
        values = values - piece
    return jnp.stack(pieces)


def shards(
    inputs, cotangent, gain_one, shift_one, attend_in, attend_bias, attend_out, out_bias,
    gain_two, shift_two, expand_in, expand_bias, reduce_out, reduce_bias,
):
    count = lax.axis_size("tensor")
    x, y, c, z = (lax.axis_index(axis) for axis in AXES)
    is_first = x == 0
    core = jnp.stack([c, jnp.ones_like(c)]).astype(jnp.int32)
    core_a = jnp.stack([c, 1 - x]).astype(jnp.int32)
    width = attend_in.shape[1]
    local = attend_in.shape[3]
    units = expand_in.shape[2]
    part = units // 4
    spare = 16

    def either(index, pair):
        first, second = pair
        return jnp.where(index == 0, first, second), jnp.where(index == 0, second, first)

    def relative(blocks):
        rows = [either(y, blocks[:2]), either(y, blocks[2:])]
        return list(zip(*(either(c, pair) for pair in zip(*rows))))

    def quarters(value, axis):
        return relative(jnp.split(value, 4, axis))

    typed = [*attend_in[0].transpose(1, 2, 0), attend_out[0]]
    (mine, mine_y), _ = relative(typed)
    biases = thirds(jnp.concatenate([attend_bias[0].reshape(2 * local), expand_bias[0]])).reshape(-1)
    biases = jnp.pad(biases, (0, spare * width - biases.size)).reshape(spare, width)
    piece = jnp.concatenate([mine, biases])
    bias_rows = [biases]
    own_parts = [quarters(expand_in[0].T, 0), quarters(reduce_out[0], 0)]
    feed = [jnp.concatenate([value[0][0] for value in own_parts])]
    feed_y = [jnp.concatenate([value[0][1] for value in own_parts])]
    pieces, pieces_y = [ring(piece)], []
    arrived = fetch(inputs[0, 0], None)
    while len(pieces) < count - 1:
        pieces_y.append(swap(pieces[-1][:local], "y"))
        pieces.append(ring(pieces[-1]))
        if len(pieces) < count - 1:
            pieces[-1], pieces_y[-1], feed[0], *arrived = lax.optimization_barrier(
                (pieces[-1], pieces_y[-1], feed[0], *arrived)
            )
    feed.append(ring(feed[0]))
    passed = [along_pipe(rows, -1) for rows in arrived]
    pieces[-1], pieces_y[-1] = lax.optimization_barrier((pieces[-1], pieces_y[-1]))
    pieces_y.append(swap(pieces[-1][:local], "y"))
    feed[1], pieces_y[-1], *passed = lax.optimization_barrier((feed[1], pieces_y[-1], *passed))
    arrived = [jnp.where(z % 2 == 0, here, there) for here, there in zip(arrived, passed)]
    feed_y.append(swap(feed[1], "y"))
    feed.append(ring(feed[1]))
    feed[2], feed_y[1] = lax.optimization_barrier((feed[2], feed_y[1]))
    feed_y.append(swap(feed[2], "y"))
    before = (ring(feed[2]), feed_y[2])
    bias_rows += [value[local:] for value in pieces]
    pieces = [mine] + [value[:local] for value in pieces]
    pieces_y = [mine_y] + pieces_y
    pieces = jnp.concatenate(pieces)
    pieces_y = jnp.concatenate(pieces_y)
    proj = relative([pieces, pieces_y, swap(pieces, "core"), swap(pieces_y, "core")])
    proj = [*proj[0], *proj[1]]
    biases = jnp.stack(bias_rows).reshape(count, -1)[:, : 3 * (2 * local + units)].reshape(count, 3, 2 * local + units)
    biases = biases.astype(F32)
    biases = biases[:, 0] + (biases[:, 1] + biases[:, 2])
    bias_q, bias_v = biases[:, :local].reshape(width), biases[:, local : 2 * local].reshape(width)
    expand_b = quarters(biases[:, 2 * local :], 1)
    expand_b = [jnp.concatenate([value.reshape(count * part) for value in pair]) for pair in expand_b]
    attention_weights = (gain_one[0], shift_one[0], proj, bias_q, bias_v, out_bias[0])

    rows_in = jnp.concatenate(arrived)
    middle, _, after = attention_forward(
        core_a, rows_in.astype(F32), attention_weights, False, before,
        lambda ready: (*ready, swap(ready[0], "y")),
    )
    feed.append(after[0])
    feed_y[2:] = after[1:]
    own_half = [
        jnp.concatenate([value[kind * part : (kind + 1) * part] for value in feed + feed_y]) for kind in range(2)
    ]
    other_half = [swap(value, "core") for value in own_half]
    feed_weights = (
        gain_two[0],
        shift_two[0],
        [(own_half[0], expand_b[0], own_half[1]), (other_half[0], expand_b[1], other_half[1])],
        reduce_bias[0],
    )
    passed = jnp.concatenate([along_pipe(rows, 1) for rows in feed_forward_only(core_a, middle, feed_weights)])
    last = fetch(tie(cotangent[0, 0], passed), 1)
    rows_in = jnp.where(is_first, rows_in, passed)
    middle, kept_attention, last = attention_forward(
        core, rows_in.astype(F32), attention_weights, True, (), last
    )
    last = jnp.concatenate(last)
    result, grad_middle, kept_feed = feed_forward_and_back(middle, last.astype(F32), feed_weights)
    block = result.shape[0] // 2
    outputs = give_back(result[:block], result[block:], 1)
    _, grad_qkv, _, (outputs,) = attention_backward(
        core, kept_attention, grad_middle, attention_weights, (), (outputs,)
    )
    grad_in = narrow(attention_input_grad(kept_attention, grad_middle, grad_qkv, attention_weights)[0])
    returned = jnp.concatenate([along_pipe(grad_in[:block], -1), along_pipe(grad_in[block:], -1)])
    grad_result = jnp.where(is_first, returned, last).astype(F32)
    grad_outcome = BRANCH * grad_result
    rounded_outcome = narrow(grad_outcome)
    normed_two, inverse_two, ready_two, hidden, slope = kept_feed
    span = count * part

    def by_slot(value):
        return [value[slot * part : (slot + 1) * part] for slot in range(count)]

    def steps_of(parts):
        state = [parts[1 % count]]

        def start():
            state.append(ring(state[-1]))
            return state[-1]

        def finish(arrived, step):
            state.append(wide_add(arrived, parts[(step + 1) % count]))
            return state[-1]

        return start, finish

    send = narrow(tn(hidden[1], rounded_outcome))
    arrived = swap(send, "core")
    keep = tn(hidden[0], tie(rounded_outcome, send))
    reduce_sums = wide_add(keep, tie(arrived, keep))
    to_y = reduce_sums[span:]
    to_y = [to_y[part : 3 * part], jnp.concatenate([to_y[3 * part :], to_y[:part]])]
    reduce_y = [swap(value, "y") for value in to_y]
    total, pre_own, pre_other, sums_own, sums_other = feed_back(
        tie(rounded_outcome, reduce_sums, *to_y), feed_weights[2], slope
    )
    pre_other, reduce_y[0] = lax.optimization_barrier((pre_other, reduce_y[0]))
    reduce_keep = by_slot(reduce_sums[:span])
    reduce_parts = [None, *(wide_add(reduce_keep[i + 1], reduce_y[0][i * part : (i + 1) * part]) for i in range(2)), None]
    reduce_start, reduce_finish = steps_of(reduce_parts)
    grad_middle = grad_result + norm_backward(total, normed_two, inverse_two, gain_two[0])
    shared_feed = [total * normed_two, total, grad_outcome]
    send = narrow(tn(tie(pre_other, grad_middle), ready_two))
    arrived = swap(send, "core")
    keep = tn(pre_own, tie(ready_two, send))
    expand_sums = wide_add(keep, tie(arrived, keep))
    expand_parts = [jnp.concatenate(pair) for pair in zip(by_slot(expand_sums[:span]), by_slot(expand_sums[span:]))]
    expand_start, expand_finish = steps_of(expand_parts)
    rounded_attended, grad_qkv, sums_qv, after = attention_backward(
        core, kept_attention, grad_middle, attention_weights, (*expand_parts, *reduce_parts[1:3]),
        (expand_start(), reduce_start(), reduce_y[1]),
    )
    expand_step, reduce_step = expand_finish(after[0], 1), reduce_finish(after[1], 1)
    reduce_parts[3] = wide_add(reduce_keep[3], after[2][:part])
    reduce_parts[0] = wide_add(reduce_keep[0], after[2][part:])
    moving_e, moving_r = expand_start(), reduce_start()
    grad_qkv = lax.optimization_barrier((*grad_qkv, expand_step, reduce_step))[:3]
    mixed, ready_one = kept_attention[4], kept_attention[2]
    left = jnp.stack([*grad_qkv, mixed])
    index = 2 * c + y

    def typed_grad(shift):
        right = jnp.where((index ^ shift) == 3, rounded_attended, ready_one)
        return tn(lax.dynamic_index_in_dim(left, index ^ shift, 0, False), right)

    send = [narrow(typed_grad(shift)) for shift in (3, 2)]
    arrived = [swap(value, "core") for value in send]
    left = tie(left, *send)
    keep = [typed_grad(shift) for shift in (1, 0)]
    moving_e, *keep = lax.optimization_barrier((moving_e, *keep))
    expand_finish(moving_e, 2)
    moving_e = expand_start()
    sums = [wide_add(a, b) for a, b in zip(keep, arrived)]
    to_y, to_keep = by_slot(sums[0]), by_slot(sums[1])
    typed_parts = [None] * count

    def typed_swap(slot):
        return swap(to_y[slot], "y")

    def typed_part(slot, arrived):
        typed_parts[slot] = wide_add(to_keep[slot], arrived)

    moving_y, moving_z = typed_swap(1), typed_swap(2)
    grad_qkv = lax.optimization_barrier((grad_qkv, sums))[0]
    grad_in, shared_attention = attention_input_grad(kept_attention, grad_middle, grad_qkv, attention_weights)
    grad_in = narrow(grad_in)
    shared = jnp.stack([jnp.sum(value, axis=0) for value in shared_attention + shared_feed])
    sums_qv = sums_qv.reshape(2, count, local)
    sums_qv = jnp.concatenate([sums_qv[0], sums_qv[1], jnp.zeros((count, width - 2 * local), F32)], axis=1)[:, None]
    sums_pre = [value.reshape(count, part) for half in (sums_own[0], sums_other[0]) for value in jnp.split(half, 2)]
    sums_pre = quarters(jnp.concatenate(sums_pre, axis=1), 1)
    sums_pre = jnp.concatenate(sums_pre[0] + sums_pre[1], axis=1)[:, None]
    vectors = jnp.concatenate([jnp.broadcast_to(shared, (count,) + shared.shape), sums_qv, sums_pre], axis=1)
    vectors = vectors + swap(vectors, "core")

    moving_y, moving_r, to_y[3], to_y[0] = lax.optimization_barrier((moving_y, moving_r, to_y[3], to_y[0]))
    typed_part(1, moving_y)
    reduce_finish(moving_r, 2)
    typed_start, typed_finish = steps_of(typed_parts)
    moving_t, moving_y, moving_v, moving_r = typed_start(), typed_swap(3), swap(vectors, "y"), reduce_start()
    moving_t, moving_z, moving_v, moving_e = lax.optimization_barrier((moving_t, moving_z, moving_v, moving_e))
    vectors = vectors + moving_v
    typed_part(2, moving_z)
    typed_finish(moving_t, 1)
    expand_total = expand_finish(moving_e, 3).reshape(2, part, width)
    moving_t, moving_z, moving_v = typed_start(), typed_swap(0), ring(vectors[1])
    moving_t, moving_y, moving_v, moving_r = lax.optimization_barrier((moving_t, moving_y, moving_v, moving_r))
    reduce_total = over_groups(reduce_finish(moving_r, 3))
    typed_part(3, moving_y)
    typed_finish(moving_t, 2)
    moving_v = ring(moving_v + vectors[2])
    moving_t, reduce_other, expand_other = typed_start(), swap(reduce_total, "y"), swap(expand_total, "y")
    moving_t, moving_z, moving_v, reduce_other, grad_in = lax.optimization_barrier(
        (moving_t, moving_z, moving_v, reduce_other, grad_in)
    )
    typed_part(0, moving_z)
    typed_total = over_groups(typed_finish(moving_t, 3))
    moving_v = ring(moving_v + vectors[3])
    typed_other = swap(typed_total, "y")
    input_grad = give_back(grad_in[:block], grad_in[block:], 0)
    typed_other, expand_other, moving_v = lax.optimization_barrier((typed_other, expand_other, moving_v))
    vectors = over_groups(moving_v + vectors[0])
    def gathered(pair):
        pair = jnp.concatenate(pair)
        blocks = quarters(jnp.concatenate([pair, swap(pair, "core")]), 0)
        return jnp.concatenate(blocks[0] + blocks[1])

    pair = jnp.concatenate([typed_total, typed_other])
    pair_other = swap(pair, "core")
    grad_expand = [over_groups(wide_add(expand_total[i], expand_other[1 - i])) for i in range(2)]
    grad_expand = gathered(grad_expand).T.astype(F32)
    grad_reduce = gathered([reduce_total, reduce_other]).astype(F32)
    whole = relative([pair[:local], pair[local:], pair_other[:local], pair_other[local:]])
    whole = [*whole[0], *whole[1]]
    grad_attend_in = jnp.stack(whole[:3]).transpose(2, 0, 1).astype(F32)
    grad_attend_out = whole[3].astype(F32)
    return (
        outputs[None, None],
        input_grad[None, None],
        vectors[0][None],
        vectors[1][None],
        grad_attend_in[None],
        vectors[6, : 2 * local].reshape(1, 2, local),
        grad_attend_out[None],
        vectors[2][None],
        vectors[3][None],
        vectors[4][None],
        grad_expand[None],
        vectors[7, :units][None],
        grad_reduce[None],
        vectors[5][None],
    )


def solution(mesh):
    pipe, groups, count = mesh.devices.shape
    split = Mesh(mesh.devices.reshape(pipe, groups // 4, 2, 2, count), ("pipe", "outer", "y", "core", "tensor"))
    dp = ("outer", "y", "core")
    rows = P("pipe", dp, "tensor", None)
    vector = P("pipe", None)
    placed = (
        rows,
        rows,
        vector,
        vector,
        P("pipe", None, None, "tensor"),
        P("pipe", None, "tensor"),
        P("pipe", "tensor", None),
        vector,
        vector,
        vector,
        P("pipe", None, "tensor"),
        P("pipe", "tensor"),
        P("pipe", "tensor", None),
        vector,
    )
    return jax.shard_map(shards, mesh=split, in_specs=placed, out_specs=(rows, rows) + placed[2:], check_vma=False)
```

```python
import functools

import jax
import jax.numpy as jnp
import numpy as np
from jax import lax
from jax.experimental import pallas as pl
from jax.experimental.pallas import tpu as pltpu
from jax.sharding import Mesh
from jax.sharding import PartitionSpec as P

HEAD = 64
DEPTH = 12
BRANCH = DEPTH ** (-0.5)
EPSILON = 1e-05
NEGATIVE = -1e30
LANES = 128
AXES = ("pipe", "y", "core", "tensor")
F32 = jnp.float32
BF16 = jnp.bfloat16


def ring_order(count):
    return list(range(0, count, 2)) + list(range(1, count, 2))[::-1]


def ring(value):
    order = ring_order(lax.axis_size("tensor"))
    return lax.ppermute(value, "tensor", list(zip(order, order[1:] + order[:1])))


def swap(value, axis):
    return lax.ppermute(value, axis, [(0, 1), (1, 0)])


def along_pipe(value, by):
    return lax.ppermute(value, "pipe", [(0, 1)] if by > 0 else [(1, 0)])


def routes(section, large):
    count = lax.axis_size("tensor")

    def index(x, y, c, z):
        return ((x * 2 + y) * 2 + c) * count + z

    pairs = []
    for micro in range(2):
        for y in range(2):
            for c in range(2):
                for core in range(2):
                    block = 3 - core if large else core
                    place = micro if section is None else section
                    pairs.append((index(micro, y, c, block), index(place, y, core, 2 * c + micro)))
    return pairs


def fetch(block, section):
    return [lax.ppermute(block, AXES, routes(section, large)) for large in (False, True)]


def give_back(small, large, section):
    pieces = []
    for rows, is_large in ((small, False), (large, True)):
        pairs = [(b, a) for a, b in routes(section, is_large)]
        pieces.append(lax.ppermute(rows, AXES, pairs))
    return jnp.where(lax.axis_index("tensor") < 2, pieces[0], pieces[1])


def nt(left, right):
    return lax.dot_general(left, right, (((1,), (1,)), ((), ())), preferred_element_type=F32)


def tn(left, right):
    return lax.dot_general(left, right, (((0,), (0,)), ((), ())), preferred_element_type=F32)


def nn(left, right):
    return lax.dot_general(left, right, (((1,), (0,)), ((), ())), preferred_element_type=F32)


def estimate(flops, size):
    return pl.CostEstimate(flops=flops, bytes_accessed=size, transcendentals=0)


def head_mask(rows, head):
    lanes = lax.broadcasted_iota(jnp.int32, (rows, LANES), 1)
    return (lanes >= head * HEAD) & (lanes < (head + 1) * HEAD)


def only(mask, value, factor=1.0):
    return jnp.where(mask, value.astype(F32) * factor, 0.0).astype(BF16)


def turned(value):
    return value.astype(F32).T.astype(BF16)


def attend_kernel(keep_weights, core_ref, *refs):
    @pl.when(core_ref[1] == 1)
    def _():
        attend_pair(keep_weights, core_ref, *refs)


def attend_pair(keep_weights, core_ref, q_ref, k_ref, v_ref, ko_ref, vo_ref, o_ref, *kept_refs):
    rows = q_ref.shape[0] // 2
    second = core_ref[0] == 1
    keys = lax.broadcasted_iota(jnp.int32, (rows, rows), 0)
    places = lax.broadcasted_iota(jnp.int32, (rows, rows), 1)
    allowed = keys <= places
    factor = HEAD ** (-0.5)
    small = pl.ds(0, rows)
    large = pl.ds(rows, rows)

    def fifth(ref):
        return jnp.where(second, ref[small, :].astype(F32), ref[large, :].astype(F32)).astype(BF16)

    k5, q5 = fifth(ko_ref), fifth(q_ref)
    vs, vl, v4, v5 = turned(v_ref[small, :]), turned(v_ref[large, :]), turned(vo_ref[small, :]), turned(fifth(vo_ref))
    small_parts, large_parts, scales = [], [], []
    for head in range(LANES // HEAD):
        mask = head_mask(rows, head)
        lanes = slice(head * HEAD, (head + 1) * HEAD)
        qs, ql, qf = (only(mask, value, factor) for value in (q_ref[small, :], q_ref[large, :], q5))
        s1 = jnp.where(allowed, nt(k_ref[small, :], qs), NEGATIVE)
        s2 = nt(k_ref[small, :], ql)
        s3 = jnp.where(allowed, nt(k_ref[large, :], ql), NEGATIVE)
        s4 = nt(ko_ref[small, :], ql)
        s5 = nt(k5, qf)

        def peak(value):
            return jnp.max(value, axis=0, keepdims=True)

        def total(value):
            return jnp.sum(value, axis=0, keepdims=True)

        m5 = peak(s5)
        ms = peak(s1)
        ml = jnp.maximum(jnp.maximum(peak(s2), peak(s3)), peak(s4))
        ms = jnp.where(second, jnp.maximum(ms, m5), ms)
        ml = jnp.where(second, ml, jnp.maximum(ml, m5))
        mf = jnp.where(second, ms, ml)
        e1 = jnp.exp(s1 - ms)
        e2 = jnp.exp(s2 - ml)
        e3 = jnp.exp(s3 - ml)
        e4 = jnp.exp(s4 - ml)
        e5 = jnp.exp(s5 - mf)
        t5 = total(e5)
        rs = total(e1)
        rl = total(e2) + total(e3) + total(e4)
        rs = 1.0 / jnp.where(second, rs + t5, rs)
        rl = 1.0 / jnp.where(second, rl, rl + t5)
        e1, e2, e3, e4, e5 = (value.astype(BF16) for value in (e1, e2, e3, e4, e5))
        if keep_weights:
            for place, value in enumerate((e1, e2, e3, e4, e5)):
                kept_refs[0][head, place] = value
            scales.append(jnp.concatenate([rs, rl], axis=1))
        o5 = nn(v5[lanes], e5)
        small_parts.append((nn(vs[lanes], e1) + jnp.where(second, o5, 0.0)) * rs)
        large_parts.append(
            (nn(vs[lanes], e2) + nn(vl[lanes], e3) + nn(v4[lanes], e4) + jnp.where(second, 0.0, o5)) * rl
        )
    o_ref[small, :] = jnp.concatenate(small_parts).T.astype(BF16)
    o_ref[large, :] = jnp.concatenate(large_parts).T.astype(BF16)
    if keep_weights:
        row = lax.broadcasted_iota(jnp.int32, (8, 2 * rows), 0)
        kept_refs[1][...] = jnp.where(row == 0, scales[0], scales[1])


def attend_back_kernel(
    core_ref, q_ref, k_ref, v_ref, ko_ref, vo_ref, go_ref, o_ref, e_ref, scale_ref, gq_ref, own_ref, other_ref, sums_ref
):
    rows = q_ref.shape[0] // 2
    second = core_ref[0] == 1
    factor = HEAD ** (-0.5)
    small = pl.ds(0, rows)
    large = pl.ds(rows, rows)

    def fifth(first, last):
        return jnp.where(second, first.astype(F32), last.astype(F32)).astype(BF16)

    row = lax.broadcasted_iota(jnp.int32, (LANES, 2 * rows), 0)
    scale = jnp.where(row < HEAD, scale_ref[0:1, :], scale_ref[1:2, :]).T
    grads = (go_ref[...].astype(F32) * scale).astype(BF16)
    product = grads.astype(F32) * o_ref[...].astype(F32)
    high = product.astype(BF16)
    low = (product - high.astype(F32)).astype(BF16)
    g_small, g_large = grads[:rows], grads[rows:]
    g5 = fifth(g_small, g_large)
    q5 = fifth(q_ref[small, :], q_ref[large, :])
    v5 = fifth(vo_ref[small, :], vo_ref[large, :])
    ks, kl, k4, k5 = (
        turned(k_ref[small, :]), turned(k_ref[large, :]), turned(ko_ref[small, :]),
        turned(fifth(ko_ref[small, :], ko_ref[large, :])),
    )
    totals = {}
    gq_small, gq_large = [], []

    def add(name, value):
        totals[name] = value if name not in totals else totals[name] + value

    for head in range(LANES // HEAD):
        mask = head_mask(rows, head)
        lanes = slice(head * HEAD, (head + 1) * HEAD)
        ones = jnp.where(head_mask(16, head), 1.0, 0.0).astype(BF16)
        inner = (nt(ones, high) + nt(ones, low))[0:1]
        ds_, dl_ = inner[:, :rows], inner[:, rows:]
        df_ = jnp.where(second, ds_, dl_)
        qs, ql, qf = (only(mask, value, factor) for value in (q_ref[small, :], q_ref[large, :], q5))
        gs, gl, gf = (only(mask, value) for value in (g_small, g_large, g5))

        def score_grad(place, values, rows_grad, shift):
            return (e_ref[head, place].astype(F32) * (nt(values, rows_grad) - shift)).astype(BF16)

        z1 = score_grad(0, v_ref[small, :], gs, ds_)
        z2 = score_grad(1, v_ref[small, :], gl, dl_)
        z3 = score_grad(2, v_ref[large, :], gl, dl_)
        z4 = score_grad(3, vo_ref[small, :], gl, dl_)
        z5 = score_grad(4, v5, gf, df_)
        gq5 = nn(k5[lanes], z5)
        gq_small.append(nn(ks[lanes], z1) + jnp.where(second, gq5, 0.0))
        gq_large.append(nn(ks[lanes], z2) + nn(kl[lanes], z3) + nn(k4[lanes], z4) + jnp.where(second, 0.0, gq5))
        add("ks", nn(z1, qs) + nn(z2, ql))
        add("kl", nn(z3, ql))
        add("k4", nn(z4, ql))
        add("k5", nn(z5, qf))
        add("vs", nn(e_ref[head, 0], gs) + nn(e_ref[head, 1], gl))
        add("vl", nn(e_ref[head, 2], gl))
        add("v4", nn(e_ref[head, 3], gl))
        add("v5", nn(e_ref[head, 4], gf))
    gqs, gql = jnp.concatenate(gq_small).T * factor, jnp.concatenate(gq_large).T * factor
    gq_ref[small, :] = gqs.astype(BF16)
    gq_ref[large, :] = gql.astype(BF16)
    for place, name in enumerate("kv"):
        own_ref[place, small, :] = totals[name + "s"]
        own_ref[place, large, :] = totals[name + "l"]
        four, five = totals[name + "4"], totals[name + "5"]
        other_ref[place, small, :] = (four + jnp.where(second, five, 0.0)).astype(BF16)
        other_ref[place, large, :] = jnp.where(second, 0.0, five).astype(BF16)
    sum_q = jnp.sum(gqs, axis=0, keepdims=True) + jnp.sum(gql, axis=0, keepdims=True)
    sum_v = jnp.sum(totals["vs"] + totals["vl"] + totals["v4"] + totals["v5"], axis=0, keepdims=True)
    row = lax.broadcasted_iota(jnp.int32, (8, LANES), 0)
    sums_ref[...] = jnp.where(row == 0, sum_q, jnp.where(row == 1, sum_v, 0.0))


def attend(core, q, k, v, k_other, v_other, keep_weights):
    length, width = q.shape
    rows = length // 2
    pairs = width // LANES
    column = pl.BlockSpec((length, LANES), lambda i: (0, i))
    shapes = [jax.ShapeDtypeStruct((length, width), BF16)]
    outs = [column]
    if keep_weights:
        shapes.append(pltpu.HBM((width // HEAD, 5, rows, rows), BF16))
        shapes.append(jax.ShapeDtypeStruct((8 * pairs, length), F32))
        outs.append(pl.BlockSpec((2, 5, rows, rows), lambda i: (i, 0, 0, 0)))
        outs.append(pl.BlockSpec((8, length), lambda i: (i, 0)))
    return pl.pallas_call(
        functools.partial(attend_pair if keep_weights else attend_kernel, keep_weights),
        grid=(pairs,),
        out_shape=shapes,
        in_specs=[pl.BlockSpec(memory_space=pltpu.SMEM)] + [column] * 5,
        out_specs=outs,
        compiler_params=pltpu.CompilerParams(vmem_limit_bytes=40 * 1024 * 1024),
        cost_estimate=estimate(20 * rows * rows * width * 2, 16 * length * width),
        name="attend",
    )(core, q, k, v, k_other, v_other)


def attend_back(core, q, k, v, k_other, v_other, grad_mixed, mixed, weights, scales):
    length, width = q.shape
    rows = length // 2
    column = pl.BlockSpec((length, LANES), lambda i: (0, i))
    double = pl.BlockSpec((2, length, LANES), lambda i: (0, 0, i))
    return pl.pallas_call(
        attend_back_kernel,
        grid=(width // LANES,),
        out_shape=[
            jax.ShapeDtypeStruct((length, width), BF16),
            jax.ShapeDtypeStruct((2, length, width), F32),
            jax.ShapeDtypeStruct((2, length, width), BF16),
            jax.ShapeDtypeStruct((8, width), F32),
        ],
        in_specs=[pl.BlockSpec(memory_space=pltpu.SMEM)]
        + [column] * 7
        + [pl.BlockSpec((2, 5, rows, rows), lambda i: (i, 0, 0, 0)), pl.BlockSpec((8, length), lambda i: (i, 0))],
        out_specs=[column, double, double, pl.BlockSpec((8, LANES), lambda i: (0, i))],
        compiler_params=pltpu.CompilerParams(vmem_limit_bytes=40 * 1024 * 1024),
        cost_estimate=estimate(40 * rows * rows * width * 2, 40 * length * width),
        name="attend_back",
    )(core, q, k, v, k_other, v_other, grad_mixed, mixed, weights, scales)


def gelu_and_slope(values):
    root = float(np.sqrt(2 / np.pi))
    cubic = 0.044715 * root
    square = values * values
    bend = jnp.tanh(values * (root + cubic * square))
    half = 0.5 + 0.5 * bend
    gate = values * half
    slope = half + gate * ((1.0 - bend) * (root + (3 * cubic) * square))
    return (gate, slope)


def expand_kernel(core_ref, rows_ref, expand_ref, bias_ref, reduce_ref, start_ref, total_ref):
    @pl.when(core_ref[1] == 1)
    def _():
        gate, _ = gelu_and_slope(nt(rows_ref[...], expand_ref[...]) + bias_ref[...])
        total_ref[...] = start_ref[...] + nn(gate.astype(BF16), reduce_ref[...])


def feed_half(core, rows, expand_w, bias, reduce_w, start, row_part=None):
    length, width = rows.shape
    units = expand_w.shape[0]
    if row_part is not None:
        length = length // 2
    place = row_part or 0
    whole = pl.BlockSpec((length, width), lambda i: (0, 0))
    taken = pl.BlockSpec((length, width), lambda i: (place, 0))
    start_place = 0 if start.shape[0] == length else place
    begun = pl.BlockSpec((length, width), lambda i: (start_place, 0))
    weight = pl.BlockSpec((units, width), lambda i: (0, 0))
    return pl.pallas_call(
        expand_kernel,
        grid=(1,),
        out_shape=jax.ShapeDtypeStruct((length, width), F32),
        in_specs=[
            pl.BlockSpec(memory_space=pltpu.SMEM),
            taken, weight, pl.BlockSpec((1, units), lambda i: (0, 0)), weight, begun,
        ],
        out_specs=whole,
        compiler_params=pltpu.CompilerParams(vmem_limit_bytes=40 * 1024 * 1024),
        cost_estimate=estimate(4 * length * width * units, 4 * width * units),
        name="feed_half",
    )(core, rows, expand_w, bias.reshape(1, units), reduce_w, start)


def both_kernel(
    steps, rows_ref, grad_ref, e0_ref, e1_ref, b0_ref, b1_ref, r0_ref, r1_ref,
    total_ref, grad_total_ref, h0_ref, h1_ref, s0_ref, s1_ref,
):
    place = pl.program_id(0)

    @pl.when(place == 0)
    def _():
        total_ref[...] = jnp.zeros_like(total_ref)
        grad_total_ref[...] = jnp.zeros_like(grad_total_ref)

    def tile(expand_ref, bias_ref, reduce_ref, hidden_ref, slope_ref):
        gate, slope = gelu_and_slope(nt(rows_ref[...], expand_ref[...]) + bias_ref[...])
        hidden = gate.astype(BF16)
        slope = slope.astype(BF16)
        hidden_ref[...] = hidden
        slope_ref[...] = slope
        total_ref[...] += nn(hidden, reduce_ref[...])
        pre = nt(grad_ref[...], reduce_ref[...]) * slope.astype(F32)
        grad_total_ref[...] += nn(pre.astype(BF16), expand_ref[...])

    @pl.when(place < steps)
    def _():
        tile(e0_ref, b0_ref, r0_ref, h0_ref, s0_ref)

    @pl.when(place >= steps)
    def _():
        tile(e1_ref, b1_ref, r1_ref, h1_ref, s1_ref)


def back_kernel(
    steps, grad_ref, e0_ref, e1_ref, r0_ref, r1_ref, s0_ref, s1_ref,
    total_ref, p0_ref, p1_ref, sums0_ref, sums1_ref,
):
    place = pl.program_id(0)

    @pl.when(place == 0)
    def _():
        total_ref[...] = jnp.zeros_like(total_ref)

    def tile(expand_ref, reduce_ref, slope_ref, pre_ref, sums_ref):
        pre = nt(grad_ref[...], reduce_ref[...]) * slope_ref[...].astype(F32)
        sums_ref[...] = jnp.broadcast_to(jnp.sum(pre, axis=0, keepdims=True), sums_ref.shape)
        rounded = pre.astype(BF16)
        pre_ref[...] = rounded
        total_ref[...] += nn(rounded, expand_ref[...])

    @pl.when(place < steps)
    def _():
        tile(e0_ref, r0_ref, s0_ref, p0_ref, sums0_ref)

    @pl.when(place >= steps)
    def _():
        tile(e1_ref, r1_ref, s1_ref, p1_ref, sums1_ref)


def feed_specs(length, width, units, steps):
    tile = units // steps
    whole = pl.BlockSpec((length, width), lambda i: (0, 0))

    def early(i):
        return jnp.minimum(i, steps - 1)

    def late(i):
        return jnp.maximum(i - steps, 0)

    weight = [pl.BlockSpec((tile, width), lambda i, f=f: (f(i), 0)) for f in (early, late)]
    across = [pl.BlockSpec((length, tile), lambda i, f=f: (0, f(i))) for f in (early, late)]
    row = [pl.BlockSpec((1, tile), lambda i, f=f: (0, f(i))) for f in (early, late)]
    rows = [pl.BlockSpec((8, tile), lambda i, f=f: (0, f(i))) for f in (early, late)]
    return steps, whole, weight, across, row, rows


def feed_both(rows, grad, halves):
    length, width = rows.shape
    units = halves[0][0].shape[0]
    steps, whole, weight, across, row, _ = feed_specs(length, width, units, 2)
    total = jax.ShapeDtypeStruct((length, width), F32)
    kept = jax.ShapeDtypeStruct((length, units), BF16)
    (e0, b0, r0), (e1, b1, r1) = halves
    return pl.pallas_call(
        functools.partial(both_kernel, steps),
        grid=(2 * steps,),
        out_shape=[total, total, kept, kept, kept, kept],
        in_specs=[whole, whole, *weight, *row, *weight],
        out_specs=[whole, whole, *across, *across],
        compiler_params=pltpu.CompilerParams(vmem_limit_bytes=40 * 1024 * 1024),
        cost_estimate=estimate(16 * length * width * units, 8 * width * units),
        name="feed_both",
    )(rows, grad, e0, e1, b0.reshape(1, units), b1.reshape(1, units), r0, r1)


def feed_back(grad, halves, slope):
    length, width = grad.shape
    units = halves[0][0].shape[0]
    steps, whole, weight, across, _, rows = feed_specs(length, width, units, 1)
    kept = jax.ShapeDtypeStruct((length, units), BF16)
    sums = jax.ShapeDtypeStruct((8, units), F32)
    (e0, _, r0), (e1, _, r1) = halves
    return pl.pallas_call(
        functools.partial(back_kernel, steps),
        grid=(2 * steps,),
        out_shape=[jax.ShapeDtypeStruct((length, width), F32), kept, kept, sums, sums],
        in_specs=[whole, *weight, *weight, *across],
        out_specs=[whole, *across, *rows],
        compiler_params=pltpu.CompilerParams(vmem_limit_bytes=40 * 1024 * 1024),
        cost_estimate=estimate(8 * length * width * units, 8 * width * units),
        name="feed_back",
    )(grad, e0, e1, r0, r1, *slope)


def tie(value, *others):
    return lax.optimization_barrier((value, *others))[0]


def normalize_rows(rows):
    centred = rows - jnp.mean(rows, axis=-1, keepdims=True)
    inverse = lax.rsqrt(jnp.mean(centred * centred, axis=-1, keepdims=True) + EPSILON)
    return (centred * inverse, inverse)


def norm_backward(grad_normed, normed, inverse, gain):
    scaled = grad_normed * gain
    centred = scaled - jnp.mean(scaled, axis=-1, keepdims=True)
    return inverse * (centred - normed * jnp.mean(scaled * normed, axis=-1, keepdims=True))


def attention_forward(core, rows_in, weights, keep, before=(), after=()):
    gain_a, shift_a, proj, bias_q, bias_v, bias_out = weights
    normed_one, inverse_one = normalize_rows(rows_in)
    ready_one = narrow(normed_one * gain_a + shift_a)
    k = narrow(nt(ready_one, proj[1]))
    k_other = swap(k, "core")
    v = narrow(nt(ready_one, proj[2]) + bias_v)
    v_other = swap(v, "core")
    q = narrow(nt(ready_one, proj[0]) + bias_q)
    if before:
        q, proj_out, *before = lax.optimization_barrier((q, proj[3], *before))
        proj = [*proj[:3], proj_out]
        after = after(before)
    mixed, *kept_weights = attend(core, q, k, v, k_other, v_other, keep)
    mixed, *after = lax.optimization_barrier((mixed, *after))
    middle = rows_in + BRANCH * (nn(mixed, proj[3]) + bias_out)
    kept = (normed_one, inverse_one, ready_one, (q, k, v, k_other, v_other), mixed, *kept_weights)
    return middle, kept, after


def feed_start(middle, weights):
    gain_b, shift_b, _, _ = weights
    normed_two, inverse_two = normalize_rows(middle)
    return normed_two, inverse_two, narrow(normed_two * gain_b + shift_b)


def feed_forward_only(core, middle, weights):
    ready_two = feed_start(middle, weights)[2]
    first, second = weights[2]
    block = middle.shape[0] // 2
    total = jnp.broadcast_to(weights[3], (block, middle.shape[1]))
    totals = [feed_half(core, ready_two, *first, total, 0)]
    results = []
    for part in range(2):
        rows = slice(part * block, (part + 1) * block)
        if part:
            totals.append(feed_half(core, ready_two, *first, tie(total, *results), part))
        piece = feed_half(core, ready_two, *second, totals[part], part)
        results.append(narrow(middle[rows] + BRANCH * piece))
    return results


def feed_forward_and_back(middle, grad_result, weights):
    normed_two, inverse_two, ready_two = feed_start(middle, weights)
    rounded = narrow(BRANCH * grad_result)
    total, grad_total, *kept = feed_both(ready_two, rounded, weights[2])
    result = narrow(middle + BRANCH * (total + weights[3]))
    grad_middle = grad_result + norm_backward(grad_total, normed_two, inverse_two, weights[0])
    return result, grad_middle, (normed_two, inverse_two, ready_two, kept[:2], kept[2:])


def attention_backward(core, kept, grad_middle, weights, before=(), after=()):
    _, _, _, projected, mixed, *attention = kept
    rounded_attended = narrow(BRANCH * grad_middle)
    grad_mixed = narrow(nt(tie(rounded_attended, *before), weights[2][3]))
    grad_q, own, other, sums = attend_back(core, *projected, grad_mixed, mixed, *attention)
    other, *after = lax.optimization_barrier((other, *after))
    grad_kv = narrow(own + swap(other, "core").astype(F32))
    return rounded_attended, (grad_q, grad_kv[0], grad_kv[1]), sums[:2], after


def attention_input_grad(kept, grad_middle, grad_qkv, weights):
    gain_a, _, proj, _, _, _ = weights
    normed_one, inverse_one, *_ = kept
    grad_normed_one = sum(nn(grad, part) for grad, part in zip(grad_qkv, proj))
    grad_in = grad_middle + norm_backward(grad_normed_one, normed_one, inverse_one, gain_a)
    return grad_in, [grad_normed_one * normed_one, grad_normed_one, BRANCH * grad_middle]


def narrow(value):
    return value.astype(BF16)


def wide_add(left, right):
    return narrow(left.astype(F32) + right.astype(F32))


def over_groups(value):
    return lax.psum(value, "outer") if lax.axis_size("outer") > 1 else value


def ring_add(parts):
    count = len(parts)
    total = parts[1 % count]
    for step in range(1, count):
        total = wide_add(ring(total), parts[(step + 1) % count])
    return total


def thirds(values):
    pieces = []
    for _ in range(3):
        piece = lax.reduce_precision(values, 8, 7)
        pieces.append(narrow(piece))
        values = values - piece
    return jnp.stack(pieces)


def shards(
    inputs, cotangent, gain_one, shift_one, attend_in, attend_bias, attend_out, out_bias,
    gain_two, shift_two, expand_in, expand_bias, reduce_out, reduce_bias,
):
    count = lax.axis_size("tensor")
    x, y, c, z = (lax.axis_index(axis) for axis in AXES)
    is_first = x == 0
    core = jnp.stack([c, jnp.ones_like(c)]).astype(jnp.int32)
    core_a = jnp.stack([c, 1 - x]).astype(jnp.int32)
    width = attend_in.shape[1]
    local = attend_in.shape[3]
    units = expand_in.shape[2]
    part = units // 4
    spare = 16

    def either(index, pair):
        first, second = pair
        return jnp.where(index == 0, first, second), jnp.where(index == 0, second, first)

    def relative(blocks):
        rows = [either(y, blocks[:2]), either(y, blocks[2:])]
        return list(zip(*(either(c, pair) for pair in zip(*rows))))

    def quarters(value, axis):
        return relative(jnp.split(value, 4, axis))

    typed = [*attend_in[0].transpose(1, 2, 0), attend_out[0]]
    (mine, mine_y), _ = relative(typed)
    biases = thirds(jnp.concatenate([attend_bias[0].reshape(2 * local), expand_bias[0]])).reshape(-1)
    biases = jnp.pad(biases, (0, spare * width - biases.size)).reshape(spare, width)
    piece = jnp.concatenate([mine, biases])
    bias_rows = [biases]
    own_parts = [quarters(expand_in[0].T, 0), quarters(reduce_out[0], 0)]
    feed = [jnp.concatenate([value[0][0] for value in own_parts])]
    feed_y = [jnp.concatenate([value[0][1] for value in own_parts])]
    pieces, pieces_y = [ring(piece)], []
    arrived = fetch(inputs[0, 0], None)
    while len(pieces) < count - 1:
        pieces_y.append(swap(pieces[-1][:local], "y"))
        pieces.append(ring(pieces[-1]))
        if len(pieces) < count - 1:
            pieces[-1], pieces_y[-1], feed[0], *arrived = lax.optimization_barrier(
                (pieces[-1], pieces_y[-1], feed[0], *arrived)
            )
    feed.append(ring(feed[0]))
    passed = [along_pipe(rows, -1) for rows in arrived]
    pieces[-1], pieces_y[-1] = lax.optimization_barrier((pieces[-1], pieces_y[-1]))
    pieces_y.append(swap(pieces[-1][:local], "y"))
    feed[1], pieces_y[-1], passed[0] = lax.optimization_barrier((feed[1], pieces_y[-1], passed[0]))
    feed_y.append(swap(feed[1], "y"))
    feed.append(ring(feed[1]))
    feed[2], feed_y[1], passed[1] = lax.optimization_barrier((feed[2], feed_y[1], passed[1]))
    arrived = [jnp.where(z % 2 == 0, here, there) for here, there in zip(arrived, passed)]
    feed_y.append(swap(feed[2], "y"))
    before = (ring(feed[2]), feed_y[2])
    bias_rows += [value[local:] for value in pieces]
    pieces = [mine] + [value[:local] for value in pieces]
    pieces_y = [mine_y] + pieces_y
    pieces = jnp.concatenate(pieces)
    pieces_y = jnp.concatenate(pieces_y)
    proj = relative([pieces, pieces_y, swap(pieces, "core"), swap(pieces_y, "core")])
    proj = [*proj[0], *proj[1]]
    biases = jnp.stack(bias_rows).reshape(count, -1)[:, : 3 * (2 * local + units)].reshape(count, 3, 2 * local + units)
    biases = biases.astype(F32)
    biases = biases[:, 0] + (biases[:, 1] + biases[:, 2])
    bias_q, bias_v = biases[:, :local].reshape(width), biases[:, local : 2 * local].reshape(width)
    expand_b = quarters(biases[:, 2 * local :], 1)
    expand_b = [jnp.concatenate([value.reshape(count * part) for value in pair]) for pair in expand_b]
    attention_weights = (gain_one[0], shift_one[0], proj, bias_q, bias_v, out_bias[0])

    rows_in = jnp.concatenate(arrived)
    middle, _, after = attention_forward(
        core_a, rows_in.astype(F32), attention_weights, False, before,
        lambda ready: (*ready, swap(ready[0], "y")),
    )
    feed.append(after[0])
    feed_y[2:] = after[1:]
    own_half = [
        jnp.concatenate([value[kind * part : (kind + 1) * part] for value in feed + feed_y]) for kind in range(2)
    ]
    other_half = [swap(value, "core") for value in own_half]
    feed_weights = (
        gain_two[0],
        shift_two[0],
        [(own_half[0], expand_b[0], own_half[1]), (other_half[0], expand_b[1], other_half[1])],
        reduce_bias[0],
    )
    passed = jnp.concatenate([along_pipe(rows, 1) for rows in feed_forward_only(core_a, middle, feed_weights)])
    last = fetch(tie(cotangent[0, 0], passed), 1)
    rows_in = jnp.where(is_first, rows_in, passed)
    middle, kept_attention, last = attention_forward(
        core, rows_in.astype(F32), attention_weights, True, (), last
    )
    last = jnp.concatenate(last)
    result, grad_middle, kept_feed = feed_forward_and_back(middle, last.astype(F32), feed_weights)
    block = result.shape[0] // 2
    outputs = give_back(result[:block], result[block:], 1)
    _, grad_qkv, _, (outputs,) = attention_backward(
        core, kept_attention, grad_middle, attention_weights, (), (outputs,)
    )
    grad_in = narrow(attention_input_grad(kept_attention, grad_middle, grad_qkv, attention_weights)[0])
    returned = jnp.concatenate([along_pipe(grad_in[:block], -1), along_pipe(grad_in[block:], -1)])
    grad_result = jnp.where(is_first, returned, last).astype(F32)
    grad_outcome = BRANCH * grad_result
    rounded_outcome = narrow(grad_outcome)
    normed_two, inverse_two, ready_two, hidden, slope = kept_feed
    span = count * part

    def by_slot(value):
        return [value[slot * part : (slot + 1) * part] for slot in range(count)]

    def steps_of(parts):
        state = [parts[1 % count]]

        def start():
            state.append(ring(state[-1]))
            return state[-1]

        def finish(arrived, step):
            state.append(wide_add(arrived, parts[(step + 1) % count]))
            return state[-1]

        return start, finish

    send = narrow(tn(hidden[1], rounded_outcome))
    arrived = swap(send, "core")
    keep = tn(hidden[0], tie(rounded_outcome, send))
    reduce_sums = wide_add(keep, tie(arrived, keep))
    to_y = reduce_sums[span:]
    to_y = [to_y[part : 3 * part], jnp.concatenate([to_y[3 * part :], to_y[:part]])]
    reduce_y = [swap(value, "y") for value in to_y]
    total, pre_own, pre_other, sums_own, sums_other = feed_back(
        tie(rounded_outcome, reduce_sums, *to_y), feed_weights[2], slope
    )
    pre_other, reduce_y[0] = lax.optimization_barrier((pre_other, reduce_y[0]))
    reduce_keep = by_slot(reduce_sums[:span])
    reduce_parts = [None, *(wide_add(reduce_keep[i + 1], reduce_y[0][i * part : (i + 1) * part]) for i in range(2)), None]
    reduce_start, reduce_finish = steps_of(reduce_parts)
    grad_middle = grad_result + norm_backward(total, normed_two, inverse_two, gain_two[0])
    shared_feed = [total * normed_two, total, grad_outcome]
    send = narrow(tn(tie(pre_other, grad_middle), ready_two))
    arrived = swap(send, "core")
    keep = tn(pre_own, tie(ready_two, send))
    expand_sums = wide_add(keep, tie(arrived, keep))
    expand_parts = [jnp.concatenate(pair) for pair in zip(by_slot(expand_sums[:span]), by_slot(expand_sums[span:]))]
    expand_start, expand_finish = steps_of(expand_parts)
    rounded_attended, grad_qkv, sums_qv, after = attention_backward(
        core, kept_attention, grad_middle, attention_weights, (*expand_parts, *reduce_parts[1:3]),
        (expand_start(), reduce_start(), reduce_y[1]),
    )
    expand_step, reduce_step = expand_finish(after[0], 1), reduce_finish(after[1], 1)
    reduce_parts[3] = wide_add(reduce_keep[3], after[2][:part])
    reduce_parts[0] = wide_add(reduce_keep[0], after[2][part:])
    moving_e, moving_r = expand_start(), reduce_start()
    grad_qkv = lax.optimization_barrier((*grad_qkv, expand_step, reduce_step))[:3]
    mixed, ready_one = kept_attention[4], kept_attention[2]
    left = jnp.stack([*grad_qkv, mixed])
    index = 2 * c + y

    def typed_grad(shift):
        right = jnp.where((index ^ shift) == 3, rounded_attended, ready_one)
        return tn(lax.dynamic_index_in_dim(left, index ^ shift, 0, False), right)

    send = [narrow(typed_grad(shift)) for shift in (3, 2)]
    arrived = [swap(value, "core") for value in send]
    left = tie(left, *send)
    keep = [typed_grad(shift) for shift in (1, 0)]
    moving_e, *keep = lax.optimization_barrier((moving_e, *keep))
    expand_finish(moving_e, 2)
    moving_e = expand_start()
    sums = [wide_add(a, b) for a, b in zip(keep, arrived)]
    to_y, to_keep = by_slot(sums[0]), by_slot(sums[1])
    typed_parts = [None] * count

    def typed_swap(slot):
        return swap(to_y[slot], "y")

    def typed_part(slot, arrived):
        typed_parts[slot] = wide_add(to_keep[slot], arrived)

    moving_y, moving_z = typed_swap(1), typed_swap(2)
    grad_qkv = lax.optimization_barrier((grad_qkv, sums))[0]
    grad_in, shared_attention = attention_input_grad(kept_attention, grad_middle, grad_qkv, attention_weights)
    grad_in = narrow(grad_in)
    shared = jnp.stack([jnp.sum(value, axis=0) for value in shared_attention + shared_feed])
    sums_qv = sums_qv.reshape(2, count, local)
    sums_qv = jnp.concatenate([sums_qv[0], sums_qv[1], jnp.zeros((count, width - 2 * local), F32)], axis=1)[:, None]
    sums_pre = [value.reshape(count, part) for half in (sums_own[0], sums_other[0]) for value in jnp.split(half, 2)]
    sums_pre = quarters(jnp.concatenate(sums_pre, axis=1), 1)
    sums_pre = jnp.concatenate(sums_pre[0] + sums_pre[1], axis=1)[:, None]
    vectors = jnp.concatenate([jnp.broadcast_to(shared, (count,) + shared.shape), sums_qv, sums_pre], axis=1)
    vectors = vectors + swap(vectors, "core")

    moving_y, moving_r, to_y[3], to_y[0] = lax.optimization_barrier((moving_y, moving_r, to_y[3], to_y[0]))
    typed_part(1, moving_y)
    reduce_finish(moving_r, 2)
    typed_start, typed_finish = steps_of(typed_parts)
    moving_t, moving_y, moving_v, moving_r = typed_start(), typed_swap(3), swap(vectors, "y"), reduce_start()
    moving_t, moving_z, moving_v, moving_e = lax.optimization_barrier((moving_t, moving_z, moving_v, moving_e))
    vectors = vectors + moving_v
    typed_part(2, moving_z)
    typed_finish(moving_t, 1)
    expand_total = expand_finish(moving_e, 3).reshape(2, part, width)
    moving_t, moving_z, moving_v = typed_start(), typed_swap(0), ring(vectors[1])
    moving_t, moving_y, moving_v, moving_r = lax.optimization_barrier((moving_t, moving_y, moving_v, moving_r))
    reduce_total = over_groups(reduce_finish(moving_r, 3))
    typed_part(3, moving_y)
    typed_finish(moving_t, 2)
    moving_v = ring(moving_v + vectors[2])
    moving_t, reduce_other, expand_other = typed_start(), swap(reduce_total, "y"), swap(expand_total, "y")
    moving_t, moving_z, moving_v, reduce_other, grad_in = lax.optimization_barrier(
        (moving_t, moving_z, moving_v, reduce_other, grad_in)
    )
    typed_part(0, moving_z)
    typed_total = over_groups(typed_finish(moving_t, 3))
    moving_v = ring(moving_v + vectors[3])
    typed_other = swap(typed_total, "y")
    input_grad = give_back(grad_in[:block], grad_in[block:], 0)
    typed_other, expand_other, moving_v = lax.optimization_barrier((typed_other, expand_other, moving_v))
    vectors = over_groups(moving_v + vectors[0])
    def gathered(pair):
        pair = jnp.concatenate(pair)
        blocks = quarters(jnp.concatenate([pair, swap(pair, "core")]), 0)
        return jnp.concatenate(blocks[0] + blocks[1])

    pair = jnp.concatenate([typed_total, typed_other])
    pair_other = swap(pair, "core")
    grad_expand = [over_groups(wide_add(expand_total[i], expand_other[1 - i])) for i in range(2)]
    grad_expand = gathered(grad_expand).T.astype(F32)
    grad_reduce = gathered([reduce_total, reduce_other]).astype(F32)
    whole = relative([pair[:local], pair[local:], pair_other[:local], pair_other[local:]])
    whole = [*whole[0], *whole[1]]
    grad_attend_in = jnp.stack(whole[:3]).transpose(2, 0, 1).astype(F32)
    grad_attend_out = whole[3].astype(F32)
    return (
        outputs[None, None],
        input_grad[None, None],
        vectors[0][None],
        vectors[1][None],
        grad_attend_in[None],
        vectors[6, : 2 * local].reshape(1, 2, local),
        grad_attend_out[None],
        vectors[2][None],
        vectors[3][None],
        vectors[4][None],
        grad_expand[None],
        vectors[7, :units][None],
        grad_reduce[None],
        vectors[5][None],
    )


def solution(mesh):
    pipe, groups, count = mesh.devices.shape
    split = Mesh(mesh.devices.reshape(pipe, groups // 4, 2, 2, count), ("pipe", "outer", "y", "core", "tensor"))
    dp = ("outer", "y", "core")
    rows = P("pipe", dp, "tensor", None)
    vector = P("pipe", None)
    placed = (
        rows,
        rows,
        vector,
        vector,
        P("pipe", None, None, "tensor"),
        P("pipe", None, "tensor"),
        P("pipe", "tensor", None),
        vector,
        vector,
        vector,
        P("pipe", None, "tensor"),
        P("pipe", "tensor"),
        P("pipe", "tensor", None),
        vector,
    )
    return jax.shard_map(shards, mesh=split, in_specs=placed, out_specs=(rows, rows) + placed[2:], check_vma=False)
```
